32 devices in a mesh: section: 2 (over x), dp: 16 (over z, y, core).
Axes of the slice: x: 2, y: 2, z: 4, core: 2. Of those that a mesh axis runs over, the one named last changes fastest.
Arguments:
- content_in: bfloat16 [32, 128, 768], P('dp'), may hold values from -6 to 6
- memory: bfloat16 [2, 32, 128, 768], P('section', 'dp'), may hold values from -6 to 6
- mask_embed: bfloat16 [768], replicated, may hold values from -5 to 5
- doc_ids: int32 [32, 128], P('dp'), may hold values from 0 to 3, never falling along the last dimension, each value on 1 to 64 neighbouring positions
- orders: int32 [32, 128], P('dp'), may hold values from 0 to 127, each once within a row
- targets: int32 [32, 128], P('dp'), may hold values 0 or 1
- slot_used: int32 [32], P('dp'), may hold values from 0 to 1, as said below
- w_query: bfloat16 [2, 768, 768], P('section'), may hold values from -0.21875 to 0.21875
- w_key: bfloat16 [2, 768, 768], P('section'), may hold values from -0.21875 to 0.21875
- w_value: bfloat16 [2, 768, 768], P('section'), may hold values from -0.21875 to 0.21875
- w_out: bfloat16 [2, 768, 768], P('section'), may hold values from -3.5 to 3.5
- w_rel: bfloat16 [2, 768, 768], P('section'), may hold values from -0.21875 to 0.21875
- bias_content: bfloat16 [2, 12, 64], P('section'), may hold values from -3 to 3
- bias_position: bfloat16 [2, 12, 64], P('section'), may hold values from -3 to 3
- bias_segment: bfloat16 [2, 12, 64], P('section'), may hold values from -3 to 3
- seg_embed: bfloat16 [2, 2, 12, 64], P('section'), may hold values from -3 to 3
- norm1_gain: bfloat16 [2, 768], P('section'), may hold values from 0.5 to 1.5
- norm1_shift: bfloat16 [2, 768], P('section'), may hold values from -1 to 1
- ffn_in: bfloat16 [2, 768, 3072], P('section'), may hold values from -0.21875 to 0.21875
- ffn_in_bias: bfloat16 [2, 3072], P('section'), may hold values from -1 to 1
- ffn_out: bfloat16 [2, 3072, 768], P('section'), may hold values from -0.21875 to 0.21875
- ffn_out_bias: bfloat16 [2, 768], P('section'), may hold values from -1 to 1
- norm2_gain: bfloat16 [2, 768], P('section'), may hold values from 0.5 to 1.5
- norm2_shift: bfloat16 [2, 768], P('section'), may hold values from -1 to 1
- content_cot: bfloat16 [2, 32, 128, 768], P('section', 'dp'), may hold values from -6 to 6
- query_cot: bfloat16 [2, 32, 128, 768], P('section', 'dp'), may hold values from -6 to 6
Outputs:
- content_out: bfloat16 [2, 32, 128, 768], P('section', 'dp')
- query_out: bfloat16 [2, 32, 128, 768], P('section', 'dp')
- input_grad: bfloat16 [2, 32, 128, 768], P('section', 'dp')
- mask_grad: float32 [768], replicated
- grad_w_query: float32 [2, 768, 768], P('section')
- grad_w_key: float32 [2, 768, 768], P('section')
- grad_w_value: float32 [2, 768, 768], P('section')
- grad_w_out: float32 [2, 768, 768], P('section')
- grad_w_rel: float32 [2, 768, 768], P('section')
- grad_bias_content: float32 [2, 12, 64], P('section')
- grad_bias_position: float32 [2, 12, 64], P('section')
- grad_bias_segment: float32 [2, 12, 64], P('section')
- grad_seg_embed: float32 [2, 2, 12, 64], P('section')
- grad_norm1_gain: float32 [2, 768], P('section')
- grad_norm1_shift: float32 [2, 768], P('section')
- grad_ffn_in: float32 [2, 768, 3072], P('section')
- grad_ffn_in_bias: float32 [2, 3072], P('section')
- grad_ffn_out: float32 [2, 3072, 768], P('section')
- grad_ffn_out_bias: float32 [2, 768], P('section')
- grad_norm2_gain: float32 [2, 768], P('section')
- grad_norm2_shift: float32 [2, 768], P('section')
The draws below stay inside these ranges and needn't reach their ends.
Inputs may be any that keep to these rules, and one draw needn't show every extreme that they name: `doc_ids`: each row's document numbers never fall; every document has 1 to 64 rows and one has exactly 64. `orders`: each row is a permutation of 0 to 127. `slot_used`: in each aligned block of 2 entries at least one is 1.
All inputs are finite; a program needn't handle non-finite values. No bound on the sum of `targets` on one device may be relied on, other than what follows from the above.
Results may differ from the reference program's by a relative error of at most 0.035.
Values may be sent and summed in bfloat16 or wider, within the bound.
No kernel may reach another device: no remote copies, remote signals or barrier semaphores. Data moves between devices by JAX's collectives and lax.ppermute only.
A program may use at most 256 MiB of HBM per device.

```python
import math
import jax
import jax.numpy as jnp
import numpy as np
from jax import lax

D = 768
HEADS = 12
HEAD_DIM = 64
FF = 3072
SEG = 128
MEM = 128
SLOTS = 2
LAYERS = 2
SEQS = 32
KR = 384


def draw_slot_used(key, part):
    key = jax.random.fold_in(key, 11)
    coin_key, pick_key = jax.random.split(key)
    replicas = SEQS // SLOTS
    tosses = jax.random.randint(coin_key, (replicas, SLOTS), 0, 5)
    chosen = jax.random.randint(pick_key, (replicas, 1), 0, SLOTS)
    column_ids = jnp.arange(SLOTS)[None, :]
    slot_flags = jnp.maximum((tosses < 3).astype(jnp.int32), (column_ids == chosen).astype(jnp.int32))
    return slot_flags.reshape(SEQS)


def plant(entries, rng, smallest, high):
    shape = entries.shape
    spot = [jax.random.randint(jax.random.fold_in(rng, axis), (), 0, shape[axis]) for axis in range(len(shape))]
    entries = entries.at[tuple(spot)].set(smallest)
    longest = shape.index(max(shape))
    spot[longest] = (spot[longest] + 1) % shape[longest]
    return entries.at[tuple(spot)].set(high)


def block_scale(key, extent, pieces, low, high):
    def one(dim, blocks):
        steps = jax.random.uniform(jax.random.fold_in(jax.random.fold_in(key, 6), dim), (blocks,), jnp.float32, low / len(pieces), high / len(pieces))
        return jnp.repeat(jnp.exp(steps), extent[dim] // blocks).reshape((-1,) + (1,) * (len(extent) - dim - 1))

    level = one(*pieces[0])
    for cut in pieces[1:]:
        level = level * one(*cut)
    return level


def length_profile(count, total, most, skew):
    portions = [(1 << 20) // math.isqrt(standing ** skew) + 1 for standing in range(2, count + 1)]
    surplus, holding = total - most - (count - 1), [1] * (count - 1)
    while surplus > 0:
        movable = [i for i in range(count - 1) if holding[i] < most]
        pool, budget = sum([portions[i] for i in movable]), surplus
        for i in movable:
            addition = min(most - holding[i], max(1, budget * portions[i] // pool), surplus)
            holding[i] = holding[i] + addition
            surplus = surplus - addition
    return np.array([most] + holding)


def ragged(key, number_of, total, limit, skew):
    if number_of == 2:
        one = jax.random.randint(key, (), max(1, total - limit), min(limit, total - 1) + 1)
        return jnp.stack([one, total - one])
    sizes = jnp.asarray(length_profile(number_of, total, limit, skew), jnp.int32)
    twos = (number_of - 1) // 2
    donor, taker = sizes[1:1 + 2 * twos:2], sizes[2:2 + 2 * twos:2]
    room = jnp.minimum(donor - 1, limit - taker)
    shifted = jax.random.randint(jax.random.fold_in(key, 1), (twos,), 0, 1 << 20) % (room + 1)
    sizes = sizes.at[1:1 + 2 * twos:2].set(donor - shifted).at[2:2 + 2 * twos:2].set(taker + shifted)
    return sizes[jax.random.permutation(jax.random.fold_in(key, 2), number_of)]


def scatter_about(rng, shape, deviation, bound, cuts=(), held_as=jnp.bfloat16):
    values = deviation * jax.random.normal(rng, shape, jnp.float32)
    if cuts:
        values = values * block_scale(rng, shape, cuts, -0.22, 0.18)
    return jnp.clip(values, -bound, bound).astype(held_as)


def setup_inputs(seed: int = 0) -> dict:
    keys = jax.random.split(jax.random.key(seed), 27)
    return {
        "content_in": scatter_about(keys[0], (SEQS, SEG, D), 1.0, 6.0, ((0, 16),)),
        "memory": scatter_about(keys[1], (LAYERS, SEQS, MEM, D), 1.0, 6.0, ((0, 2), (1, 16))),
        "mask_embed": scatter_about(keys[2], (D,), 1.0, 5.0),
        "doc_ids": jax.vmap(lambda own: jnp.searchsorted(jnp.cumsum(ragged(own, 4, SEG, SEG // 2, 0)), jnp.arange(SEG), side="right"))(jax.random.split(keys[3], SEQS)).reshape((SEQS, SEG)).astype(jnp.int32),
        "orders": jax.vmap(lambda own: jax.random.permutation(own, SEG))(jax.random.split(keys[4], SEQS)).reshape((SEQS, SEG)).astype(jnp.int32),
        "targets": plant((jax.random.randint(keys[5], (SEQS, SEG), 0, 3) < 1).astype(jnp.int32), jax.random.fold_in(keys[5], 1), 0, 1),
        "slot_used": draw_slot_used(jax.random.fold_in(keys[26], 71), 0),
        "w_query": scatter_about(keys[7], (LAYERS, D, D), D ** -0.5, 0.21875, ((0, 2),)),
        "w_key": scatter_about(keys[8], (LAYERS, D, D), D ** -0.5, 0.21875, ((0, 2),)),
        "w_value": scatter_about(keys[9], (LAYERS, D, D), D ** -0.5, 0.21875, ((0, 2),)),
        "w_out": scatter_about(keys[10], (LAYERS, D, D), (max(D // 256, 1)) ** -0.5, 3.5, ((0, 2),)),
        "w_rel": scatter_about(keys[11], (LAYERS, D, D), D ** -0.5, 0.21875, ((0, 2),)),
        "bias_content": scatter_about(keys[12], (LAYERS, HEADS, HEAD_DIM), 0.5, 3.0, ((0, 2),)),
        "bias_position": scatter_about(keys[13], (LAYERS, HEADS, HEAD_DIM), 0.5, 3.0, ((0, 2),)),
        "bias_segment": scatter_about(keys[14], (LAYERS, HEADS, HEAD_DIM), 0.5, 3.0, ((0, 2),)),
        "seg_embed": scatter_about(keys[15], (LAYERS, 2, HEADS, HEAD_DIM), 0.5, 3.0, ((0, 2),)),
        "norm1_gain": jnp.clip(1.0 + 0.1 * jax.random.normal(keys[16], (LAYERS, D), jnp.float32), 0.5, 1.5).astype(jnp.bfloat16),
        "norm1_shift": scatter_about(keys[17], (LAYERS, D), 0.2, 1.0, ((0, 2),)),
        "ffn_in": scatter_about(keys[18], (LAYERS, D, FF), D ** -0.5, 0.21875, ((0, 2),)),
        "ffn_in_bias": scatter_about(keys[19], (LAYERS, FF), 0.2, 1.0, ((0, 2),)),
        "ffn_out": scatter_about(keys[20], (LAYERS, FF, D), (FF // 4) ** -0.5, 0.21875, ((0, 2),)),
        "ffn_out_bias": scatter_about(keys[21], (LAYERS, D), 0.2, 1.0, ((0, 2),)),
        "norm2_gain": jnp.clip(1.0 + 0.1 * jax.random.normal(keys[22], (LAYERS, D), jnp.float32), 0.5, 1.5).astype(jnp.bfloat16),
        "norm2_shift": scatter_about(keys[23], (LAYERS, D), 0.2, 1.0, ((0, 2),)),
        "content_cot": scatter_about(keys[24], (LAYERS, SEQS, SEG, D), 1.0, 6.0, ((0, 2), (1, 16))),
        "query_cot": scatter_about(keys[25], (LAYERS, SEQS, SEG, D), 1.0, 6.0, ((0, 2), (1, 16))),
    }


@jax.custom_vjp
def low(v):
    return lax.optimization_barrier(v.astype(jnp.bfloat16)).astype(jnp.float32)

@jax.custom_vjp
def low_back(v):
    return v

def low_keep(v):
    return (low(v), None)

def low_pass(kept, grad):
    return (grad,)

def back_keep(v):
    return (v, None)

def back_low(kept, grad):
    return (low(grad),)
low.defvjp(low_keep, low_pass)
low_back.defvjp(back_keep, back_low)
HIGHEST_PRECISION = lax.Precision.HIGHEST
NEG_FILL = -1e+30
NORM_EPS = 1e-05

def rounded_both(values_in):
    return low(low_back(values_in))

def matmul_exact(left, right):
    return jnp.dot(left, right, precision=HIGHEST_PRECISION)

def layer_norm(values_in, gain, shift):
    center = lax.optimization_barrier(jnp.mean(values_in, axis=-1, keepdims=True))
    offset = values_in - center
    spread = lax.optimization_barrier(jnp.mean(offset * offset, axis=-1, keepdims=True))
    return offset * lax.rsqrt(spread + NORM_EPS) * gain + shift

def position_table(total_rows, width_model, mem_rows, seg_rows):
    row_ids = jnp.arange(total_rows, dtype=jnp.float32)
    distance = mem_rows + seg_rows - 1 - row_ids
    freqs = 1.0 / 10000.0 ** (jnp.arange(0, width_model, 2, dtype=jnp.float32) / width_model)
    angles = distance[:, None] * freqs[None, :]
    return jnp.concatenate([jnp.sin(angles), jnp.cos(angles)], axis=1)

def shift_rows(full_block, key_count):
    row_count = full_block.shape[-2]
    width_full = full_block.shape[-1]
    leading = full_block.shape[:-2]
    flat_block = full_block.reshape(leading + (row_count * width_full,))
    part_block = flat_block[..., row_count - 1:row_count - 1 + row_count * (width_full - 1)]
    return part_block.reshape(leading + (row_count, width_full - 1))[..., :key_count]

def attention_masks(doc_row, order_row, target_row, mem_rows):
    seg_rows = doc_row.shape[0]
    places = jnp.arange(seg_rows)
    same_doc = doc_row[:, None] == doc_row[None, :]
    visible = same_doc & ((target_row[None, :] == 0) | (order_row[None, :] <= order_row[:, None]))
    visible_query = visible & (places[:, None] != places[None, :])
    memory_part = jnp.ones((seg_rows, mem_rows), dtype=jnp.bool_)
    content_mask = jnp.concatenate([memory_part, visible], axis=1)
    query_mask = jnp.concatenate([memory_part, visible_query], axis=1)
    other_doc = jnp.concatenate([jnp.ones((seg_rows, mem_rows), jnp.float32), (doc_row[:, None] != doc_row[None, :]).astype(jnp.float32)], axis=1)
    return (content_mask, query_mask, other_doc)

def attend_stream(queries, keys_heads, values_heads, rel_heads, other_doc, allowed, bias_content, bias_position, bias_segment, seg_embed, score_scale):
    query_content = low(queries + bias_content)
    query_position = low(queries + bias_position)
    query_segment = low(queries + bias_segment)
    content_part = jnp.einsum('ihd,jhd->hij', query_content, keys_heads, precision=HIGHEST_PRECISION)
    full_position = jnp.einsum('ihd,khd->hik', query_position, rel_heads, precision=HIGHEST_PRECISION)
    position_part = shift_rows(full_position, keys_heads.shape[0])
    segment_pair = jnp.einsum('ihd,shd->hsi', query_segment, seg_embed, precision=HIGHEST_PRECISION)
    segment_part = segment_pair[:, 0, :, None] * (1.0 - other_doc) + segment_pair[:, 1, :, None] * other_doc
    scores = low_back((content_part + position_part + segment_part) * score_scale)
    masked = jnp.where(allowed[None], scores, NEG_FILL)
    row_peak = lax.optimization_barrier(jnp.max(masked, axis=-1, keepdims=True))
    exp_scores = jnp.exp(masked - row_peak)
    attn_probs = exp_scores / lax.optimization_barrier(jnp.sum(exp_scores, axis=-1, keepdims=True))
    mixed_rows = jnp.einsum('hij,jhd->ihd', low(attn_probs), values_heads, precision=HIGHEST_PRECISION)
    return rounded_both(mixed_rows.reshape(queries.shape[0], -1))

def full_layer(layer_params, content_rows, query_rows, memory_rows, mask_set, pos_rows, score_scale):
    w_query, w_key, w_value, w_out, w_rel, bias_content, bias_position, bias_segment, seg_embed, norm1_gain, norm1_shift, ffn_in, ffn_in_bias, ffn_out, ffn_out_bias, norm2_gain, norm2_shift = layer_params
    head_count, head_dim = bias_content.shape
    seg_rows = content_rows.shape[0]
    joined = jnp.concatenate([memory_rows, content_rows], axis=0)
    keys_heads = rounded_both(matmul_exact(joined, w_key)).reshape(-1, head_count, head_dim)
    values_heads = rounded_both(matmul_exact(joined, w_value)).reshape(-1, head_count, head_dim)
    rel_heads = rounded_both(matmul_exact(pos_rows, w_rel)).reshape(-1, head_count, head_dim)
    content_mask, query_mask, other_doc = mask_set
    results = []
    for stream_rows, allowed in ((content_rows, content_mask), (query_rows, query_mask)):
        queries = low_back(matmul_exact(stream_rows, w_query)).reshape(seg_rows, head_count, head_dim)
        mixed_rows = attend_stream(queries, keys_heads, values_heads, rel_heads, other_doc, allowed, bias_content, bias_position, bias_segment, seg_embed, score_scale)
        attn_rows = low_back(matmul_exact(mixed_rows, w_out))
        middle = layer_norm(attn_rows + stream_rows, norm1_gain, norm1_shift)
        inner_pre = low_back(matmul_exact(low(middle), ffn_in) + ffn_in_bias)
        active = low(jax.nn.gelu(inner_pre, approximate=True))
        outer_rows = low_back(matmul_exact(active, ffn_out) + ffn_out_bias)
        results.append(layer_norm(outer_rows + middle, norm2_gain, norm2_shift))
    return (results[0], results[1])

def reference(content_in, memory, mask_embed, doc_ids, orders, targets, slot_used, w_query, w_key, w_value, w_out, w_rel, bias_content, bias_position, bias_segment, seg_embed, norm1_gain, norm1_shift, ffn_in, ffn_in_bias, ffn_out, ffn_out_bias, norm2_gain, norm2_shift, content_cot, query_cot):
    weight_set = tuple((weight.astype(jnp.float32) for weight in (w_query, w_key, w_value, w_out, w_rel, bias_content, bias_position, bias_segment, seg_embed, norm1_gain, norm1_shift, ffn_in, ffn_in_bias, ffn_out, ffn_out_bias, norm2_gain, norm2_shift)))
    start_vec = mask_embed.astype(jnp.float32)
    pos_rows = low(position_table(KR, D, MEM, SEG))
    score_scale = HEAD_DIM ** (-0.5)
    seq_count = content_in.shape[0]

    def one_sequence(carry, seq_index):
        grad_total, start_total = carry
        content_rows = content_in[seq_index].astype(jnp.float32)
        slot_weight = (slot_used[seq_index] > 0).astype(jnp.float32)
        mask_set = attention_masks(doc_ids[seq_index], orders[seq_index], targets[seq_index], MEM)
        first_memory = memory[0, seq_index].astype(jnp.float32)
        second_memory = memory[1, seq_index].astype(jnp.float32)

        def forward(weights_in, start_in, content_part, probe_rows):
            first_layer = tuple((weight[0] for weight in weights_in))
            second_layer = tuple((weight[1] for weight in weights_in))
            query_rows = jnp.broadcast_to(start_in, content_part.shape)
            mid_content, mid_query = full_layer(first_layer, content_part, query_rows, first_memory, mask_set, pos_rows, score_scale)
            sent_content = rounded_both(mid_content + probe_rows)
            sent_query = rounded_both(mid_query)
            last_content, last_query = full_layer(second_layer, sent_content, sent_query, second_memory, mask_set, pos_rows, score_scale)
            return (mid_content * slot_weight, mid_query * slot_weight, last_content * slot_weight, last_query * slot_weight)
        results, pullback = jax.vjp(forward, weight_set, start_vec, content_rows, jnp.zeros_like(content_rows))
        cotangents = (content_cot[0, seq_index].astype(jnp.float32), query_cot[0, seq_index].astype(jnp.float32), content_cot[1, seq_index].astype(jnp.float32), query_cot[1, seq_index].astype(jnp.float32))
        grad_weights, grad_start, grad_content, grad_probe = pullback(cotangents)
        grad_total = jax.tree.map(jnp.add, grad_total, grad_weights)
        return ((grad_total, start_total + grad_start), results + (grad_content, grad_probe))
    initial = (tuple((jnp.zeros_like(weight) for weight in weight_set)), jnp.zeros_like(start_vec))
    (grad_total, start_total), stacked = lax.scan(one_sequence, initial, jnp.arange(seq_count))
    mid_content, mid_query, last_content, last_query, grad_content, grad_probe = stacked
    content_out = jnp.stack([mid_content, last_content]).astype(jnp.bfloat16)
    query_out = jnp.stack([mid_query, last_query]).astype(jnp.bfloat16)
    input_grad = jnp.stack([grad_content, grad_probe]).astype(jnp.bfloat16)
    return (content_out, query_out, input_grad, start_total, grad_total[0], grad_total[1], grad_total[2], grad_total[3], grad_total[4], grad_total[5], grad_total[6], grad_total[7], grad_total[8], grad_total[9], grad_total[10], grad_total[11], grad_total[12], grad_total[13], grad_total[14], grad_total[15], grad_total[16])
```

```python
import functools

import jax
import jax.numpy as jnp
import numpy as np
from jax import lax
from jax.experimental import pallas as pl
from jax.experimental.pallas import tpu as pltpu
from jax.sharding import PartitionSpec as P

BF16 = jnp.bfloat16
F32 = jnp.float32
NEG_FILL = -1e30
NORM_EPS = 1e-05
GELU_A = 0.7978845608028654
GELU_B = 0.044715
VMEM_LIMIT = 60 * 1024 * 1024
LANES = 128

ROW_BC, ROW_BP, ROW_BS, ROW_SEG0, ROW_SEG1 = 0, 1, 2, 3, 4
ROW_N1G, ROW_N1S, ROW_FOB, ROW_N2G, ROW_N2S, ROW_MASK, ROW_FIB = 5, 6, 7, 8, 9, 10, 11
SMALL_ROWS = 16


def dot_nn(left, right):
    return jnp.dot(left, right, preferred_element_type=F32)


def dot_nt(left, right):
    return lax.dot_general(left, right, (((1,), (1,)), ((), ())), preferred_element_type=F32)


def dot_tn(left, right):
    return lax.dot_general(left, right, (((0,), (0,)), ((), ())), preferred_element_type=F32)


def col_sum(block):
    return jnp.sum(block, axis=0, keepdims=True)


def norm_parts(rows):
    center = jnp.mean(rows, axis=-1, keepdims=True)
    offset = rows - center
    spread = jnp.mean(offset * offset, axis=-1, keepdims=True)
    scale = lax.rsqrt(spread + NORM_EPS)
    return offset * scale, scale


def norm_back(grad, unit, scale, gain):
    inner = grad * gain
    mean_inner = jnp.mean(inner, axis=-1, keepdims=True)
    mean_cross = jnp.mean(inner * unit, axis=-1, keepdims=True)
    return (inner - mean_inner - unit * mean_cross) * scale


def half_masks():
    lane = lax.broadcasted_iota(jnp.int32, (1, LANES), 1)
    low = lane < LANES // 2
    return low, low.astype(F32).astype(BF16), (~low).astype(F32).astype(BF16)


def stack_heads(block, low_b, high_b):
    return jnp.concatenate([block * low_b, block * high_b], axis=0)


def copy_in(pairs, sems):
    copies = [
        pltpu.make_async_copy(src, dst, sems.at[n]) for n, (src, dst) in enumerate(pairs)
    ]
    for copy in copies:
        copy.start()
    return copies


def forward_body(section, slot, names_in, names_out, names_scratch, *refs):
    count_in, count_out = len(names_in), len(names_out)
    r = dict(zip(names_in, refs[:count_in]))
    o = dict(zip(names_out, refs[count_in : count_in + count_out]))
    s = dict(zip(names_scratch, refs[count_in + count_out :]))
    meta = r["meta"]
    seg_rows, width = s["stream"].shape[0] // 2, s["stream"].shape[1]
    key_rows = s["joined"].shape[0]
    pairs_count = width // LANES
    ff = s["act"].shape[1]
    score_scale = 0.125

    @pl.when(meta[0] == section)
    def _run():
        sem_in, sem_out = s["sem_in"], s["sem_out"]
        mem_rows = key_rows - seg_rows
        x_src = r["content_in"].at[slot] if section == 0 else r["arrived"].at[pl.ds(0, seg_rows)]
        loads = [
            (r["memory"].at[0, slot], s["joined"].at[pl.ds(0, mem_rows)]),
            (x_src, s["joined"].at[pl.ds(mem_rows, seg_rows)]),
            (x_src, s["stream"].at[pl.ds(0, seg_rows)]),
            (r["w_key"].at[0], s["wk"]),
            (r["w_query"].at[0], s["wq"]),
            (r["rel"], s["rel"]),
            (r["w_value"].at[0], s["wv"]),
            (r["w_out"].at[0], s["wo"]),
            (r["ffn_in"].at[0], s["fi"]),
            (r["ffn_out"].at[0], s["fo"]),
        ]
        if section == 1:
            loads.append(
                (r["arrived"].at[pl.ds(seg_rows, seg_rows)], s["stream"].at[pl.ds(seg_rows, seg_rows)])
            )
        moves = copy_in(loads, sem_in)
        stores = []

        def store(name, src):
            copy = pltpu.make_async_copy(src, o[name].at[slot], sem_out.at[len(stores)])
            copy.start()
            stores.append(copy)

        small = r["small"]
        used = meta[1 + slot].astype(F32)
        if section == 0:
            s["stream"][seg_rows:, :] = jnp.broadcast_to(
                small[ROW_MASK : ROW_MASK + 1, :], (seg_rows, width)
            ).astype(BF16)
        square = (seg_rows, seg_rows)
        doc = jnp.broadcast_to(r["docs"][slot : slot + 1, :].astype(F32), square)
        order = jnp.broadcast_to(r["orders"][slot : slot + 1, :].astype(F32), square)
        target = jnp.broadcast_to(r["targets"][slot : slot + 1, :].astype(F32), square)
        same = doc == doc.T
        visible = same & ((target == 0.0) | (order <= order.T))
        row_id = lax.broadcasted_iota(jnp.int32, square, 0)
        col_id = lax.broadcasted_iota(jnp.int32, square, 1)
        s["same"][...] = same.astype(F32)
        s["bias"][0] = jnp.where(visible, 0.0, NEG_FILL)
        s["bias"][1] = jnp.where(visible & (row_id != col_id), 0.0, NEG_FILL)

        for n in (0, 1, 3):
            moves[n].wait()
        s["k"][...] = dot_nn(s["joined"][...], s["wk"][...]).astype(BF16)
        store("k", s["k"])
        store("joined", s["joined"])
        moves[2].wait()
        if section == 1:
            moves[10].wait()
        store("stream", s["stream"])
        moves[4].wait()
        queries = dot_nn(s["stream"][...], s["wq"][...])
        for name, row in (("qc", ROW_BC), ("qp", ROW_BP), ("qs", ROW_BS)):
            with_bias = (queries + small[row : row + 1, :]).astype(BF16)
            s[name][...] = (with_bias.astype(F32) * score_scale).astype(BF16)
            store(name, s[name])
        moves[6].wait()
        s["v"][...] = dot_nn(s["joined"][...], s["wv"][...]).astype(BF16)
        store("v", s["v"])
        moves[5].wait()

        low, low_b, high_b = half_masks()
        same_f = s["same"][...]
        bias_by_stream = [s["bias"][0], s["bias"][1]]
        for pair in range(pairs_count):
            sl = slice(pair * LANES, (pair + 1) * LANES)
            content = dot_nt(stack_heads(s["qc"][:, sl], low_b, high_b), s["k"][:, sl])
            position = dot_nt(stack_heads(s["qp"][:, sl], low_b, high_b), s["rel"][:, sl])
            seg = small[ROW_SEG0 : ROW_SEG1 + 1, sl]
            lane8 = lax.broadcasted_iota(jnp.int32, (8, LANES), 1)
            row8 = lax.broadcasted_iota(jnp.int32, (8, LANES), 0)
            seg8 = jnp.where(row8 % 2 == 0, seg[0:1, :], seg[1:2, :])
            seg8 = jnp.where((row8 < 4) & ((row8 < 2) == (lane8 < LANES // 2)), seg8, 0.0)
            pieces = dot_nt(s["qs"][:, sl], seg8.astype(BF16))
            probs_pair = []
            for head in range(2):
                probs_streams = []
                for stream in range(2):
                    base = (2 * head + stream) * seg_rows
                    rolled = pltpu.roll(
                        position[base : base + seg_rows, :], key_rows + 1, axis=1, stride=1, stride_axis=0
                    )
                    rows = slice(stream * seg_rows, (stream + 1) * seg_rows)
                    same_part = pieces[rows, 2 * head : 2 * head + 1]
                    other_part = pieces[rows, 2 * head + 1 : 2 * head + 2]
                    body = content[base : base + seg_rows, :] + rolled[:, :key_rows] + other_part
                    left = body[:, :mem_rows]
                    right = (
                        body[:, mem_rows:] + (same_part - other_part) * same_f + bias_by_stream[stream]
                    )
                    peak = jnp.maximum(
                        jnp.max(left, axis=-1, keepdims=True), jnp.max(right, axis=-1, keepdims=True)
                    )
                    left = jnp.exp(left - peak)
                    right = jnp.exp(right - peak)
                    total = jnp.sum(left + right, axis=-1, keepdims=True)
                    inverse = 1.0 / total
                    probs_streams.append(
                        jnp.concatenate([left * inverse, right * inverse], axis=1).astype(BF16)
                    )
                probs = jnp.concatenate(probs_streams, axis=0)
                s["p"][2 * pair + head] = probs
                probs_pair.append(probs)
            mixed = dot_nn(
                jnp.concatenate(probs_pair, axis=1), stack_heads(s["v"][:, sl], low_b, high_b)
            )
            s["mixed"][:, sl] = mixed.astype(BF16)
        store("p", s["p"])
        store("mixed", s["mixed"])

        moves[7].wait()
        middle_in = dot_nn(s["mixed"][...], s["wo"][...]) + s["stream"][...].astype(F32)
        s["mid_in"][...] = middle_in
        store("mid_in", s["mid_in"])
        unit, _ = norm_parts(middle_in)
        middle = unit * small[ROW_N1G : ROW_N1G + 1, :] + small[ROW_N1S : ROW_N1S + 1, :]
        s["midb"][...] = middle.astype(BF16)
        copy = pltpu.make_async_copy(s["midb"], o["me"].at[0, slot], sem_out.at[len(stores)])
        copy.start()
        stores.append(copy)
        s["outer"][...] = middle + small[ROW_FOB : ROW_FOB + 1, :]
        moves[8].wait()
        moves[9].wait()
        for step in range(ff // width):
            cols = slice(step * width, (step + 1) * width)
            inner = (
                dot_nn(s["midb"][...], s["fi"][:, cols])
                + small[ROW_FIB + step : ROW_FIB + step + 1, :]
            )
            square_in = inner * inner
            wave = jnp.tanh(GELU_A * inner * (1.0 + GELU_B * square_in))
            half = 0.5 * (1.0 + wave)
            active = (inner * half).astype(BF16)
            slope = half + (0.5 * GELU_A) * inner * (1.0 - wave * wave) * (1.0 + 3.0 * GELU_B * square_in)
            s["act"][:, cols] = active
            s["slope"][:, cols] = slope.astype(BF16)
            s["outer"][...] += dot_nn(active, s["fo"][cols, :])
        copy = pltpu.make_async_copy(s["act"], o["ua"].at[1, slot], sem_out.at[len(stores)])
        copy.start()
        stores.append(copy)
        store("slope", s["slope"])
        store("outer", s["outer"])
        unit, _ = norm_parts(s["outer"][...])
        result = unit * small[ROW_N2G : ROW_N2G + 1, :] + small[ROW_N2S : ROW_N2S + 1, :]
        s["out"][...] = (result * used).astype(BF16)
        for name, first in (("content_out", 0), ("query_out", seg_rows)):
            copy = pltpu.make_async_copy(
                s["out"].at[pl.ds(first, seg_rows)], o[name].at[0, slot], sem_out.at[len(stores)]
            )
            copy.start()
            stores.append(copy)
        if "sent" in o:
            copy = pltpu.make_async_copy(s["out"], o["sent"], sem_out.at[len(stores)])
            copy.start()
            stores.append(copy)
        for copy in stores:
            copy.wait()


def tail_body(section, slot, names_in, names_out, names_scratch, *refs):
    count_in, count_out = len(names_in), len(names_out)
    r = dict(zip(names_in, refs[:count_in]))
    o = dict(zip(names_out, refs[count_in : count_in + count_out]))
    s = dict(zip(names_scratch, refs[count_in + count_out :]))
    meta = r["meta"]
    rows, width = s["outer"].shape
    seg_rows = rows // 2
    ff = s["slope"].shape[1]

    @pl.when(meta[0] == section)
    def _run():
        sem_in, sem_out = s["sem_in"], s["sem_out"]
        loads = [
            (r["outer"].at[slot], s["outer"]),
            (r["content_cot"].at[0, slot], s["cot"].at[pl.ds(0, seg_rows)]),
            (r["query_cot"].at[0, slot], s["cot"].at[pl.ds(seg_rows, seg_rows)]),
            (r["ffn_out"].at[0], s["fo"]),
            (r["slope"].at[slot], s["slope"]),
            (r["ffn_in"].at[0], s["fi"]),
            (r["mid_in"].at[slot], s["mid_in"]),
        ]
        if section == 0:
            loads.append((r["returned"], s["returned"]))
        moves = copy_in(loads, sem_in)
        stores = []

        def store(src, dst):
            copy = pltpu.make_async_copy(src, dst, sem_out.at[len(stores)])
            copy.start()
            stores.append(copy)

        small = r["small"]
        used = meta[1 + slot].astype(F32)
        for n in (0, 1, 2):
            moves[n].wait()
        grad = s["cot"][...].astype(F32) * used
        if section == 0:
            moves[7].wait()
            grad = grad + s["returned"][...].astype(F32)
        unit, scale = norm_parts(s["outer"][...])
        out = s["sums"]
        out[...] = jnp.zeros_like(out)
        out[4:5, :] = col_sum(grad * unit)
        out[5:6, :] = col_sum(grad)
        grad_outer = norm_back(grad, unit, scale, small[ROW_N2G : ROW_N2G + 1, :])
        s["e"][...] = grad_outer.astype(BF16)
        store(s["e"], o["me"].at[1, slot])
        out[3:4, :] = col_sum(s["e"][...].astype(F32))
        s["acc"][...] = grad_outer
        moves[3].wait()
        moves[4].wait()
        moves[5].wait()
        for step in range(ff // width):
            cols = slice(step * width, (step + 1) * width)
            grad_active = dot_nt(s["e"][...], s["fo"][cols, :])
            inner_b = (s["slope"][:, cols].astype(F32) * grad_active).astype(BF16)
            s["u"][:, cols] = inner_b
            out[8 + step : 9 + step, :] = col_sum(inner_b.astype(F32))
            s["acc"][...] += dot_nt(inner_b, s["fi"][:, cols])
        store(s["u"], o["ua"].at[0, slot])
        moves[6].wait()
        unit, scale = norm_parts(s["mid_in"][...])
        grad = s["acc"][...]
        out[1:2, :] = col_sum(grad * unit)
        out[2:3, :] = col_sum(grad)
        s["a"][...] = norm_back(grad, unit, scale, small[ROW_N1G : ROW_N1G + 1, :])
        s["ab"][...] = s["a"][...].astype(BF16)
        store(s["a"], o["a"])
        store(s["ab"], o["ab"].at[slot])
        store(s["sums"], o["sums_tail"].at[slot])
        for copy in stores:
            copy.wait()


def head_body(section, slot, names_in, names_out, names_scratch, *refs):
    count_in, count_out = len(names_in), len(names_out)
    r = dict(zip(names_in, refs[:count_in]))
    o = dict(zip(names_out, refs[count_in : count_in + count_out]))
    s = dict(zip(names_scratch, refs[count_in + count_out :]))
    meta = r["meta"]
    rows, width = s["a"].shape
    seg_rows = rows // 2
    key_rows = s["k"].shape[0]
    rel_rows = s["rel"].shape[0]
    mem_rows = key_rows - seg_rows
    pairs_count = width // LANES
    score_scale = 0.125

    @pl.when(meta[0] == section)
    def _run():
        sem_in, sem_out = s["sem_in"], s["sem_out"]
        loads = [
            (r["ab"].at[slot], s["ab"]),
            (r["w_out"].at[0], s["wo"]),
            (r["v"].at[slot], s["v"]),
            (r["p"].at[slot], s["p"]),
            (r["k"].at[slot], s["k"]),
            (r["qc"].at[slot], s["qc"]),
            (r["qp"].at[slot], s["qp"]),
            (r["qs"].at[slot], s["qs"]),
            (r["rel"], s["rel"]),
            (r["w_query"].at[0], s["wq"]),
            (r["w_key"].at[0], s["wk"]),
            (r["w_value"].at[0], s["wv"]),
            (r["a"], s["a"]),
        ]
        moves = copy_in(loads, sem_in)
        stores = []

        def store(src, dst):
            copy = pltpu.make_async_copy(src, dst, sem_out.at[len(stores)])
            copy.start()
            stores.append(copy)

        small = r["small"]
        square = (seg_rows, seg_rows)
        doc = jnp.broadcast_to(r["docs"][slot : slot + 1, :].astype(F32), square)
        same_one = (doc == doc.T).astype(F32)
        same = jnp.concatenate([same_one, same_one], axis=0)
        flip_rows = lax.broadcasted_iota(jnp.int32, (rows, rows), 0)
        flip_cols = lax.broadcasted_iota(jnp.int32, (rows, rows), 1)
        flipped_to = jnp.where(flip_rows < seg_rows, seg_rows - 1, rows + seg_rows - 1) - flip_rows
        flip = (flip_cols == flipped_to).astype(F32).astype(BF16)
        out = s["sums"]
        out[...] = jnp.zeros_like(out)
        moves[0].wait()
        moves[1].wait()
        s["x"][...] = dot_nt(s["ab"][...], s["wo"][...]).astype(BF16)
        for n in (2, 3, 4, 5, 6, 7, 8):
            moves[n].wait()
        s["qpf"][...] = dot_nn(flip, s["qp"][...]).astype(BF16)

        low, low_b, high_b = half_masks()
        blank = jnp.zeros((seg_rows, rel_rows - key_rows), F32)
        for pair in range(pairs_count):
            sl = slice(pair * LANES, (pair + 1) * LANES)
            grads_mixed = stack_heads(s["x"][:, sl], low_b, high_b)
            grad_probs = dot_nt(grads_mixed, s["v"][:, sl])
            scores_b = []
            same_sums, other_sums = [], []
            for head in range(2):
                probs = s["p"][2 * pair + head].astype(F32)
                product = probs * grad_probs[head * rows : (head + 1) * rows, :]
                delta = jnp.sum(product, axis=-1, keepdims=True)
                rounded = (product - probs * delta).astype(BF16)
                scores_b.append(rounded)
                wide = rounded.astype(F32)
                right = wide[:, mem_rows:] * same
                same_sum = jnp.sum(right, axis=-1, keepdims=True)
                same_sums.append(same_sum)
                other_sums.append(
                    jnp.sum(wide[:, :mem_rows] + (wide[:, mem_rows:] - right), axis=-1, keepdims=True)
                )
            stacked = jnp.concatenate(scores_b, axis=0)
            beside = jnp.concatenate(scores_b, axis=1)
            probs_stacked = jnp.concatenate([s["p"][2 * pair], s["p"][2 * pair + 1]], axis=0)
            s["dv"][:, sl] = dot_tn(probs_stacked, grads_mixed).astype(BF16)
            s["dk"][:, sl] = dot_tn(stacked, stack_heads(s["qc"][:, sl], low_b, high_b)).astype(BF16)
            grad_content = dot_nn(beside, stack_heads(s["k"][:, sl], low_b, high_b)) * score_scale
            same_sel = jnp.where(low, same_sums[0], same_sums[1])
            other_sel = jnp.where(low, other_sums[0], other_sums[1])
            seg0 = small[ROW_SEG0 : ROW_SEG0 + 1, sl]
            seg1 = small[ROW_SEG1 : ROW_SEG1 + 1, sl]
            grad_segment = (same_sel * seg0 + other_sel * seg1) * score_scale
            qs = s["qs"][:, sl].astype(F32)
            out[0:1, sl] = col_sum(grad_content)
            out[2:3, sl] = col_sum(grad_segment)
            out[3:4, sl] = col_sum(same_sel * qs)
            out[4:5, sl] = col_sum(other_sel * qs)
            s["dq"][:, sl] = grad_content + grad_segment
            turned = dot_nn(flip, beside)
            shifted_heads = []
            for head in range(2):
                parts = []
                for stream in range(2):
                    block = turned[
                        stream * seg_rows : (stream + 1) * seg_rows,
                        head * key_rows : (head + 1) * key_rows,
                    ]
                    block = jnp.concatenate([block, blank], axis=1)
                    parts.append(pltpu.roll(block, 0, axis=1, stride=1, stride_axis=0).astype(BF16))
                shifted_heads.append(jnp.concatenate(parts, axis=0))
            grad_position = (
                dot_nn(
                    jnp.concatenate(shifted_heads, axis=1),
                    stack_heads(s["rel"][:, sl], low_b, high_b),
                )
                * score_scale
            )
            out[1:2, sl] = col_sum(grad_position)
            s["dqp"][:, sl] = grad_position
            s["drel"][:, sl] = dot_tn(
                jnp.concatenate(shifted_heads, axis=0),
                stack_heads(s["qpf"][:, sl], low_b, high_b),
            )
        store(s["dk"], o["dk"].at[slot])
        store(s["dv"], o["dv"].at[slot])
        store(s["drel"], o["drel"].at[slot])
        grad_position = s["dqp"][...]
        position_high = grad_position.astype(BF16)
        position_low = (grad_position - position_high.astype(F32)).astype(BF16)
        grad_queries = s["dq"][...] + dot_nn(flip, position_high) + dot_nn(flip, position_low)
        s["dqb"][...] = grad_queries.astype(BF16)
        store(s["dqb"], o["dq"].at[slot])
        for n in (9, 10, 11, 12):
            moves[n].wait()
        grad_rows = s["a"][...] + dot_nt(s["dqb"][...], s["wq"][...])
        grad_content = (
            grad_rows[:seg_rows, :]
            + dot_nt(s["dk"][mem_rows:, :], s["wk"][...])
            + dot_nt(s["dv"][mem_rows:, :], s["wv"][...])
        )
        grad_query = grad_rows[seg_rows:, :]
        s["out"][:seg_rows, :] = grad_content.astype(BF16)
        s["out"][seg_rows:, :] = grad_query.astype(BF16)
        store(s["out"].at[pl.ds(0, seg_rows)], o["input_grad"].at[0, slot])
        if "sent" in o:
            store(s["out"], o["sent"])
        if section == 0:
            out[5:6, :] = col_sum(grad_query)
        store(s["sums"], o["sums_head"].at[slot])
        for copy in stores:
            copy.wait()


ANY_SPEC = pl.BlockSpec(memory_space=pl.ANY)
SMEM_SPEC = pl.BlockSpec(memory_space=pltpu.SMEM)
VMEM_SPEC = pl.BlockSpec(memory_space=pltpu.VMEM)


def call_kernel(body, section, slot, inputs, carried, fresh, scratch, name, flops):
    names_in = list(inputs)
    arrays = [inputs[n][1] for n in names_in]
    specs = [inputs[n][0] for n in names_in]
    aliases = {}
    names_out = list(carried) + list(fresh)
    out_shapes = []
    for position, key in enumerate(carried):
        value = carried[key]
        out_shapes.append(jax.ShapeDtypeStruct(value.shape, value.dtype))
        if not isinstance(value, jax.ShapeDtypeStruct):
            aliases[len(arrays)] = position
            arrays.append(value)
            specs.append(ANY_SPEC)
            names_in.append("_" + key)
    out_shapes += [fresh[key] for key in fresh]
    results = pl.pallas_call(
        functools.partial(body, section, slot, names_in, names_out, list(scratch)),
        out_shape=tuple(out_shapes),
        in_specs=specs,
        out_specs=tuple(ANY_SPEC for _ in out_shapes),
        scratch_shapes=list(scratch.values()),
        input_output_aliases=aliases,
        compiler_params=pltpu.CompilerParams(vmem_limit_bytes=VMEM_LIMIT),
        cost_estimate=pl.CostEstimate(flops=flops, bytes_accessed=20_000_000, transcendentals=0),
        name=name,
    )(*arrays)
    named = dict(zip(names_out, results))
    return {k: named[k] for k in carried}, {k: named[k] for k in fresh}


GROUP = 16
RING = 8
HEAD_ROWS = 640
REST_ROWS = 128
COLS = 384
REL_PIECE = 48
B_ROWS = REST_ROWS + COLS + 64


def ffn_pieces_body(first, last, meta, me, ua_in, ua_out, e_half, own, other):
    first_piece = dot_tn(me[:, first:last], ua_in[...]).astype(BF16)
    second_piece = dot_tn(ua_out[:, first:last], e_half[...]).astype(BF16)
    low_core = meta[3] == 0

    @pl.when(low_core)
    def _low():
        own[0] = first_piece
        other[0] = second_piece

    @pl.when(~low_core)
    def _high():
        own[0] = second_piece
        other[0] = first_piece


def ffn_pieces(meta, me, ua):
    rows, width = me.shape[1] * me.shape[2], me.shape[3]
    ff = ua.shape[3]
    me2 = me.reshape(2, rows, width)
    ua2 = ua.reshape(2, rows, ff)
    piece = jax.ShapeDtypeStruct((RING, HEAD_ROWS, COLS), BF16)
    out_spec = pl.BlockSpec((1, HEAD_ROWS, COLS), lambda k: (k, 0, 0))
    squeezed = pl.Squeezed()
    return pl.pallas_call(
        functools.partial(ffn_pieces_body, 0, HEAD_ROWS),
        out_shape=(piece, piece),
        grid=(RING,),
        in_specs=[
            SMEM_SPEC,
            pl.BlockSpec((squeezed, rows, width), lambda k: (0, 0, 0)),
            pl.BlockSpec((squeezed, rows, COLS), lambda k: (0, 0, k)),
            pl.BlockSpec((squeezed, rows, width), lambda k: (1, 0, k // 2)),
            pl.BlockSpec((squeezed, rows, COLS), lambda k: (1, 0, k % 2)),
        ],
        out_specs=(out_spec, out_spec),
        compiler_params=pltpu.CompilerParams(vmem_limit_bytes=VMEM_LIMIT),
        cost_estimate=pl.CostEstimate(
            flops=4 * rows * HEAD_ROWS * COLS * RING, bytes_accessed=16_000_000, transcendentals=0
        ),
        name="ffn_pieces",
    )(meta, me2, ua2, ua2, me2)


def mixed_pieces_body(
    meta, me, ua_in, ua_out, e_half, stream, joined, mixed, dq, dk, dv, ab, rel, own, other
):
    step = pl.program_id(0)
    width = me.shape[1]
    low_core = meta[3] == 0

    def write(low_ref, high_ref):
        low_ref[0, :REST_ROWS] = dot_tn(me[:, HEAD_ROWS:], ua_in[...]).astype(BF16)
        high_ref[0, :REST_ROWS] = dot_tn(ua_out[:, HEAD_ROWS:], e_half[...]).astype(BF16)
        block = slice(REST_ROWS, REST_ROWS + COLS)

        @pl.when(step < RING // 2)
        def _early():
            low_ref[0, block] = dot_tn(stream[...], dq[...]).astype(BF16)
            high_ref[0, block] = dot_tn(joined[...], dv[...]).astype(BF16)

        @pl.when(step >= RING // 2)
        def _late():
            low_ref[0, block] = dot_tn(joined[...], dk[...]).astype(BF16)
            high_ref[0, block] = dot_tn(mixed[...], ab[...]).astype(BF16)

        rel_sum = (rel[0] + rel[1]).astype(BF16)
        low_ref[0, REST_ROWS + COLS : REST_ROWS + COLS + REL_PIECE] = rel_sum[:, :COLS]
        high_ref[0, REST_ROWS + COLS : REST_ROWS + COLS + REL_PIECE] = rel_sum[:, COLS:]
        blank = jnp.zeros((B_ROWS - REST_ROWS - COLS - REL_PIECE, COLS), BF16)
        low_ref[0, REST_ROWS + COLS + REL_PIECE :] = blank
        high_ref[0, REST_ROWS + COLS + REL_PIECE :] = blank

    @pl.when(low_core)
    def _low():
        write(own, other)

    @pl.when(~low_core)
    def _high():
        write(other, own)


def mixed_pieces(meta, me, ua, stream, joined, mixed, dq, dk, dv, ab, drel):
    rows, width = me.shape[1] * me.shape[2], me.shape[3]
    ff = ua.shape[3]
    me2 = me.reshape(2, rows, width)
    ua2 = ua.reshape(2, rows, ff)
    flat = [v.reshape(rows, width) for v in (stream, joined, mixed, dq, dk, dv, ab)]
    piece = jax.ShapeDtypeStruct((RING, B_ROWS, COLS), BF16)
    out_spec = pl.BlockSpec((1, B_ROWS, COLS), lambda k: (k, 0, 0))
    squeezed = pl.Squeezed()
    left = pl.BlockSpec((rows, COLS), lambda k: (0, (k % 4) // 2))
    right = pl.BlockSpec((rows, COLS), lambda k: (0, k % 2))
    return pl.pallas_call(
        mixed_pieces_body,
        out_shape=(piece, piece),
        grid=(RING,),
        in_specs=[
            SMEM_SPEC,
            pl.BlockSpec((squeezed, rows, width), lambda k: (0, 0, 0)),
            pl.BlockSpec((squeezed, rows, COLS), lambda k: (0, 0, k)),
            pl.BlockSpec((squeezed, rows, width), lambda k: (1, 0, k // 2)),
            pl.BlockSpec((squeezed, rows, COLS), lambda k: (1, 0, k % 2)),
            left, left, left, right, right, right, right,
            pl.BlockSpec((2, REL_PIECE, width), lambda k: (0, k, 0)),
        ],
        out_specs=(out_spec, out_spec),
        compiler_params=pltpu.CompilerParams(vmem_limit_bytes=VMEM_LIMIT),
        cost_estimate=pl.CostEstimate(
            flops=4 * rows * B_ROWS * COLS * RING, bytes_accessed=16_000_000, transcendentals=0
        ),
        name="mixed_pieces",
    )(meta, me2, ua2, ua2, me2, *flat, drel)


def unpack_body(
    meta, place, own_a, own_b, other_a, other_b, *refs
):
    fi, fo, wq, wk, wv, wo, rel, low_f, high_f, sems = refs[-10:]
    low_core = meta[3] == 0
    low_at, high_at = place[0], place[1]

    def fill(low_a, low_b, high_a, high_b):
        for full, a, b in ((low_f, low_a, low_b), (high_f, high_a, high_b)):
            full[:HEAD_ROWS] = a[...].astype(F32)
            full[HEAD_ROWS : HEAD_ROWS + B_ROWS] = b[...].astype(F32)

    @pl.when(low_core)
    def _low():
        fill(own_a, own_b, other_a, other_b)

    @pl.when(~low_core)
    def _high():
        fill(other_a, other_b, own_a, own_b)

    ffn_rows = HEAD_ROWS + REST_ROWS
    block = pl.ds(ffn_rows, COLS)
    copies = [
        pltpu.make_async_copy(
            low_f.at[pl.ds(0, ffn_rows)],
            fi.at[0, :, pl.ds(pl.multiple_of(low_at * COLS, LANES), COLS)],
            sems.at[0],
        ),
        pltpu.make_async_copy(
            high_f.at[pl.ds(0, ffn_rows)],
            fo.at[
                0,
                pl.ds(pl.multiple_of((high_at // 2) * ffn_rows, LANES), ffn_rows),
                pl.ds(pl.multiple_of((high_at % 2) * COLS, LANES), COLS),
            ],
            sems.at[1],
        ),
        pltpu.make_async_copy(
            low_f.at[pl.ds(ffn_rows + COLS, REL_PIECE)],
            rel.at[pl.ds(pl.multiple_of(low_at * REL_PIECE, 16), REL_PIECE), pl.ds(0, COLS)],
            sems.at[2],
        ),
        pltpu.make_async_copy(
            high_f.at[pl.ds(ffn_rows + COLS, REL_PIECE)],
            rel.at[pl.ds(pl.multiple_of(high_at * REL_PIECE, 16), REL_PIECE), pl.ds(COLS, COLS)],
            sems.at[3],
        ),
    ]

    def block_copy(src, at, dst, sem):
        inside = at % 4
        return pltpu.make_async_copy(
            src.at[block],
            dst.at[
                0,
                pl.ds(pl.multiple_of((inside // 2) * COLS, LANES), COLS),
                pl.ds(pl.multiple_of((inside % 2) * COLS, LANES), COLS),
            ],
            sem,
        )

    for copy in copies:
        copy.start()
    for src, at, early, late, n in ((low_f, low_at, wq, wk, 4), (high_f, high_at, wv, wo, 5)):

        @pl.when(at < 4)
        def _early(src=src, at=at, early=early, n=n):
            copy = block_copy(src, at, early, sems.at[n])
            copy.start()
            copy.wait()

        @pl.when(at >= 4)
        def _late(src=src, at=at, late=late, n=n):
            copy = block_copy(src, at, late, sems.at[n])
            copy.start()
            copy.wait()

    for copy in copies:
        copy.wait()


def unpack(meta, place, own_a, own_b, other_a, other_b, outs, shapes):
    given = [] if outs is None else list(outs)
    return pl.pallas_call(
        unpack_body,
        out_shape=tuple(shapes),
        in_specs=[SMEM_SPEC, SMEM_SPEC] + [VMEM_SPEC] * 4 + [ANY_SPEC] * len(given),
        out_specs=tuple(ANY_SPEC for _ in shapes),
        input_output_aliases={6 + n: n for n in range(len(given))},
        scratch_shapes=[
            pltpu.VMEM((HEAD_ROWS + B_ROWS, COLS), F32),
            pltpu.VMEM((HEAD_ROWS + B_ROWS, COLS), F32),
            pltpu.SemaphoreType.DMA((6,)),
        ],
        compiler_params=pltpu.CompilerParams(vmem_limit_bytes=VMEM_LIMIT),
        cost_estimate=pl.CostEstimate(flops=0, bytes_accessed=6_000_000, transcendentals=0),
        name="unpack",
    )(meta, place, own_a, own_b, other_a, other_b, *given)


def finish_body(small, mask, pos, rel, bc, bp, bs, seg, n1g, n1s, fib, fob, n2g, n2s, mask_out, wrel):
    heads, dim = bc.shape[1], bc.shape[2]
    for head in range(heads):
        cols = slice(head * dim, (head + 1) * dim)
        bc[0, head : head + 1, :] = small[0:1, cols]
        bp[0, head : head + 1, :] = small[1:2, cols]
        bs[0, head : head + 1, :] = small[2:3, cols]
        seg[0, 0, head : head + 1, :] = small[3:4, cols]
        seg[0, 1, head : head + 1, :] = small[4:5, cols]
    n1g[...] = small[9:10, :]
    n1s[...] = small[10:11, :]
    fob[...] = small[11:12, :]
    n2g[...] = small[12:13, :]
    n2s[...] = small[13:14, :]
    width = small.shape[1]
    for step in range(4):
        fib[:, step * width : (step + 1) * width] = small[16 + step : 17 + step, :]
    mask_out[...] = mask[...]
    wrel[0] = dot_tn(pos[...], rel[...].astype(BF16))


def ring_tables(count):
    cycle = [(z, 0) for z in range(4)] + [(z, 1) for z in (3, 2, 1, 0)]
    place, steps = [], []
    for index in range(count):
        base, inside = index - index % GROUP, index % GROUP
        z, y, core = inside // 4, (inside // 2) % 2, inside % 2
        at = cycle.index((z, y))
        place.append(at)
        z2, y2 = cycle[(at + (1 if core == 0 else -1)) % RING]
        steps.append((index, base + (z2 * 2 + y2) * 2 + core))
    return np.array(place, np.int32), steps


def swapped(value, axis, bit):
    count = lax.axis_size(axis)
    return lax.ppermute(value, axis, [(index, index ^ bit) for index in range(count)])


def position_table(total_rows, width_model, mem_rows, seg_rows):
    row_ids = np.arange(total_rows, dtype=np.float32)
    distance = np.float32(mem_rows + seg_rows - 1) - row_ids
    power = np.arange(0, width_model, 2, dtype=np.float32) / np.float32(width_model)
    freqs = np.float32(1.0) / np.power(np.float32(10000.0), power)
    angles = distance[:, None] * freqs[None, :]
    return np.concatenate([np.sin(angles), np.cos(angles)], axis=1).astype(np.float32)


def shards(
    content_in, memory, mask_embed, doc_ids, orders, targets, slot_used,
    w_query, w_key, w_value, w_out, w_rel, bias_content, bias_position, bias_segment, seg_embed,
    norm1_gain, norm1_shift, ffn_in, ffn_in_bias, ffn_out, ffn_out_bias, norm2_gain, norm2_shift,
    content_cot, query_cot,
):
    slots, seg_rows, width = content_in.shape
    mem_rows = memory.shape[2]
    heads, dim = bias_content.shape[1:]
    ff = ffn_in.shape[2]
    key_rows, rows = mem_rows + seg_rows, 2 * seg_rows
    rel_rows = key_rows + seg_rows
    section = lax.axis_index("section")
    dp = lax.axis_index("dp")
    dp_count = lax.axis_size("dp")
    core = dp % 2
    pos_b = jnp.asarray(position_table(rel_rows, width, mem_rows, seg_rows)).astype(BF16)
    rel = jnp.dot(pos_b, w_rel[0], preferred_element_type=F32).astype(BF16)
    used = (slot_used > 0).astype(jnp.int32)
    meta = jnp.stack([section.astype(jnp.int32), used[0], used[1], core.astype(jnp.int32)])
    small = jnp.concatenate(
        [
            v.reshape(-1, width).astype(F32)
            for v in (
                bias_content, bias_position, bias_segment, seg_embed, norm1_gain, norm1_shift,
                ffn_out_bias, norm2_gain, norm2_shift, mask_embed, ffn_in_bias,
            )
        ]
        + [jnp.zeros((1, width), F32)],
        axis=0,
    )

    def shape(*dims, dtype=BF16):
        return jax.ShapeDtypeStruct(dims, dtype)

    vm, dma = pltpu.VMEM, pltpu.SemaphoreType.DMA
    kept = {name: shape(slots, rows, width) for name in ("joined", "stream", "qc", "qp", "qs", "k", "v", "mixed")}
    kept |= {
        "p": shape(slots, heads, rows, key_rows),
        "mid_in": shape(slots, rows, width, dtype=F32),
        "outer": shape(slots, rows, width, dtype=F32),
        "slope": shape(slots, rows, ff),
        "me": shape(2, slots, rows, width),
        "ua": shape(2, slots, rows, ff),
        "content_out": shape(1, slots, seg_rows, width),
        "query_out": shape(1, slots, seg_rows, width),
    }
    forward_scratch = {
        name: vm((rows, width), BF16)
        for name in ("joined", "stream", "qc", "qp", "qs", "k", "v", "mixed", "midb", "out")
    }
    forward_scratch |= {name: vm((width, width), BF16) for name in ("wk", "wq", "wv", "wo")}
    forward_scratch |= {
        "rel": vm((rel_rows, width), BF16),
        "fi": vm((width, ff), BF16),
        "fo": vm((ff, width), BF16),
        "p": vm((heads, rows, key_rows), BF16),
        "same": vm((seg_rows, seg_rows), F32),
        "bias": vm((2, seg_rows, seg_rows), F32),
        "mid_in": vm((rows, width), F32),
        "outer": vm((rows, width), F32),
        "act": vm((rows, ff), BF16),
        "slope": vm((rows, ff), BF16),
        "sem_in": dma((11,)),
        "sem_out": dma((20,)),
    }
    layer_flops = 9_000_000_000
    common = {
        "meta": (SMEM_SPEC, meta),
        "small": (VMEM_SPEC, small),
        "docs": (VMEM_SPEC, doc_ids),
    }
    sent = {}
    for call in range(4):
        layer, slot = call // 2, call % 2
        inputs = dict(common)
        inputs |= {
            "orders": (VMEM_SPEC, orders),
            "targets": (VMEM_SPEC, targets),
            "memory": (ANY_SPEC, memory),
            "rel": (ANY_SPEC, rel),
        }
        for name, value in (
            ("w_key", w_key), ("w_query", w_query), ("w_value", w_value), ("w_out", w_out),
            ("ffn_in", ffn_in), ("ffn_out", ffn_out),
        ):
            inputs[name] = (ANY_SPEC, value)
        if layer == 0:
            inputs["content_in"] = (ANY_SPEC, content_in)
        else:
            inputs["arrived"] = (ANY_SPEC, sent[slot])
        fresh = {"sent": shape(rows, width)} if layer == 0 else {}
        kept, new = call_kernel(
            forward_body, layer, slot, inputs, kept, fresh, forward_scratch,
            f"forward_{layer}_{slot}", layer_flops,
        )
        if layer == 0:
            sent[slot] = lax.ppermute(new["sent"], "section", [(0, 1)])

    tail_scratch = {
        "outer": vm((rows, width), F32),
        "mid_in": vm((rows, width), F32),
        "cot": vm((rows, width), BF16),
        "returned": vm((rows, width), BF16),
        "e": vm((rows, width), BF16),
        "ab": vm((rows, width), BF16),
        "a": vm((rows, width), F32),
        "acc": vm((rows, width), F32),
        "u": vm((rows, ff), BF16),
        "slope": vm((rows, ff), BF16),
        "fi": vm((width, ff), BF16),
        "fo": vm((ff, width), BF16),
        "sums": vm((16, width), F32),
        "sem_in": dma((8,)),
        "sem_out": dma((8,)),
    }
    head_scratch = {
        name: vm((rows, width), BF16)
        for name in ("ab", "x", "k", "v", "qc", "qp", "qs", "qpf", "dk", "dv", "dqb", "out")
    }
    head_scratch |= {name: vm((width, width), BF16) for name in ("wk", "wq", "wv", "wo")}
    head_scratch |= {
        "rel": vm((rel_rows, width), BF16),
        "p": vm((heads, rows, key_rows), BF16),
        "a": vm((rows, width), F32),
        "dq": vm((rows, width), F32),
        "dqp": vm((rows, width), F32),
        "drel": vm((rel_rows, width), F32),
        "sums": vm((8, width), F32),
        "sem_in": dma((13,)),
        "sem_out": dma((8,)),
    }
    tail_kept = {
        "me": kept["me"],
        "ua": kept["ua"],
        "ab": shape(slots, rows, width),
        "sums_tail": shape(slots, 16, width, dtype=F32),
    }
    head_kept = {name: shape(slots, rows, width) for name in ("dk", "dv", "dq")}
    head_kept |= {
        "drel": shape(slots, rel_rows, width, dtype=F32),
        "input_grad": shape(1, slots, seg_rows, width),
        "sums_head": shape(slots, 8, width, dtype=F32),
    }
    returned = {}
    for call in range(4):
        layer, slot = 1 - call // 2, 1 - call % 2
        inputs = dict(common)
        del inputs["docs"]
        for name in ("outer", "slope", "mid_in"):
            inputs[name] = (ANY_SPEC, kept[name])
        for name, value in (
            ("content_cot", content_cot), ("query_cot", query_cot), ("ffn_in", ffn_in), ("ffn_out", ffn_out),
        ):
            inputs[name] = (ANY_SPEC, value)
        if layer == 0:
            inputs["returned"] = (ANY_SPEC, returned[slot])
        tail_kept, new = call_kernel(
            tail_body, layer, slot, inputs, tail_kept, {"a": shape(rows, width, dtype=F32)}, tail_scratch,
            f"tail_{layer}_{slot}", layer_flops,
        )
        if call == 3:
            own_a, other_a = ffn_pieces(meta, tail_kept["me"], tail_kept["ua"])
            other_a = swapped(other_a, "dp", 1)
        inputs = dict(common)
        for name in ("p", "k", "v", "qc", "qp", "qs"):
            inputs[name] = (ANY_SPEC, kept[name])
        for name, value in (
            ("w_key", w_key), ("w_query", w_query), ("w_value", w_value), ("w_out", w_out), ("rel", rel),
            ("ab", tail_kept["ab"]), ("a", new["a"]),
        ):
            inputs[name] = (ANY_SPEC, value)
        fresh = {"sent": shape(rows, width)} if layer == 1 else {}
        head_kept, new = call_kernel(
            head_body, layer, slot, inputs, head_kept, fresh, head_scratch,
            f"head_{layer}_{slot}", layer_flops,
        )
        if layer == 1:
            returned[slot] = lax.ppermute(new["sent"], "section", [(1, 0)])

    sums = jnp.concatenate(
        [head_kept["sums_head"][0] + head_kept["sums_head"][1], tail_kept["sums_tail"][0] + tail_kept["sums_tail"][1]],
        axis=0,
    )
    mask_row = jnp.where(section == 0, sums[5:6, :], 0.0)
    sums = jnp.concatenate([sums[:5], mask_row, sums[6:]], axis=0)
    bit = 1
    while bit < dp_count:
        sums = sums + swapped(sums, "dp", bit)
        bit *= 2
    mask_total = sums[5:6, :]
    mask_total = mask_total + swapped(mask_total, "section", 1)

    own_b, other_b = mixed_pieces(
        meta, tail_kept["me"], tail_kept["ua"], kept["stream"], kept["joined"], kept["mixed"],
        head_kept["dq"], head_kept["dk"], head_kept["dv"], tail_kept["ab"], head_kept["drel"],
    )
    other_b = swapped(other_b, "dp", 1)

    table, steps = ring_tables(dp_count)
    at = jnp.asarray(table)[dp]
    me = jnp.where(core == 0, at, -at)

    def pick(own, other, step):
        index = jnp.mod(me - step, RING)
        return (
            lax.dynamic_index_in_dim(own, index, 0, keepdims=False).astype(F32)
            + lax.dynamic_index_in_dim(other, index, 0, keepdims=False).astype(F32)
        )

    acc_a = pick(own_a, other_a, 0).astype(BF16)
    acc_b = pick(own_b, other_b, 0).astype(BF16)
    for step in range(1, RING):
        acc_a = (lax.ppermute(acc_a, "dp", steps).astype(F32) + pick(own_a, other_a, step)).astype(BF16)
        acc_b = (lax.ppermute(acc_b, "dp", steps).astype(F32) + pick(own_b, other_b, step)).astype(BF16)
    bit = GROUP
    while bit < dp_count:
        acc_a = (acc_a.astype(F32) + swapped(acc_a, "dp", bit).astype(F32)).astype(BF16)
        acc_b = (acc_b.astype(F32) + swapped(acc_b, "dp", bit).astype(F32)).astype(BF16)
        bit *= 2
    shapes = [
        shape(1, width, ff, dtype=F32), shape(1, ff, width, dtype=F32),
        *[shape(1, width, width, dtype=F32) for _ in range(4)], shape(rel_rows, width, dtype=F32),
    ]
    outs = None
    for step in range(RING):
        if step:
            acc_a = lax.ppermute(acc_a, "dp", steps)
            acc_b = lax.ppermute(acc_b, "dp", steps)
        place = jnp.mod(jnp.stack([at, -at]) + 1 - step, RING).astype(jnp.int32)
        outs = unpack(
            meta, place, acc_a, acc_b, swapped(acc_a, "dp", 1), swapped(acc_b, "dp", 1), outs, shapes
        )
    grad_ffn_in, grad_ffn_out, grad_w_query, grad_w_key, grad_w_value, grad_w_out, grad_rel = outs
    head_shape = shape(1, heads, dim, dtype=F32)
    row_shape = shape(1, width, dtype=F32)
    (
        grad_bc, grad_bp, grad_bs, grad_seg, grad_n1g, grad_n1s, grad_fib, grad_fob, grad_n2g, grad_n2s,
        mask_grad, grad_w_rel,
    ) = pl.pallas_call(
        finish_body,
        out_shape=(
            head_shape, head_shape, head_shape, shape(1, 2, heads, dim, dtype=F32), row_shape, row_shape,
            shape(1, ff, dtype=F32), row_shape, row_shape, row_shape, row_shape,
            shape(1, width, width, dtype=F32),
        ),
        compiler_params=pltpu.CompilerParams(vmem_limit_bytes=VMEM_LIMIT),
        name="finish",
    )(sums, mask_total, pos_b, grad_rel)
    return (
        kept["content_out"], kept["query_out"], head_kept["input_grad"], mask_grad.reshape(width),
        grad_w_query, grad_w_key, grad_w_value, grad_w_out, grad_w_rel, grad_bc, grad_bp, grad_bs, grad_seg,
        grad_n1g, grad_n1s, grad_ffn_in, grad_fib, grad_ffn_out, grad_fob, grad_n2g, grad_n2s,
    )


def solution(mesh):
    placed = (
        P("dp", None, None),
        P("section", "dp", None, None),
        P(),
        P("dp", None),
        P("dp", None),
        P("dp", None),
        P("dp"),
        *[P("section", None, None)] * 8,
        P("section", None, None, None),
        P("section", None),
        P("section", None),
        P("section", None, None),
        P("section", None),
        P("section", None, None),
        P("section", None),
        P("section", None),
        P("section", None),
        P("section", "dp", None, None),
        P("section", "dp", None, None),
    )
    return jax.shard_map(
        shards,
        mesh=mesh,
        in_specs=placed,
        out_specs=(
            *[P("section", "dp", None, None)] * 3,
            P(),
            *[P("section", None, None)] * 8,
            P("section", None, None, None),
            P("section", None),
            P("section", None),
            P("section", None, None),
            P("section", None),
            P("section", None, None),
            P("section", None),
            P("section", None),
            P("section", None),
        ),
        check_vma=False,
    )
```

```python
import functools
import types

import jax
import jax.numpy as jnp
import numpy as np
from jax import lax
from jax.experimental import pallas as pl
from jax.experimental.pallas import tpu as pltpu
from jax.sharding import PartitionSpec as P

BF16 = jnp.bfloat16
F32 = jnp.float32
NEG_FILL = -1e30
NORM_EPS = 1e-05
GELU_A = 0.7978845608028654
GELU_B = 0.044715
VMEM_LIMIT = 60 * 1024 * 1024
LANES = 128
LAYER_FLOPS = 9_000_000_000
RING = 8
META_CORE, META_SECTION = 2 * RING, 2 * RING + 1

ROW_BC, ROW_BP, ROW_BS, ROW_SEG0, ROW_SEG1 = 0, 1, 2, 3, 4
ROW_N1G, ROW_N1S, ROW_FOB, ROW_N2G, ROW_N2S, ROW_MASK, ROW_FIB = 5, 6, 7, 8, 9, 10, 11
SMALL_ROWS = 16


def dot_nn(left, right):
    return jnp.dot(left, right, preferred_element_type=F32)


def dot_nt(left, right):
    return lax.dot_general(left, right, (((1,), (1,)), ((), ())), preferred_element_type=F32)


def dot_tn(left, right):
    return lax.dot_general(left, right, (((0,), (0,)), ((), ())), preferred_element_type=F32)


def col_sum(block):
    return jnp.sum(block, axis=0, keepdims=True)


def norm_parts(rows):
    center = jnp.mean(rows, axis=-1, keepdims=True)
    offset = rows - center
    spread = jnp.mean(offset * offset, axis=-1, keepdims=True)
    scale = lax.rsqrt(spread + NORM_EPS)
    return offset * scale, scale


def norm_back(grad, unit, scale, gain):
    inner = grad * gain
    mean_inner = jnp.mean(inner, axis=-1, keepdims=True)
    mean_cross = jnp.mean(inner * unit, axis=-1, keepdims=True)
    return (inner - mean_inner - unit * mean_cross) * scale


def half_masks():
    lane = lax.broadcasted_iota(jnp.int32, (1, LANES), 1)
    low = lane < LANES // 2
    return low, low.astype(F32).astype(BF16), (~low).astype(F32).astype(BF16)


def stack_heads(block, low_b, high_b):
    return jnp.concatenate([block * low_b, block * high_b], axis=0)


def copy_in(pairs, sems):
    copies = [
        pltpu.make_async_copy(src, dst, sems.at[n]) for n, (src, dst) in enumerate(pairs)
    ]
    for copy in copies:
        copy.start()
    return copies


def name_refs(names_in, names_out, names_scratch, refs):
    groups, start = [], 0
    for names in (names_in, names_out, names_scratch):
        groups.append(types.SimpleNamespace(**dict(zip(names, refs[start : start + len(names)]))))
        start += len(names)
    return groups


def forward_body(section, slot, names_in, names_out, names_scratch, *refs):
    r, o, s = name_refs(names_in, names_out, names_scratch, refs)
    meta = r.meta
    seg_rows, width = s.stream.shape[0] // 2, s.stream.shape[1]
    key_rows = s.joined.shape[0]
    pairs_count = width // LANES
    ff = s.act.shape[1]
    score_scale = 0.125

    @pl.when(meta[META_SECTION] == section)
    def _run():
        sem_in, sem_out = s.sem_in, s.sem_out
        mem_rows = key_rows - seg_rows
        x_src = r.content_in.at[slot] if section == 0 else r.arrived.at[pl.ds(0, seg_rows)]
        loads = [
            (r.memory.at[0, slot], s.joined.at[pl.ds(0, mem_rows)]),
            (x_src, s.joined.at[pl.ds(mem_rows, seg_rows)]),
            (x_src, s.stream.at[pl.ds(0, seg_rows)]),
            (r.w_key.at[0], s.wk),
            (r.w_query.at[0], s.wq),
            (r.rel, s.rel),
            (r.w_value.at[0], s.wv),
            (r.w_out.at[0], s.wo),
            (r.ffn_in.at[0], s.fi),
            (r.ffn_out.at[0], s.fo),
        ]
        if section == 1:
            loads.append(
                (r.arrived.at[pl.ds(seg_rows, seg_rows)], s.stream.at[pl.ds(seg_rows, seg_rows)])
            )
        moves = copy_in(loads, sem_in)
        stores = []

        def store(src, dst):
            copy = pltpu.make_async_copy(src, dst, sem_out.at[len(stores)])
            copy.start()
            stores.append(copy)

        small = r.small
        used = (r.slot_used[slot] > 0).astype(jnp.int32).astype(F32)
        if section == 0:
            s.stream[seg_rows:, :] = jnp.broadcast_to(
                small[ROW_MASK : ROW_MASK + 1, :], (seg_rows, width)
            ).astype(BF16)
        square = (seg_rows, seg_rows)
        doc = jnp.broadcast_to(r.docs[slot : slot + 1, :].astype(F32), square)
        order = jnp.broadcast_to(r.orders[slot : slot + 1, :].astype(F32), square)
        target = jnp.broadcast_to(r.targets[slot : slot + 1, :].astype(F32), square)
        same = doc == doc.T
        visible = same & ((target == 0.0) | (order <= order.T))
        row_id = lax.broadcasted_iota(jnp.int32, square, 0)
        col_id = lax.broadcasted_iota(jnp.int32, square, 1)
        s.same[...] = same.astype(F32)
        s.bias[0] = jnp.where(visible, 0.0, NEG_FILL)
        s.bias[1] = jnp.where(visible & (row_id != col_id), 0.0, NEG_FILL)

        for n in (0, 1, 3):
            moves[n].wait()
        s.k[...] = dot_nn(s.joined[...], s.wk[...]).astype(BF16)
        store(s.k, o.k.at[slot])
        store(s.joined, o.joined.at[slot])
        moves[2].wait()
        if section == 1:
            moves[10].wait()
        store(s.stream, o.stream.at[slot])
        moves[4].wait()
        queries = dot_nn(s.stream[...], s.wq[...])
        for block, kept, row in ((s.qc, o.qc, ROW_BC), (s.qp, o.qp, ROW_BP), (s.qs, o.qs, ROW_BS)):
            with_bias = (queries + small[row : row + 1, :]).astype(BF16)
            block[...] = (with_bias.astype(F32) * score_scale).astype(BF16)
            store(block, kept.at[slot])
        moves[6].wait()
        s.v[...] = dot_nn(s.joined[...], s.wv[...]).astype(BF16)
        store(s.v, o.v.at[slot])
        moves[5].wait()

        low, low_b, high_b = half_masks()
        same_f = s.same[...]
        bias_by_stream = [s.bias[0], s.bias[1]]
        for pair in range(pairs_count):
            sl = slice(pair * LANES, (pair + 1) * LANES)
            content = dot_nt(stack_heads(s.qc[:, sl], low_b, high_b), s.k[:, sl])
            position = dot_nt(stack_heads(s.qp[:, sl], low_b, high_b), s.rel[:, sl])
            seg = small[ROW_SEG0 : ROW_SEG1 + 1, sl]
            lane8 = lax.broadcasted_iota(jnp.int32, (8, LANES), 1)
            row8 = lax.broadcasted_iota(jnp.int32, (8, LANES), 0)
            seg8 = jnp.where(row8 % 2 == 0, seg[0:1, :], seg[1:2, :])
            seg8 = jnp.where((row8 < 4) & ((row8 < 2) == (lane8 < LANES // 2)), seg8, 0.0)
            pieces = dot_nt(s.qs[:, sl], seg8.astype(BF16))
            probs_pair = []
            for head in range(2):
                probs_streams = []
                for stream in range(2):
                    base = (2 * head + stream) * seg_rows
                    rolled = pltpu.roll(
                        position[base : base + seg_rows, :], key_rows + 1, axis=1, stride=1, stride_axis=0
                    )
                    rows = slice(stream * seg_rows, (stream + 1) * seg_rows)
                    same_part = pieces[rows, 2 * head : 2 * head + 1]
                    other_part = pieces[rows, 2 * head + 1 : 2 * head + 2]
                    body = content[base : base + seg_rows, :] + rolled[:, :key_rows] + other_part
                    left = body[:, :mem_rows]
                    right = (
                        body[:, mem_rows:] + (same_part - other_part) * same_f + bias_by_stream[stream]
                    )
                    peak = jnp.maximum(
                        jnp.max(left, axis=-1, keepdims=True), jnp.max(right, axis=-1, keepdims=True)
                    )
                    left = jnp.exp(left - peak)
                    right = jnp.exp(right - peak)
                    total = jnp.sum(left + right, axis=-1, keepdims=True)
                    inverse = 1.0 / total
                    probs_streams.append(
                        jnp.concatenate([left * inverse, right * inverse], axis=1).astype(BF16)
                    )
                probs = jnp.concatenate(probs_streams, axis=0)
                s.p[2 * pair + head] = probs
                probs_pair.append(probs)
            mixed = dot_nn(
                jnp.concatenate(probs_pair, axis=1), stack_heads(s.v[:, sl], low_b, high_b)
            )
            s.mixed[:, sl] = mixed.astype(BF16)
        store(s.p, o.p.at[slot])
        store(s.mixed, o.mixed.at[slot])

        moves[7].wait()
        middle_in = dot_nn(s.mixed[...], s.wo[...]) + s.stream[...].astype(F32)
        s.mid_in[...] = middle_in
        store(s.mid_in, o.mid_in.at[slot])
        unit, _ = norm_parts(middle_in)
        middle = unit * small[ROW_N1G : ROW_N1G + 1, :] + small[ROW_N1S : ROW_N1S + 1, :]
        s.midb[...] = middle.astype(BF16)
        store(s.midb, o.me.at[0, slot])
        s.outer[...] = middle + small[ROW_FOB : ROW_FOB + 1, :]
        moves[8].wait()
        moves[9].wait()
        for step in range(ff // width):
            cols = slice(step * width, (step + 1) * width)
            inner = (
                dot_nn(s.midb[...], s.fi[:, cols])
                + small[ROW_FIB + step : ROW_FIB + step + 1, :]
            )
            square_in = inner * inner
            wave = jnp.tanh(GELU_A * inner * (1.0 + GELU_B * square_in))
            half = 0.5 * (1.0 + wave)
            active = (inner * half).astype(BF16)
            slope = half + (0.5 * GELU_A) * inner * (1.0 - wave * wave) * (1.0 + 3.0 * GELU_B * square_in)
            s.act[:, cols] = active
            s.slope[:, cols] = slope.astype(BF16)
            s.outer[...] += dot_nn(active, s.fo[cols, :])
        store(s.act, o.ua.at[1, slot])
        store(s.slope, o.slope.at[slot])
        store(s.outer, o.outer.at[slot])
        unit, _ = norm_parts(s.outer[...])
        result = unit * small[ROW_N2G : ROW_N2G + 1, :] + small[ROW_N2S : ROW_N2S + 1, :]
        s.out[...] = (result * used).astype(BF16)
        store(s.out.at[pl.ds(0, seg_rows)], o.content_out.at[0, slot])
        store(s.out.at[pl.ds(seg_rows, seg_rows)], o.query_out.at[0, slot])
        if section == 0:
            store(s.out, o.sent)
        for copy in stores:
            copy.wait()


def tail_body(section, slot, names_in, names_out, names_scratch, *refs):
    r, o, s = name_refs(names_in, names_out, names_scratch, refs)
    meta = r.meta
    rows, width = s.outer.shape
    seg_rows = rows // 2
    ff = s.slope.shape[1]

    @pl.when(meta[META_SECTION] == section)
    def _run():
        sem_in, sem_out = s.sem_in, s.sem_out
        loads = [
            (r.outer.at[slot], s.outer),
            (r.content_cot.at[0, slot], s.cot.at[pl.ds(0, seg_rows)]),
            (r.query_cot.at[0, slot], s.cot.at[pl.ds(seg_rows, seg_rows)]),
            (r.ffn_out.at[0], s.fo),
            (r.slope.at[slot], s.slope),
            (r.ffn_in.at[0], s.fi),
            (r.mid_in.at[slot], s.mid_in),
        ]
        if section == 0:
            loads.append((r.returned, s.returned))
        moves = copy_in(loads, sem_in)
        stores = []

        def store(src, dst):
            copy = pltpu.make_async_copy(src, dst, sem_out.at[len(stores)])
            copy.start()
            stores.append(copy)

        small = r.small
        used = (r.slot_used[slot] > 0).astype(jnp.int32).astype(F32)
        for n in (0, 1, 2):
            moves[n].wait()
        grad = s.cot[...].astype(F32) * used
        if section == 0:
            moves[7].wait()
            grad = grad + s.returned[...].astype(F32)
        unit, scale = norm_parts(s.outer[...])
        out = s.sums
        out[...] = jnp.zeros_like(out)
        out[4:5, :] = col_sum(grad * unit)
        out[5:6, :] = col_sum(grad)
        grad_outer = norm_back(grad, unit, scale, small[ROW_N2G : ROW_N2G + 1, :])
        s.e[...] = grad_outer.astype(BF16)
        store(s.e, o.me.at[1, slot])
        out[3:4, :] = col_sum(s.e[...].astype(F32))
        s.acc[...] = grad_outer
        moves[3].wait()
        moves[4].wait()
        moves[5].wait()
        for step in range(ff // width):
            cols = slice(step * width, (step + 1) * width)
            grad_active = dot_nt(s.e[...], s.fo[cols, :])
            inner_b = (s.slope[:, cols].astype(F32) * grad_active).astype(BF16)
            s.u[:, cols] = inner_b
            out[8 + step : 9 + step, :] = col_sum(inner_b.astype(F32))
            s.acc[...] += dot_nt(inner_b, s.fi[:, cols])
        store(s.u, o.ua.at[0, slot])
        moves[6].wait()
        unit, scale = norm_parts(s.mid_in[...])
        grad = s.acc[...]
        out[1:2, :] = col_sum(grad * unit)
        out[2:3, :] = col_sum(grad)
        s.a[...] = norm_back(grad, unit, scale, small[ROW_N1G : ROW_N1G + 1, :])
        s.ab[...] = s.a[...].astype(BF16)
        store(s.a, o.a)
        store(s.ab, o.ab.at[slot])
        store(s.sums, o.sums_tail.at[slot])
        for copy in stores:
            copy.wait()


def head_body(section, slot, names_in, names_out, names_scratch, *refs):
    r, o, s = name_refs(names_in, names_out, names_scratch, refs)
    meta = r.meta
    rows, width = s.a.shape
    seg_rows = rows // 2
    key_rows = s.k.shape[0]
    rel_rows = s.rel.shape[0]
    mem_rows = key_rows - seg_rows
    pairs_count = width // LANES
    score_scale = 0.125

    @pl.when(meta[META_SECTION] == section)
    def _run():
        sem_in, sem_out = s.sem_in, s.sem_out
        loads = [
            (r.ab.at[slot], s.ab),
            (r.w_out.at[0], s.wo),
            (r.v.at[slot], s.v),
            (r.p.at[slot], s.p),
            (r.k.at[slot], s.k),
            (r.qc.at[slot], s.qc),
            (r.qp.at[slot], s.qp),
            (r.qs.at[slot], s.qs),
            (r.rel, s.rel),
            (r.w_query.at[0], s.wq),
            (r.w_key.at[0], s.wk),
            (r.w_value.at[0], s.wv),
            (r.a, s.a),
        ]
        moves = copy_in(loads, sem_in)
        stores = []

        def store(src, dst):
            copy = pltpu.make_async_copy(src, dst, sem_out.at[len(stores)])
            copy.start()
            stores.append(copy)

        small = r.small
        square = (seg_rows, seg_rows)
        doc = jnp.broadcast_to(r.docs[slot : slot + 1, :].astype(F32), square)
        same_one = (doc == doc.T).astype(F32)
        same = jnp.concatenate([same_one, same_one], axis=0)
        flip_rows = lax.broadcasted_iota(jnp.int32, (rows, rows), 0)
        flip_cols = lax.broadcasted_iota(jnp.int32, (rows, rows), 1)
        flipped_to = jnp.where(flip_rows < seg_rows, seg_rows - 1, rows + seg_rows - 1) - flip_rows
        flip = (flip_cols == flipped_to).astype(F32).astype(BF16)
        out = s.sums
        out[...] = jnp.zeros_like(out)
        moves[0].wait()
        moves[1].wait()
        s.x[...] = dot_nt(s.ab[...], s.wo[...]).astype(BF16)
        for n in (2, 3, 4, 5, 6, 7, 8):
            moves[n].wait()
        s.qpf[...] = dot_nn(flip, s.qp[...]).astype(BF16)

        low, low_b, high_b = half_masks()
        blank = jnp.zeros((seg_rows, rel_rows - key_rows), F32)
        for pair in range(pairs_count):
            sl = slice(pair * LANES, (pair + 1) * LANES)
            grads_mixed = stack_heads(s.x[:, sl], low_b, high_b)
            grad_probs = dot_nt(grads_mixed, s.v[:, sl])
            scores_b = []
            same_sums, other_sums = [], []
            for head in range(2):
                probs = s.p[2 * pair + head].astype(F32)
                product = probs * grad_probs[head * rows : (head + 1) * rows, :]
                delta = jnp.sum(product, axis=-1, keepdims=True)
                rounded = (product - probs * delta).astype(BF16)
                scores_b.append(rounded)
                wide = rounded.astype(F32)
                right = wide[:, mem_rows:] * same
                same_sum = jnp.sum(right, axis=-1, keepdims=True)
                same_sums.append(same_sum)
                other_sums.append(
                    jnp.sum(wide[:, :mem_rows] + (wide[:, mem_rows:] - right), axis=-1, keepdims=True)
                )
            stacked = jnp.concatenate(scores_b, axis=0)
            beside = jnp.concatenate(scores_b, axis=1)
            probs_stacked = jnp.concatenate([s.p[2 * pair], s.p[2 * pair + 1]], axis=0)
            s.dv[:, sl] = dot_tn(probs_stacked, grads_mixed).astype(BF16)
            s.dk[:, sl] = dot_tn(stacked, stack_heads(s.qc[:, sl], low_b, high_b)).astype(BF16)
            grad_content = dot_nn(beside, stack_heads(s.k[:, sl], low_b, high_b)) * score_scale
            same_sel = jnp.where(low, same_sums[0], same_sums[1])
            other_sel = jnp.where(low, other_sums[0], other_sums[1])
            seg0 = small[ROW_SEG0 : ROW_SEG0 + 1, sl]
            seg1 = small[ROW_SEG1 : ROW_SEG1 + 1, sl]
            grad_segment = (same_sel * seg0 + other_sel * seg1) * score_scale
            qs = s.qs[:, sl].astype(F32)
            out[0:1, sl] = col_sum(grad_content)
            out[2:3, sl] = col_sum(grad_segment)
            out[3:4, sl] = col_sum(same_sel * qs)
            out[4:5, sl] = col_sum(other_sel * qs)
            s.dq[:, sl] = grad_content + grad_segment
            turned = dot_nn(flip, beside)
            shifted_heads = []
            for head in range(2):
                parts = []
                for stream in range(2):
                    block = turned[
                        stream * seg_rows : (stream + 1) * seg_rows,
                        head * key_rows : (head + 1) * key_rows,
                    ]
                    block = jnp.concatenate([block, blank], axis=1)
                    parts.append(pltpu.roll(block, 0, axis=1, stride=1, stride_axis=0).astype(BF16))
                shifted_heads.append(jnp.concatenate(parts, axis=0))
            grad_position = (
                dot_nn(
                    jnp.concatenate(shifted_heads, axis=1),
                    stack_heads(s.rel[:, sl], low_b, high_b),
                )
                * score_scale
            )
            out[1:2, sl] = col_sum(grad_position)
            s.dqp[:, sl] = grad_position
            s.drel[:, sl] = dot_tn(
                jnp.concatenate(shifted_heads, axis=0),
                stack_heads(s.qpf[:, sl], low_b, high_b),
            )
        store(s.dk, o.dk.at[slot])
        store(s.dv, o.dv.at[slot])
        store(s.drel, o.drel.at[slot])
        grad_position = s.dqp[...]
        position_high = grad_position.astype(BF16)
        position_low = (grad_position - position_high.astype(F32)).astype(BF16)
        grad_queries = s.dq[...] + dot_nn(flip, position_high) + dot_nn(flip, position_low)
        s.dqb[...] = grad_queries.astype(BF16)
        store(s.dqb, o.dq.at[slot])
        for n in (9, 10, 11, 12):
            moves[n].wait()
        grad_rows = s.a[...] + dot_nt(s.dqb[...], s.wq[...])
        grad_content = (
            grad_rows[:seg_rows, :]
            + dot_nt(s.dk[mem_rows:, :], s.wk[...])
            + dot_nt(s.dv[mem_rows:, :], s.wv[...])
        )
        grad_query = grad_rows[seg_rows:, :]
        s.out[:seg_rows, :] = grad_content.astype(BF16)
        s.out[seg_rows:, :] = grad_query.astype(BF16)
        store(s.out.at[pl.ds(0, seg_rows)], o.input_grad.at[0, slot])
        if section == 1:
            store(s.out, o.sent)
        if section == 0:
            out[5:6, :] = col_sum(grad_query)
        store(s.sums, o.sums_head.at[slot])
        for copy in stores:
            copy.wait()


ANY_SPEC = pl.BlockSpec(memory_space=pl.ANY)
SMEM_SPEC = pl.BlockSpec(memory_space=pltpu.SMEM)
VMEM_SPEC = pl.BlockSpec(memory_space=pltpu.VMEM)


def call_kernel(body, section, slot, inputs, carried, fresh, scratch):
    names_in = list(inputs)
    arrays = [inputs[n][1] for n in names_in]
    specs = [inputs[n][0] for n in names_in]
    aliases = {}
    names_out = list(carried) + list(fresh)
    out_shapes = []
    for position, key in enumerate(carried):
        value = carried[key]
        out_shapes.append(jax.ShapeDtypeStruct(value.shape, value.dtype))
        if not isinstance(value, jax.ShapeDtypeStruct):
            aliases[len(arrays)] = position
            arrays.append(value)
            specs.append(ANY_SPEC)
            names_in.append(key + "_")
    out_shapes += [fresh[key] for key in fresh]
    results = pl.pallas_call(
        functools.partial(body, section, slot, names_in, names_out, list(scratch)),
        out_shape=tuple(out_shapes),
        in_specs=specs,
        out_specs=tuple(ANY_SPEC for _ in out_shapes),
        scratch_shapes=list(scratch.values()),
        input_output_aliases=aliases,
        compiler_params=pltpu.CompilerParams(vmem_limit_bytes=VMEM_LIMIT),
        cost_estimate=pl.CostEstimate(flops=LAYER_FLOPS, bytes_accessed=20_000_000, transcendentals=0),
    )(*arrays)
    named = dict(zip(names_out, results))
    return {k: named[k] for k in carried}, {k: named[k] for k in fresh}


def in_hbm(**arrays):
    return {key: (ANY_SPEC, value) for key, value in arrays.items()}


def in_vmem(**arrays):
    return {key: (VMEM_SPEC, value) for key, value in arrays.items()}


def params():
    return pltpu.CompilerParams(vmem_limit_bytes=VMEM_LIMIT)


def cost(flops, moved):
    return pl.CostEstimate(flops=flops, bytes_accessed=moved, transcendentals=0)


def shape(*dims, dtype=BF16):
    return jax.ShapeDtypeStruct(dims, dtype)


def prepare_body(bc, bp, bs, seg, n1g, n1s, fob, n2g, n2s, mask, fib, pos, w_rel, small, rel):
    heads, dim = bc.shape[1:]
    width = heads * dim
    wide = [(row, value[0].astype(F32)) for row, value in ((ROW_BC, bc), (ROW_BP, bp), (ROW_BS, bs))]
    for head in range(heads):
        cols = slice(head * dim, (head + 1) * dim)
        for row, value in wide:
            small[row : row + 1, cols] = value[head : head + 1, :]
        small[ROW_SEG0 : ROW_SEG1 + 1, cols] = seg[head].astype(F32)
    for row, value in (
        (ROW_N1G, n1g), (ROW_N1S, n1s), (ROW_FOB, fob), (ROW_N2G, n2g), (ROW_N2S, n2s), (ROW_MASK, mask),
    ):
        small[row : row + 1, :] = value[...].astype(F32)
    for step in range(4):
        small[ROW_FIB + step : ROW_FIB + step + 1, :] = fib[:, step * width : (step + 1) * width].astype(F32)
    small[SMALL_ROWS - 1 : SMALL_ROWS, :] = jnp.zeros((1, width), F32)
    rel[...] = dot_nn(pos[...], w_rel[0]).astype(BF16)


GROUP = 16
HALF = 384
HEAD_ROWS = 320
REST_ROWS = HALF - HEAD_ROWS
REL_PIECE = 24
BLOCK = slice(REST_ROWS, REST_ROWS + HALF // 2)
REL = slice(BLOCK.stop, BLOCK.stop + REL_PIECE)
B_ROWS = BLOCK.stop + 32


def lane_slice(start, size):
    return pl.ds(pl.multiple_of(start, LANES), size)


def block_rows(index, size):
    return pl.ds(pl.multiple_of(index * size, size), size)


def put_piece(meta, step, place, outs, low, high, low_rest, high_rest):
    own_a, other_a, own_b, other_b = outs

    def write(low_a, low_b, high_a, high_b):
        for whole, rest, a, b in ((low, low_rest, low_a, low_b), (high, high_rest, high_a, high_b)):
            block, rel = rest
            a[place] = whole[:HEAD_ROWS]
            b[place, :REST_ROWS] = whole[HEAD_ROWS:]
            b[place, BLOCK] = jnp.concatenate([block[: HALF // 2], block[HALF // 2 :]], axis=1)
            b[place, BLOCK.stop :] = jnp.concatenate(
                [rel, jnp.zeros((B_ROWS - REL.stop, rel.shape[1]), F32)], axis=0
            ).astype(BF16)

    core0 = meta[META_CORE] == 0

    @pl.when(core0)
    def _low():
        write(own_a, own_b, other_a, other_b)

    @pl.when(~core0)
    def _high():
        write(other_a, other_b, own_a, own_b)


def first_pieces_body(meta, me, ua, stream, joined, mixed, dq, dk, dv, ab, drel, *refs):
    own_a, other_a, own_b, other_b = refs[:4]
    low_l, low_r, high_l, high_r, left, right, left2, right2, rel, sems = refs[4:]
    low_at, high_at = meta[0], meta[RING]
    width = low_r.shape[1]

    def start(src, dst, n):
        copy = pltpu.make_async_copy(src, dst, sems.at[n])
        copy.start()
        return copy

    moves = [
        start(me.at[0, :, block_rows(low_at % 2, HALF)], low_l, 0),
        start(ua.at[0, :, block_rows(low_at // 2, width)], low_r, 1),
        start(ua.at[1, :, block_rows(high_at, HALF)], high_l, 2),
        start(me.at[1], high_r, 3),
        start(drel.at[:, pl.ds(pl.multiple_of(low_at * REL_PIECE, 8), REL_PIECE), :], rel.at[0], 4),
        start(drel.at[:, pl.ds(pl.multiple_of((RING + high_at) * REL_PIECE, 8), REL_PIECE), :], rel.at[1], 5),
    ]

    def fetch(at, early, late, to_left, to_right, n):
        inside = at % 4
        rows_at, cols_at = block_rows(inside // 2, HALF), block_rows(inside % 2, HALF)

        @pl.when(at < RING // 2)
        def _early():
            start(early[0].at[:, rows_at], to_left, n)
            start(early[1].at[:, cols_at], to_right, n + 1)

        @pl.when(at >= RING // 2)
        def _late():
            start(late[0].at[:, rows_at], to_left, n)
            start(late[1].at[:, cols_at], to_right, n + 1)

        for dst, sem in ((to_left, n), (to_right, n + 1)):
            moves.append(pltpu.make_async_copy(early[0].at[:, rows_at], dst, sems.at[sem]))

    fetch(low_at, (stream, dq), (joined, dk), left, right, 6)
    fetch(high_at, (joined, dv), (mixed, ab), left2, right2, 8)
    for copy in moves:
        copy.wait()
    put_piece(
        meta, 0, 0, (own_a, other_a, own_b, other_b),
        dot_tn(low_l[...], low_r[...]).astype(BF16),
        dot_tn(high_l[...], high_r[...]).astype(BF16),
        (dot_tn(left[...], right[...]).astype(BF16), rel[0, 0] + rel[0, 1]),
        (dot_tn(left2[...], right2[...]).astype(BF16), rel[1, 0] + rel[1, 1]),
    )


def later_pieces_body(first, last, meta, me, ua, stream, joined, mixed, dq, dk, dv, ab, drel, *refs):
    outs_hbm = refs[:4]
    vme, vua, vs, vj, vm_, vdq, vdk, vdv, vab, vrel, *outs, sems, out_sems = refs[4:]
    loads = (
        (me.at[0], vme.at[0]), (ua.at[0], vua.at[0]), (me.at[1], vme.at[1]), (ua.at[1], vua.at[1]),
        (stream, vs), (dq, vdq), (joined, vj), (dk, vdk), (dv, vdv), (mixed, vm_), (ab, vab), (drel, vrel),
    )
    moves = copy_in(loads, sems)
    width = stream.shape[1]
    writes = []
    for step in range(first, last):
        place = step - first
        low_at, high_at = meta[step], meta[RING + step]
        if place == 0:
            moves[0].wait()
            moves[1].wait()
        low = dot_tn(vme[0, :, block_rows(low_at % 2, HALF)], vua[0, :, block_rows(low_at // 2, width)])
        if place == 0:
            moves[2].wait()
            moves[3].wait()
        high = dot_tn(vua[1, :, block_rows(high_at, HALF)], vme[1])
        if place == 0:
            for move in moves[4:]:
                move.wait()
        own_a, other_a, own_b, other_b = outs

        def write(low_a, low_b, high_a, high_b, place=place, low=low, high=high, low_at=low_at, high_at=high_at):
            for whole, a, b, at, early, late, base in (
                (low, low_a, low_b, low_at, (vs, vdq), (vj, vdk), 0),
                (high, high_a, high_b, high_at, (vj, vdv), (vm_, vab), RING),
            ):
                whole = whole.astype(BF16)
                a[place] = whole[:HEAD_ROWS]
                b[place, :REST_ROWS] = whole[HEAD_ROWS:]
                inside = at % 4
                rows_at, cols_at = block_rows(inside // 2, HALF), block_rows(inside % 2, HALF)

                def block(pair, b=b, place=place, rows_at=rows_at, cols_at=cols_at):
                    value = dot_tn(pair[0][:, rows_at], pair[1][:, cols_at]).astype(BF16)
                    b[place, BLOCK] = jnp.concatenate([value[: HALF // 2], value[HALF // 2 :]], axis=1)

                pl.when(at < RING // 2)(functools.partial(block, early))
                pl.when(at >= RING // 2)(functools.partial(block, late))
                rel_rows = pl.ds(pl.multiple_of((base + at) * REL_PIECE, 8), REL_PIECE)
                rel = vrel[0, rel_rows, :] + vrel[1, rel_rows, :]
                b[place, BLOCK.stop :] = jnp.concatenate(
                    [rel, jnp.zeros((B_ROWS - REL.stop, width), F32)], axis=0
                ).astype(BF16)

        core0 = meta[META_CORE] == 0
        pl.when(core0)(functools.partial(write, own_a, own_b, other_a, other_b))
        pl.when(~core0)(functools.partial(write, other_a, other_b, own_a, own_b))
        for n, (src, dst) in enumerate(zip(outs, outs_hbm)):
            copy = pltpu.make_async_copy(src.at[place], dst.at[place], out_sems.at[4 * place + n])
            copy.start()
            writes.append(copy)
    for copy in writes:
        copy.wait()


def pieces(first, last, meta, me, ua, operands):
    rows, width = operands[0].shape
    ff, rel_rows = ua.shape[2], operands[-1].shape[1]
    count = last - first
    outs = [shape(count, size, width) for size in (HEAD_ROWS, HEAD_ROWS, B_ROWS, B_ROWS)]
    vm = pltpu.VMEM
    if count == 1:
        narrow, full = vm((rows, HALF), BF16), vm((rows, width), BF16)
        body, out_spec = first_pieces_body, VMEM_SPEC
        scratch = [narrow, full, narrow, full, *[narrow] * 4, vm((2, 2, REL_PIECE, width), F32)]
        sems = [pltpu.SemaphoreType.DMA((10,))]
    else:
        body, out_spec = functools.partial(later_pieces_body, first, last), ANY_SPEC
        scratch = [
            vm((2, rows, width), BF16), vm((2, rows, ff), BF16), *[vm((rows, width), BF16)] * 7,
            vm((2, rel_rows, width), F32), *[vm(v.shape, BF16) for v in outs],
        ]
        sems = [pltpu.SemaphoreType.DMA((12,)), pltpu.SemaphoreType.DMA((4 * count,))]
    return pl.pallas_call(
        body,
        out_shape=outs,
        in_specs=[SMEM_SPEC] + [ANY_SPEC] * (2 + len(operands)),
        out_specs=[out_spec] * 4,
        scratch_shapes=scratch + sems,
        compiler_params=params(),
        cost_estimate=cost(6 * rows * HALF * width * count, 4_000_000 * count),
    )(meta, me, ua, *operands)


def by_core(meta, own, other, low_f, high_f):
    low = meta[META_CORE] == 0

    @pl.when(low)
    def _low():
        low_f[...] = own[...].astype(F32)
        high_f[...] = other[...].astype(F32)

    @pl.when(~low)
    def _high():
        low_f[...] = other[...].astype(F32)
        high_f[...] = own[...].astype(F32)


def ffn_places(fi, fo, low_at, high_at, first, count):
    width = fo.shape[2]
    return (
        fi.at[0, pl.ds(pl.multiple_of((low_at % 2) * HALF + first, 8), count), lane_slice((low_at // 2) * width, width)],
        fo.at[0, pl.ds(pl.multiple_of(high_at * HALF + first, 8), count), :],
    )


def unpack_a_body(step, meta, own, other, *refs):
    fi, fo, token, low_f, high_f, sems = refs[-6:]
    token[...] = jnp.zeros_like(token)
    by_core(meta, own, other, low_f, high_f)
    low_to, high_to = ffn_places(fi, fo, meta[step], meta[RING + step], 0, HEAD_ROWS)
    copies = [
        pltpu.make_async_copy(low_f, low_to, sems.at[0]),
        pltpu.make_async_copy(high_f, high_to, sems.at[1]),
    ]
    for copy in copies:
        copy.start()
    for copy in copies:
        copy.wait()


def unpack_b_body(step, meta, own, other, *refs):
    fi, fo, wq, wk, wv, wo, rel, token, low_f, high_f, sems = refs[-11:]
    token[...] = jnp.zeros_like(token)
    low_at, high_at = meta[step], meta[RING + step]
    by_core(meta, own, other, low_f, high_f)
    low_to, high_to = ffn_places(fi, fo, low_at, high_at, HEAD_ROWS, REST_ROWS)
    rest = pl.ds(0, REST_ROWS)
    rel_part = pl.ds(REL.start, REL_PIECE)

    def rel_to(at):
        return rel.at[pl.ds(pl.multiple_of(at * REL_PIECE, 8), REL_PIECE), :]

    copies = [
        pltpu.make_async_copy(low_f.at[rest], low_to, sems.at[0]),
        pltpu.make_async_copy(high_f.at[rest], high_to, sems.at[1]),
        pltpu.make_async_copy(low_f.at[rel_part], rel_to(low_at), sems.at[2]),
        pltpu.make_async_copy(high_f.at[rel_part], rel_to(RING + high_at), sems.at[3]),
    ]
    for copy in copies:
        copy.start()

    def block_copies(src, at, dst, sem):
        inside = at % 4
        for part in range(2):
            copy = pltpu.make_async_copy(
                src.at[pl.ds(BLOCK.start, HALF // 2), pl.ds(part * HALF, HALF)],
                dst.at[
                    0,
                    pl.ds(pl.multiple_of((inside // 2) * HALF + part * (HALF // 2), 8), HALF // 2),
                    lane_slice((inside % 2) * HALF, HALF),
                ],
                sems.at[sem + part],
            )
            copy.start()
            yield copy

    for src, at, early, late, n in ((low_f, low_at, wq, wk, 4), (high_f, high_at, wv, wo, 6)):

        @pl.when(at < RING // 2)
        def _early(src=src, at=at, early=early, n=n):
            for copy in list(block_copies(src, at, early, n)):
                copy.wait()

        @pl.when(at >= RING // 2)
        def _late(src=src, at=at, late=late, n=n):
            for copy in list(block_copies(src, at, late, n)):
                copy.wait()

    for copy in copies:
        copy.wait()


def unpack(body, step, rows, meta, own, other, outs, earlier):
    given = [v for v in outs if not isinstance(v, jax.ShapeDtypeStruct)]
    assert len(given) in (0, 2, len(outs))
    *results, token = pl.pallas_call(
        functools.partial(body, (step + RING - 1) % RING),
        out_shape=tuple(shape(*v.shape, dtype=v.dtype) for v in outs) + (shape(8, LANES, dtype=F32),),
        in_specs=[SMEM_SPEC] + [VMEM_SPEC] * 2 + [ANY_SPEC] * (len(given) + len(earlier)),
        out_specs=tuple(ANY_SPEC for _ in outs) + (VMEM_SPEC,),
        input_output_aliases={3 + n: n for n in range(len(given))},
        scratch_shapes=[
            pltpu.VMEM((rows, own.shape[-1]), F32),
            pltpu.VMEM((rows, own.shape[-1]), F32),
            pltpu.SemaphoreType.DMA((8,)),
        ],
        compiler_params=params(),
        cost_estimate=cost(0, 4_000_000),
    )(meta, own, other, *given, *earlier)
    return results, token


def finish_small_body(small, mask, bc, bp, bs, seg, n1g, n1s, fib, fob, n2g, n2s, mask_out):
    heads, dim = bc.shape[0], bc.shape[2]
    width = heads * dim
    for head in range(heads):
        cols = slice(head * dim, (head + 1) * dim)
        bc[head] = small[0:1, cols]
        bp[head] = small[1:2, cols]
        bs[head] = small[2:3, cols]
        seg[head] = small[3:5, cols]
    n1g[...] = small[9:10, :]
    n1s[...] = small[10:11, :]
    fob[...] = small[11:12, :]
    n2g[...] = small[12:13, :]
    n2s[...] = small[13:14, :]
    for step in range(4):
        fib[:, step * width : (step + 1) * width] = small[16 + step : 17 + step, :]
    mask_out[...] = mask[...]


def finish_rel_body(pos, rel, out):
    out[0] = dot_tn(pos[...], rel[...].astype(BF16))


def ring_steps(count):
    cycle = [(z, 0) for z in range(4)] + [(z, 1) for z in (3, 2, 1, 0)]
    steps = []
    for index in range(count):
        base, inside = index - index % GROUP, index % GROUP
        at = cycle.index((inside // 4, (inside // 2) % 2))
        z, y = cycle[(at + (1 if inside % 2 == 0 else -1)) % RING]
        steps.append((index, base + (z * 2 + y) * 2 + inside % 2))
    return steps


SECTION, DP = "section", "dp"


def swapped(value, axis, bit):
    count = lax.axis_size(axis)
    return lax.ppermute(value, axis, [(index, index ^ bit) for index in range(count)])


def position_table(total_rows, width_model, mem_rows, seg_rows):
    row_ids = np.arange(total_rows, dtype=np.float32)
    distance = np.float32(mem_rows + seg_rows - 1) - row_ids
    power = np.arange(0, width_model, 2, dtype=np.float32) / np.float32(width_model)
    freqs = np.float32(1.0) / np.power(np.float32(10000.0), power)
    angles = distance[:, None] * freqs[None, :]
    return np.concatenate([np.sin(angles), np.cos(angles)], axis=1).astype(np.float32)


def shards(
    content_in, memory, mask_embed, doc_ids, orders, targets, slot_used,
    w_query, w_key, w_value, w_out, w_rel, bias_content, bias_position, bias_segment, seg_embed,
    norm1_gain, norm1_shift, ffn_in, ffn_in_bias, ffn_out, ffn_out_bias, norm2_gain, norm2_shift,
    content_cot, query_cot,
):
    slots, seg_rows, width = content_in.shape
    mem_rows = memory.shape[2]
    heads, dim = bias_content.shape[1:]
    ff = ffn_in.shape[2]
    key_rows, rows = mem_rows + seg_rows, 2 * seg_rows
    rel_rows = key_rows + seg_rows
    section = lax.axis_index(SECTION).astype(jnp.int32)
    dp = lax.axis_index(DP).astype(jnp.int32)
    dp_count = lax.axis_size(DP)
    inside = dp % GROUP
    at = jnp.where((inside // 2) % 2 == 0, inside // 4, RING - 1 - inside // 4)
    lane = jnp.arange(2 * RING + 2, dtype=jnp.int32)
    meta = jnp.where(
        lane < RING,
        (at - lane) & (RING - 1),
        jnp.where(
            lane < 2 * RING,
            (-at - lane) & (RING - 1),
            jnp.where(lane == META_CORE, dp % 2, section),
        ),
    )
    pos_b = jnp.asarray(position_table(rel_rows, width, mem_rows, seg_rows)).astype(BF16)
    small, rel = pl.pallas_call(
        prepare_body,
        out_shape=(shape(SMALL_ROWS, width, dtype=F32), shape(rel_rows, width)),
        compiler_params=params(),
    )(
        bias_content, bias_position, bias_segment,
        jnp.transpose(seg_embed[0], (1, 0, 2)), norm1_gain, norm1_shift, ffn_out_bias, norm2_gain,
        norm2_shift, mask_embed.reshape(1, width), ffn_in_bias, pos_b, w_rel,
    )

    vm, dma = pltpu.VMEM, pltpu.SemaphoreType.DMA
    row_b, row_f = shape(slots, rows, width), shape(slots, rows, width, dtype=F32)
    kept = dict(
        joined=row_b, stream=row_b, qc=row_b, qp=row_b, qs=row_b, k=row_b, v=row_b, mixed=row_b,
        p=shape(slots, heads, rows, key_rows),
        mid_in=row_f,
        outer=row_f,
        slope=shape(slots, rows, ff),
        me=shape(2, slots, rows, width),
        ua=shape(2, slots, rows, ff),
        content_out=shape(1, slots, seg_rows, width),
        query_out=shape(1, slots, seg_rows, width),
    )
    vrow_b, vrow_f, square, wide = vm((rows, width), BF16), vm((rows, width), F32), vm((width, width), BF16), vm((rows, ff), BF16)
    weights_f = dict(fi=vm((width, ff), BF16), fo=vm((ff, width), BF16))
    weights_a = dict(wk=square, wq=square, wv=square, wo=square, rel=vm((rel_rows, width), BF16))
    probs_scratch = vm((heads, rows, key_rows), BF16)
    forward_scratch = dict(
        joined=vrow_b, stream=vrow_b, qc=vrow_b, qp=vrow_b, qs=vrow_b, k=vrow_b, v=vrow_b, mixed=vrow_b,
        midb=vrow_b, out=vrow_b, p=probs_scratch,
        same=vm((seg_rows, seg_rows), F32),
        bias=vm((2, seg_rows, seg_rows), F32),
        mid_in=vrow_f, outer=vrow_f, act=wide, slope=wide,
        sem_in=dma((11,)),
        sem_out=dma((20,)),
        **weights_f, **weights_a,
    )
    common = dict(meta=(SMEM_SPEC, meta), slot_used=(SMEM_SPEC, slot_used), **in_vmem(small=small))
    ids = in_vmem(docs=doc_ids, orders=orders, targets=targets)
    weights_attention = in_hbm(w_key=w_key, w_query=w_query, w_value=w_value, w_out=w_out, rel=rel)
    weights_ffn = in_hbm(ffn_in=ffn_in, ffn_out=ffn_out)
    sent = {}
    for call in range(4):
        layer, slot = call // 2, call % 2
        source = in_hbm(content_in=content_in) if layer == 0 else in_hbm(arrived=sent[slot])
        inputs = common | ids | in_hbm(memory=memory) | weights_attention | weights_ffn | source
        fresh = dict(sent=shape(rows, width)) if layer == 0 else {}
        kept, new = call_kernel(forward_body, layer, slot, inputs, kept, fresh, forward_scratch)
        if layer == 0:
            sent[slot] = lax.ppermute(new.popitem()[1], SECTION, [(0, 1)])
    kept = types.SimpleNamespace(**kept)

    tail_scratch = dict(
        outer=vrow_f, mid_in=vrow_f, cot=vrow_b, returned=vrow_b, e=vrow_b, ab=vrow_b, a=vrow_f, acc=vrow_f,
        u=wide, slope=wide,
        sums=vm((16, width), F32),
        sem_in=dma((8,)),
        sem_out=dma((8,)),
        **weights_f,
    )
    head_scratch = dict(
        ab=vrow_b, x=vrow_b, k=vrow_b, v=vrow_b, qc=vrow_b, qp=vrow_b, qs=vrow_b, qpf=vrow_b, dk=vrow_b,
        dv=vrow_b, dqb=vrow_b, out=vrow_b, p=probs_scratch, a=vrow_f, dq=vrow_f, dqp=vrow_f,
        drel=vm((rel_rows, width), F32),
        sums=vm((8, width), F32),
        sem_in=dma((13,)),
        sem_out=dma((8,)),
        **weights_a,
    )
    tail_kept = dict(me=kept.me, ua=kept.ua, ab=row_b, sums_tail=shape(slots, 16, width, dtype=F32))
    head_kept = dict(
        dk=row_b, dv=row_b, dq=row_b,
        drel=shape(slots, rel_rows, width, dtype=F32),
        input_grad=shape(1, slots, seg_rows, width),
        sums_head=shape(slots, 8, width, dtype=F32),
    )
    flat = lambda v: v.reshape(v.shape[:-3] + (slots * rows, v.shape[-1]))
    returned = {}
    for call in range(4):
        layer, slot = 1 - call // 2, 1 - call % 2
        inputs = common | weights_ffn | in_hbm(
            outer=kept.outer, slope=kept.slope, mid_in=kept.mid_in, content_cot=content_cot, query_cot=query_cot
        )
        if layer == 0:
            inputs |= in_hbm(returned=returned[slot])
        tail_kept, new = call_kernel(
            tail_body, layer, slot, inputs, tail_kept, dict(a=shape(rows, width, dtype=F32)), tail_scratch
        )
        grad_a = new.popitem()[1]
        tail_now = types.SimpleNamespace(**tail_kept)
        inputs = common | in_vmem(docs=doc_ids) | weights_attention | in_hbm(
            p=kept.p, k=kept.k, v=kept.v, qc=kept.qc, qp=kept.qp, qs=kept.qs, ab=tail_now.ab, a=grad_a
        )
        fresh = dict(sent=shape(rows, width)) if layer == 1 else {}
        head_kept, new = call_kernel(head_body, layer, slot, inputs, head_kept, fresh, head_scratch)
        if layer == 1:
            returned[slot] = lax.ppermute(new.popitem()[1], SECTION, [(1, 0)])
    grads = types.SimpleNamespace(**head_kept)

    me, ua = flat(tail_now.me), flat(tail_now.ua)
    operands = [flat(v) for v in (kept.stream, kept.joined, kept.mixed, grads.dq, grads.dk, grads.dv, tail_now.ab)]
    operands.append(grads.drel)
    own, others = {}, {}

    def add(ring, step, came=None):
        total = own[ring, step].astype(F32) + others[ring, step].astype(F32)
        return (total if came is None else total + came.astype(F32)).astype(BF16)

    def form(first, last, after):
        meta_now = meta if after is None else lax.optimization_barrier((meta, *after))[0]
        formed = pieces(first, last, meta_now, me, ua, operands)
        for ring in range(2):
            handed = swapped(formed[2 * ring + 1], DP, 1)
            for step in range(first, last):
                own[ring, step] = formed[2 * ring][step - first]
                others[ring, step] = handed[step - first]

    form(0, 1, None)
    acc = [add(0, 0), add(1, 0)]
    form(1, RING, acc)

    sums = jnp.concatenate(
        [grads.sums_head[0] + grads.sums_head[1], tail_now.sums_tail[0] + tail_now.sums_tail[1]], axis=0
    )
    row = lax.broadcasted_iota(jnp.int32, sums.shape, 0)
    sums = jnp.where((row == 5) & (section != 0), 0.0, sums)
    bits = [1 << n for n in range(dp_count.bit_length() - 1)]

    steps = ring_steps(dp_count)
    for step in range(1, RING):
        came = [lax.ppermute(acc[ring], DP, steps) for ring in range(2)]
        moving = swapped(sums, DP, bits.pop(0)) if bits else None
        acc = [add(ring, step, came[ring]) for ring in range(2)]
        if moving is not None:
            sums = sums + moving
            sums, acc[0] = lax.optimization_barrier((sums, acc[0]))
    for bit in bits:
        sums = sums + swapped(sums, DP, bit)
    mask_total = sums[5:6, :]
    mask_total = mask_total + swapped(mask_total, SECTION, 1)
    acc_a, acc_b = acc
    bit = GROUP
    while bit < dp_count:
        acc_a = (acc_a.astype(F32) + swapped(acc_a, DP, bit).astype(F32)).astype(BF16)
        acc_b = (acc_b.astype(F32) + swapped(acc_b, DP, bit).astype(F32)).astype(BF16)
        bit *= 2
    ffn_outs = [shape(1, width, ff, dtype=F32), shape(1, ff, width, dtype=F32)]
    rest_outs = [shape(1, width, width, dtype=F32) for _ in range(4)] + [shape(rel_rows, width, dtype=F32)]
    head_shape = shape(heads, 1, dim, dtype=F32)
    row_shape = shape(1, width, dtype=F32)
    (
        grad_bc, grad_bp, grad_bs, grad_seg, grad_n1g, grad_n1s, grad_fib, grad_fob, grad_n2g, grad_n2s, mask_grad,
    ) = pl.pallas_call(
        finish_small_body,
        out_shape=(
            head_shape, head_shape, head_shape, shape(heads, 2, dim, dtype=F32), row_shape, row_shape,
            shape(1, ff, dtype=F32), row_shape, row_shape, row_shape, row_shape,
        ),
        compiler_params=params(),
    )(sums, mask_total)
    mask_grad = mask_grad.reshape(width)
    tokens_a, tokens_b = [], []
    for step in range(RING):
        before_a, before_b = [], []
        if step:
            if step > 1:
                acc_a, *before_a = lax.optimization_barrier((acc_a, tokens_a[step - 2]))
                acc_b, *before_b = lax.optimization_barrier((acc_b, tokens_b[step - 2]))
            if step == 3:
                mask_grad, acc_a = lax.optimization_barrier((mask_grad, acc_a))
            acc_a = lax.ppermute(acc_a, DP, steps)
            acc_b = lax.ppermute(acc_b, DP, steps)
        ffn_outs, token = unpack(
            unpack_a_body, step, HEAD_ROWS, meta, acc_a, swapped(acc_a, DP, 1), ffn_outs, before_a
        )
        tokens_a.append(token)
        everything, token = unpack(
            unpack_b_body, step, B_ROWS, meta, acc_b, swapped(acc_b, DP, 1), [*ffn_outs, *rest_outs], before_b
        )
        tokens_b.append(token)
        ffn_outs, rest_outs = everything[:2], everything[2:]
    grad_ffn_in, grad_ffn_out = ffn_outs
    grad_w_query, grad_w_key, grad_w_value, grad_w_out, grad_rel = rest_outs
    grad_w_rel = pl.pallas_call(
        finish_rel_body, out_shape=shape(1, width, width, dtype=F32), compiler_params=params()
    )(pos_b, grad_rel)
    one_layer = lambda v: v.reshape(1, heads, dim)
    return (
        kept.content_out, kept.query_out, grads.input_grad, mask_grad,
        grad_w_query, grad_w_key, grad_w_value, grad_w_out, grad_w_rel,
        one_layer(grad_bc), one_layer(grad_bp), one_layer(grad_bs), jnp.transpose(grad_seg, (1, 0, 2))[None],
        grad_n1g, grad_n1s, grad_ffn_in, grad_fib, grad_ffn_out, grad_fob, grad_n2g, grad_n2s,
    )


def solution(mesh):
    two, three, four = P(SECTION, None), P(SECTION, None, None), P(SECTION, None, None, None)
    rows = P(SECTION, DP, None, None)
    return jax.shard_map(
        shards,
        mesh=mesh,
        in_specs=(
            P(DP, None, None), rows, P(), P(DP, None), P(DP, None), P(DP, None), P(DP), *[three] * 8, four,
            two, two, three, two, three, two, two, two, rows, rows,
        ),
        out_specs=(
            rows, rows, rows, P(), *[three] * 8, four, two, two, three, two, three, two, two, two,
        ),
        check_vma=False,
    )
```

```python
import functools
import types

import jax
import jax.numpy as jnp
import numpy as np
from jax import lax
from jax.experimental import pallas as pl
from jax.experimental.pallas import tpu as pltpu
from jax.sharding import PartitionSpec as P

BF16 = jnp.bfloat16
F32 = jnp.float32
NEG_FILL = -1e30
NORM_EPS = 1e-05
GELU_A = 0.7978845608028654
GELU_B = 0.044715
VMEM_LIMIT = 60 * 1024 * 1024
LANES = 128
LAYER_FLOPS = 9_000_000_000
RING = 8
META_CORE, META_SECTION = 2 * RING, 2 * RING + 1

ROW_BC, ROW_BP, ROW_BS, ROW_SEG0, ROW_SEG1 = 0, 1, 2, 3, 4
ROW_N1G, ROW_N1S, ROW_FOB, ROW_N2G, ROW_N2S, ROW_MASK, ROW_FIB = 5, 6, 7, 8, 9, 10, 11
SMALL_ROWS = 16


def dot_nn(left, right):
    return jnp.dot(left, right, preferred_element_type=F32)


def dot_nt(left, right):
    return lax.dot_general(left, right, (((1,), (1,)), ((), ())), preferred_element_type=F32)


def dot_tn(left, right):
    return lax.dot_general(left, right, (((0,), (0,)), ((), ())), preferred_element_type=F32)


def col_sum(block):
    return jnp.sum(block, axis=0, keepdims=True)


def norm_parts(rows):
    center = jnp.mean(rows, axis=-1, keepdims=True)
    offset = rows - center
    spread = jnp.mean(offset * offset, axis=-1, keepdims=True)
    scale = lax.rsqrt(spread + NORM_EPS)
    return offset * scale, scale


def norm_back(grad, unit, scale, gain):
    inner = grad * gain
    mean_inner = jnp.mean(inner, axis=-1, keepdims=True)
    mean_cross = jnp.mean(inner * unit, axis=-1, keepdims=True)
    return (inner - mean_inner - unit * mean_cross) * scale


def half_masks():
    lane = lax.broadcasted_iota(jnp.int32, (1, LANES), 1)
    low = lane < LANES // 2
    return low, low.astype(F32).astype(BF16), (~low).astype(F32).astype(BF16)


def stack_heads(block, low_b, high_b):
    return jnp.concatenate([block * low_b, block * high_b], axis=0)


def copy_in(pairs, sems):
    copies = [
        pltpu.make_async_copy(src, dst, sems.at[n]) for n, (src, dst) in enumerate(pairs)
    ]
    for copy in copies:
        copy.start()
    return copies


def name_refs(names_in, names_out, names_scratch, refs):
    groups, start = [], 0
    for names in (names_in, names_out, names_scratch):
        groups.append(types.SimpleNamespace(**dict(zip(names, refs[start : start + len(names)]))))
        start += len(names)
    return groups


def forward_body(section, slot, names_in, names_out, names_scratch, *refs):
    r, o, s = name_refs(names_in, names_out, names_scratch, refs)
    meta = r.meta
    seg_rows, width = s.stream.shape[0] // 2, s.stream.shape[1]
    key_rows = s.joined.shape[0]
    pairs_count = width // LANES
    ff = s.act.shape[1]
    score_scale = 0.125

    @pl.when(meta[META_SECTION] == section)
    def _run():
        sem_in, sem_out = s.sem_in, s.sem_out
        mem_rows = key_rows - seg_rows
        x_src = r.content_in.at[slot] if section == 0 else r.arrived.at[pl.ds(0, seg_rows)]
        loads = [
            (r.memory.at[0, slot], s.joined.at[pl.ds(0, mem_rows)]),
            (x_src, s.joined.at[pl.ds(mem_rows, seg_rows)]),
            (x_src, s.stream.at[pl.ds(0, seg_rows)]),
            (r.w_key.at[0], s.wk),
            (r.w_query.at[0], s.wq),
            (r.rel, s.rel),
            (r.w_value.at[0], s.wv),
            (r.w_out.at[0], s.wo),
            (r.ffn_in.at[0], s.fi),
            (r.ffn_out.at[0], s.fo),
        ]
        moves = []
        if section == 1:
            query_rows = pl.ds(seg_rows, seg_rows)
            moves = copy_in([(r.arrived.at[query_rows], s.stream.at[query_rows])], s.sem_first)
        moves = copy_in(loads, sem_in) + moves
        stores = []

        def store(src, dst):
            copy = pltpu.make_async_copy(src, dst, sem_out.at[len(stores)])
            copy.start()
            stores.append(copy)

        small = r.small
        used = (r.slot_used[slot] > 0).astype(jnp.int32).astype(F32)
        if section == 0:
            s.stream[seg_rows:, :] = jnp.broadcast_to(
                small[ROW_MASK : ROW_MASK + 1, :], (seg_rows, width)
            ).astype(BF16)
        square = (seg_rows, seg_rows)
        doc = jnp.broadcast_to(r.docs[slot : slot + 1, :].astype(F32), square)
        order = jnp.broadcast_to(r.orders[slot : slot + 1, :].astype(F32), square)
        target = jnp.broadcast_to(r.targets[slot : slot + 1, :].astype(F32), square)
        same = doc == doc.T
        visible = same & ((target == 0.0) | (order <= order.T))
        row_id = lax.broadcasted_iota(jnp.int32, square, 0)
        col_id = lax.broadcasted_iota(jnp.int32, square, 1)
        s.bias[0] = jnp.where(visible, 0.0, NEG_FILL)
        s.bias[1] = jnp.where(visible & (row_id != col_id), 0.0, NEG_FILL)

        for n in (0, 1, 3):
            moves[n].wait()
        s.k[...] = dot_nn(s.joined[...], s.wk[...]).astype(BF16)
        store(s.k, o.k.at[slot])
        store(s.joined, o.joined.at[slot])
        moves[2].wait()
        if section == 1:
            moves[10].wait()
        store(s.stream, o.stream.at[slot])
        moves[4].wait()
        queries = dot_nn(s.stream[...], s.wq[...])
        for block, kept, row in ((s.qc, o.qc, ROW_BC), (s.qp, o.qp, ROW_BP), (s.qs, o.qs, ROW_BS)):
            with_bias = (queries + small[row : row + 1, :]).astype(BF16)
            block[...] = (with_bias.astype(F32) * score_scale).astype(BF16)
            store(block, kept.at[slot])
        moves[6].wait()
        s.v[...] = dot_nn(s.joined[...], s.wv[...]).astype(BF16)
        store(s.v, o.v.at[slot])
        moves[5].wait()

        low, low_b, high_b = half_masks()
        bias_by_stream = [s.bias[0], s.bias[1]]
        inside = col_id <= row_id
        for pair in range(pairs_count):
            sl = slice(pair * LANES, (pair + 1) * LANES)
            position = dot_nt(stack_heads(s.qp[:, sl], low_b, high_b), s.rel[:, sl])
            for part in range(4):
                base = part * seg_rows
                turned = [
                    pltpu.roll(
                        position[base : base + seg_rows, n * LANES : (n + 1) * LANES],
                        1, axis=1, stride=1, stride_axis=0,
                    )
                    for n in range(3)
                ]
                rolled = jnp.concatenate(
                    [jnp.where(inside, turned[n], turned[n + 1]) for n in range(2)], axis=1
                )
                s.pos[pair, base : base + seg_rows, :] = rolled
        for pair in range(pairs_count):
            sl = slice(pair * LANES, (pair + 1) * LANES)
            content = dot_nt(stack_heads(s.qc[:, sl], low_b, high_b), s.k[:, sl])
            segments = jnp.concatenate(
                [
                    jnp.broadcast_to(small[row : row + 1, sl].astype(BF16) * mask, (LANES, LANES))
                    for mask in (low_b, high_b)
                    for row in (ROW_SEG0, ROW_SEG1)
                ],
                axis=0,
            )
            pieces_wide = dot_nt(s.qs[:, sl], segments)
            probs_pair = []
            for head in range(2):
                probs_streams = []
                for stream in range(2):
                    base = (2 * head + stream) * seg_rows
                    rows = slice(stream * seg_rows, (stream + 1) * seg_rows)
                    same_part = pieces_wide[rows, 2 * head * LANES : (2 * head + 1) * LANES]
                    other_part = pieces_wide[rows, (2 * head + 1) * LANES : (2 * head + 2) * LANES]
                    body = content[base : base + seg_rows, :] + s.pos[pair, base : base + seg_rows, :]
                    left = body[:, :mem_rows] + other_part
                    right = body[:, mem_rows:] + jnp.where(same, same_part, other_part) + bias_by_stream[stream]
                    peak = jnp.max(jnp.maximum(left, right), axis=-1, keepdims=True)
                    left = jnp.exp(left - peak)
                    right = jnp.exp(right - peak)
                    total = jnp.sum(left + right, axis=-1, keepdims=True)
                    inverse = 1.0 / total
                    probs_streams.append(
                        jnp.concatenate([left * inverse, right * inverse], axis=1).astype(BF16)
                    )
                probs = jnp.concatenate(probs_streams, axis=0)
                s.p[2 * pair + head] = probs
                store(s.p.at[2 * pair + head], o.p.at[slot, 2 * pair + head])
                probs_pair.append(probs)
            mixed = dot_nn(
                jnp.concatenate(probs_pair, axis=1), stack_heads(s.v[:, sl], low_b, high_b)
            )
            s.mixed[:, sl] = mixed.astype(BF16)
        store(s.mixed, o.mixed.at[slot])

        moves[7].wait()
        middle_in = dot_nn(s.mixed[...], s.wo[...]) + s.stream[...].astype(F32)
        s.mid_in[...] = middle_in
        store(s.mid_in, o.mid_in.at[slot])
        unit, _ = norm_parts(middle_in)
        middle = unit * small[ROW_N1G : ROW_N1G + 1, :] + small[ROW_N1S : ROW_N1S + 1, :]
        s.midb[...] = middle.astype(BF16)
        store(s.midb, o.me.at[0, slot])
        s.outer[...] = middle + small[ROW_FOB : ROW_FOB + 1, :]
        moves[8].wait()
        moves[9].wait()
        for step in range(ff // width):
            cols = slice(step * width, (step + 1) * width)
            inner = (
                dot_nn(s.midb[...], s.fi[:, cols])
                + small[ROW_FIB + step : ROW_FIB + step + 1, :]
            )
            square_in = inner * inner
            wave = jnp.tanh(GELU_A * inner * (1.0 + GELU_B * square_in))
            half = 0.5 * (1.0 + wave)
            active = (inner * half).astype(BF16)
            slope = half + (0.5 * GELU_A) * inner * (1.0 - wave * wave) * (1.0 + 3.0 * GELU_B * square_in)
            s.act[:, cols] = active
            s.slope[:, cols] = slope.astype(BF16)
            part = pl.ds(step * width, width)
            store(s.act.at[:, part], o.ua.at[1, slot, :, part])
            store(s.slope.at[:, part], o.slope.at[slot, :, part])
            s.outer[...] += dot_nn(active, s.fo[cols, :])
        store(s.outer, o.outer.at[slot])
        unit, _ = norm_parts(s.outer[...])
        result = unit * small[ROW_N2G : ROW_N2G + 1, :] + small[ROW_N2S : ROW_N2S + 1, :]
        s.out[...] = (result * used).astype(BF16)
        store(s.out.at[pl.ds(0, seg_rows)], o.content_out.at[0, slot])
        store(s.out.at[pl.ds(seg_rows, seg_rows)], o.query_out.at[0, slot])
        if section == 0:
            store(s.out, o.sent)
        for copy in stores:
            copy.wait()


def backward_body(section, slot, names_in, names_out, names_scratch, *refs):
    r, o, s = name_refs(names_in, names_out, names_scratch, refs)
    meta = r.meta
    rows, width = s.a.shape
    seg_rows = rows // 2
    ff = s.slope.shape[1]
    key_rows = s.k.shape[0]
    mem_rows = key_rows - seg_rows
    pairs_count = width // LANES
    score_scale = 0.125

    @pl.when(meta[META_SECTION] == section)
    def _run():
        first_loads = [
            (r.content_cot.at[0, slot], s.cot.at[pl.ds(0, seg_rows)]),
            (r.query_cot.at[0, slot], s.cot.at[pl.ds(seg_rows, seg_rows)]),
            (r.outer.at[slot], s.outer),
        ]
        if section == 0:
            first_loads.append((r.returned, s.returned))
        first = copy_in(first_loads, s.sem_first)
        loads = []
        for step in range(ff // width):
            part = pl.ds(step * width, width)
            loads.append((r.ffn_out.at[0, part], s.fo.at[part]))
            loads.append((r.slope.at[slot, :, part], s.slope.at[:, part]))
            loads.append((r.ffn_in.at[0, :, part], s.fi.at[:, part]))
        loads.append((r.mid_in.at[slot], s.mid_in))
        head_loads = [
            (r.w_out.at[0], s.wo),
            (r.v.at[slot], s.v),
            (r.p.at[slot], s.p),
            (r.k.at[slot], s.k),
            (r.qc.at[slot], s.qc),
            (r.qp.at[slot], s.qp),
            (r.qs.at[slot], s.qs),
            (r.rel, s.rel),
            (r.w_query.at[0], s.wq),
            (r.w_key.at[0], s.wk),
            (r.w_value.at[0], s.wv),
        ]
        stores = []

        def store(src, dst):
            copy = pltpu.make_async_copy(src, dst, s.sem_out.at[len(stores)])
            copy.start()
            stores.append(copy)

        small = r.small
        used = (r.slot_used[slot] > 0).astype(jnp.int32).astype(F32)
        for move in first:
            move.wait()
        moves = copy_in(loads, s.sem_tail)
        grad = s.cot[...].astype(F32) * used
        if section == 0:
            grad = grad + s.returned[...].astype(F32)
        unit, scale = norm_parts(s.outer[...])
        out = s.sums_t
        out[...] = jnp.zeros_like(out)
        out[4:5, :] = col_sum(grad * unit)
        out[5:6, :] = col_sum(grad)
        grad_outer = norm_back(grad, unit, scale, small[ROW_N2G : ROW_N2G + 1, :])
        s.e[...] = grad_outer.astype(BF16)
        store(s.e, o.me.at[1, slot])
        out[3:4, :] = col_sum(s.e[...].astype(F32))
        s.acc[...] = grad_outer
        for step in range(ff // width):
            for move in moves[3 * step : 3 * step + 3]:
                move.wait()
            cols = slice(step * width, (step + 1) * width)
            if step == 1:
                head_moves = copy_in(head_loads, s.sem_head)
            grad_active = dot_nt(s.e[...], s.fo[cols, :])
            inner_b = (s.slope[:, cols].astype(F32) * grad_active).astype(BF16)
            s.u[:, cols] = inner_b
            out[8 + step : 9 + step, :] = col_sum(inner_b.astype(F32))
            s.acc[...] += dot_nt(inner_b, s.fi[:, cols])
        store(s.u, o.ua.at[0, slot])
        moves[-1].wait()
        unit, scale = norm_parts(s.mid_in[...])
        grad = s.acc[...]
        out[1:2, :] = col_sum(grad * unit)
        out[2:3, :] = col_sum(grad)
        s.a[...] = norm_back(grad, unit, scale, small[ROW_N1G : ROW_N1G + 1, :])
        s.ab[...] = s.a[...].astype(BF16)
        store(s.ab, o.ab.at[slot])
        store(s.sums_t, o.sums_tail.at[slot])

        square = (seg_rows, seg_rows)
        doc = jnp.broadcast_to(r.docs[slot : slot + 1, :].astype(F32), square)
        same_one = (doc == doc.T).astype(F32)
        same = jnp.concatenate([same_one, same_one], axis=0)
        flip_rows = lax.broadcasted_iota(jnp.int32, (rows, rows), 0)
        flip_cols = lax.broadcasted_iota(jnp.int32, (rows, rows), 1)
        flipped_to = jnp.where(flip_rows < seg_rows, seg_rows - 1, rows + seg_rows - 1) - flip_rows
        flip = (flip_cols == flipped_to).astype(F32).astype(BF16)
        out = s.sums
        out[...] = jnp.zeros_like(out)
        head_moves[0].wait()
        s.x[...] = dot_nt(s.ab[...], s.wo[...]).astype(BF16)
        for n in (1, 2, 3, 4, 5, 6, 7):
            head_moves[n].wait()
        s.qpf[...] = dot_nn(flip, s.qp[...]).astype(BF16)

        low, low_b, high_b = half_masks()
        past = lax.broadcasted_iota(jnp.int32, square, 1) >= lax.broadcasted_iota(jnp.int32, square, 0)
        for pair in range(pairs_count):
            sl = slice(pair * LANES, (pair + 1) * LANES)
            grads_mixed = stack_heads(s.x[:, sl], low_b, high_b)
            grad_probs = dot_nt(grads_mixed, s.v[:, sl])
            scores_b = []
            same_sums, other_sums = [], []
            for head in range(2):
                probs = s.p[2 * pair + head].astype(F32)
                product = probs * grad_probs[head * rows : (head + 1) * rows, :]
                delta = jnp.sum(product, axis=-1, keepdims=True)
                rounded = (product - probs * delta).astype(BF16)
                scores_b.append(rounded)
                wide = rounded.astype(F32)
                right = wide[:, mem_rows:] * same
                same_sum = jnp.sum(right, axis=-1, keepdims=True)
                same_sums.append(same_sum)
                other_sums.append(
                    jnp.sum(wide[:, :mem_rows] + (wide[:, mem_rows:] - right), axis=-1, keepdims=True)
                )
            stacked = jnp.concatenate(scores_b, axis=0)
            beside = jnp.concatenate(scores_b, axis=1)
            probs_stacked = jnp.concatenate([s.p[2 * pair], s.p[2 * pair + 1]], axis=0)
            s.dv[:, sl] = dot_tn(probs_stacked, grads_mixed).astype(BF16)
            s.dk[:, sl] = dot_tn(stacked, stack_heads(s.qc[:, sl], low_b, high_b)).astype(BF16)
            grad_content = dot_nn(beside, stack_heads(s.k[:, sl], low_b, high_b)) * score_scale
            same_sel = jnp.where(low, same_sums[0], same_sums[1])
            other_sel = jnp.where(low, other_sums[0], other_sums[1])
            seg0 = small[ROW_SEG0 : ROW_SEG0 + 1, sl]
            seg1 = small[ROW_SEG1 : ROW_SEG1 + 1, sl]
            grad_segment = (same_sel * seg0 + other_sel * seg1) * score_scale
            qs = s.qs[:, sl].astype(F32)
            out[0:1, sl] = col_sum(grad_content)
            out[2:3, sl] = col_sum(grad_segment)
            out[3:4, sl] = col_sum(same_sel * qs)
            out[4:5, sl] = col_sum(other_sel * qs)
            s.dq[:, sl] = grad_content + grad_segment
            turned = dot_nn(flip, beside)
            shifted_heads = []
            for head in range(2):
                parts = []
                for stream in range(2):
                    blocks = [
                        pltpu.roll(
                            turned[
                                stream * seg_rows : (stream + 1) * seg_rows,
                                head * key_rows + n * LANES : head * key_rows + (n + 1) * LANES,
                            ],
                            0, axis=1, stride=1, stride_axis=0,
                        )
                        for n in range(2)
                    ]
                    blocks = [
                        jnp.where(past, blocks[0], 0.0),
                        jnp.where(past, blocks[1], blocks[0]),
                        jnp.where(past, 0.0, blocks[1]),
                    ]
                    parts.append(jnp.concatenate(blocks, axis=1).astype(BF16))
                shifted_heads.append(jnp.concatenate(parts, axis=0))
            grad_position = (
                dot_nn(
                    jnp.concatenate(shifted_heads, axis=1),
                    stack_heads(s.rel[:, sl], low_b, high_b),
                )
                * score_scale
            )
            out[1:2, sl] = col_sum(grad_position)
            s.dqp[:, sl] = grad_position
            s.drel[:, sl] = dot_tn(
                jnp.concatenate(shifted_heads, axis=0),
                stack_heads(s.qpf[:, sl], low_b, high_b),
            )
        store(s.dk, o.dk.at[slot])
        store(s.dv, o.dv.at[slot])
        store(s.drel, o.drel.at[slot])
        grad_position = s.dqp[...]
        position_high = grad_position.astype(BF16)
        position_low = (grad_position - position_high.astype(F32)).astype(BF16)
        grad_queries = s.dq[...] + dot_nn(flip, position_high) + dot_nn(flip, position_low)
        s.dqb[...] = grad_queries.astype(BF16)
        store(s.dqb, o.dq.at[slot])
        for n in (8, 9, 10):
            head_moves[n].wait()
        grad_rows = s.a[...] + dot_nt(s.dqb[...], s.wq[...])
        grad_content = (
            grad_rows[:seg_rows, :]
            + dot_nt(s.dk[mem_rows:, :], s.wk[...])
            + dot_nt(s.dv[mem_rows:, :], s.wv[...])
        )
        grad_query = grad_rows[seg_rows:, :]
        s.out[:seg_rows, :] = grad_content.astype(BF16)
        s.out[seg_rows:, :] = grad_query.astype(BF16)
        store(s.out.at[pl.ds(0, seg_rows)], o.input_grad.at[0, slot])
        if section == 1:
            store(s.out, o.sent)
        if section == 0:
            out[5:6, :] = col_sum(grad_query)
        store(s.sums, o.sums_head.at[slot])
        for copy in stores:
            copy.wait()


ANY_SPEC = pl.BlockSpec(memory_space=pltpu.HBM)
SMEM_SPEC = pl.BlockSpec(memory_space=pltpu.SMEM)
VMEM_SPEC = pl.BlockSpec(memory_space=pltpu.VMEM)


def call_kernel(body, section, slot, inputs, carried, fresh, scratch):
    names_in = list(inputs)
    arrays = [inputs[n][1] for n in names_in]
    specs = [inputs[n][0] for n in names_in]
    aliases = {}
    names_out = list(carried) + list(fresh)
    out_shapes = []
    for position, key in enumerate(carried):
        value = carried[key]
        out_shapes.append(jax.ShapeDtypeStruct(value.shape, value.dtype))
        if not isinstance(value, jax.ShapeDtypeStruct):
            aliases[len(arrays)] = position
            arrays.append(value)
            specs.append(ANY_SPEC)
            names_in.append(key + "_")
    out_shapes += [fresh[key] for key in fresh]
    results = pl.pallas_call(
        functools.partial(body, section, slot, names_in, names_out, list(scratch)),
        out_shape=tuple(out_shapes),
        in_specs=specs,
        out_specs=tuple(ANY_SPEC for _ in out_shapes),
        scratch_shapes=list(scratch.values()),
        input_output_aliases=aliases,
        compiler_params=pltpu.CompilerParams(vmem_limit_bytes=VMEM_LIMIT),
        cost_estimate=pl.CostEstimate(flops=LAYER_FLOPS, bytes_accessed=20_000_000, transcendentals=0),
    )(*arrays)
    named = dict(zip(names_out, results))
    return {k: named[k] for k in carried}, {k: named[k] for k in fresh}


def in_hbm(**arrays):
    return {key: (ANY_SPEC, value) for key, value in arrays.items()}


def in_vmem(**arrays):
    return {key: (VMEM_SPEC, value) for key, value in arrays.items()}


def params():
    return pltpu.CompilerParams(vmem_limit_bytes=VMEM_LIMIT)


def cost(flops, moved):
    return pl.CostEstimate(flops=flops, bytes_accessed=moved, transcendentals=0)


def shape(*dims, dtype=BF16):
    return jax.ShapeDtypeStruct(dims, dtype)


def prepare_body(bc, bp, bs, seg, n1g, n1s, fob, n2g, n2s, mask, fib, pos, w_rel, small, rel):
    heads, dim = bc.shape[1:]
    width = heads * dim
    wide = [(row, value[0].astype(F32)) for row, value in ((ROW_BC, bc), (ROW_BP, bp), (ROW_BS, bs))]
    for head in range(heads):
        cols = slice(head * dim, (head + 1) * dim)
        for row, value in wide:
            small[row : row + 1, cols] = value[head : head + 1, :]
        small[ROW_SEG0 : ROW_SEG1 + 1, cols] = seg[head].astype(F32)
    for row, value in (
        (ROW_N1G, n1g), (ROW_N1S, n1s), (ROW_FOB, fob), (ROW_N2G, n2g), (ROW_N2S, n2s), (ROW_MASK, mask),
    ):
        small[row : row + 1, :] = value[...].astype(F32)
    for step in range(4):
        small[ROW_FIB + step : ROW_FIB + step + 1, :] = fib[:, step * width : (step + 1) * width].astype(F32)
    small[SMALL_ROWS - 1 : SMALL_ROWS, :] = jnp.zeros((1, width), F32)
    rel[...] = dot_nn(pos[...], w_rel[0]).astype(BF16)


GROUP = 16
HALF = 384
HEAD_ROWS = 320
REST_ROWS = HALF - HEAD_ROWS
REL_PIECE = 24
BLOCK = slice(REST_ROWS, REST_ROWS + HALF // 2)
REL = slice(BLOCK.stop, BLOCK.stop + REL_PIECE)
B_ROWS = BLOCK.stop + 32


def lane_slice(start, size):
    return pl.ds(pl.multiple_of(start, LANES), size)


def block_rows(index, size):
    return pl.ds(pl.multiple_of(index * size, size), size)


def piece_body(first, count, meta, me, ua, stream, joined, mixed, dq, dk, dv, ab, drel, *refs):
    own_a, other_a, own_b, other_b = refs[:4]
    low_l, low_r, high_l, high_r, left, right, rel, stage_a, stage_b, sems, out_sems = refs[4:]
    core = meta[META_CORE]
    width = low_r.shape[2]

    def start(src, dst, sem):
        copy = pltpu.make_async_copy(src, dst, sem)
        copy.start()
        return copy

    def rel_rows(at):
        return drel.at[:, pl.ds(pl.multiple_of(at * REL_PIECE, 8), REL_PIECE), :]

    def fetch(at, early, late, to_left, to_right, sem):
        inside = at % 4
        rows_at, cols_at = block_rows(inside // 2, HALF), block_rows(inside % 2, HALF)

        @pl.when(at < RING // 2)
        def _early():
            start(early[0].at[:, rows_at], to_left, sem[0])
            start(early[1].at[:, cols_at], to_right, sem[1])

        @pl.when(at >= RING // 2)
        def _late():
            start(late[0].at[:, rows_at], to_left, sem[0])
            start(late[1].at[:, cols_at], to_right, sem[1])

        return [
            pltpu.make_async_copy(early[0].at[:, rows_at], to_left, sem[0]),
            pltpu.make_async_copy(early[1].at[:, cols_at], to_right, sem[1]),
        ]

    moves = [start(me.at[1], high_r, sems.at[10 * count])]
    steps = []
    for n in range(count):
        low_at, high_at = meta[first + n], meta[RING + first + n]
        sem = [sems.at[10 * n + k] for k in range(10)]
        low_moves = [
            start(me.at[0, :, block_rows(low_at % 2, HALF)], low_l.at[n], sem[0]),
            start(ua.at[0, :, block_rows(low_at // 2, width)], low_r.at[n], sem[1]),
        ]
        high_moves = [start(ua.at[1, :, block_rows(high_at, HALF)], high_l.at[n], sem[2])]
        low_rest = fetch(low_at, (stream, dq), (joined, dk), left.at[n, 0], right.at[n, 0], sem[4:6])
        high_rest = fetch(high_at, (joined, dv), (mixed, ab), left.at[n, 1], right.at[n, 1], sem[6:8])
        low_rest.append(start(rel_rows(low_at), rel.at[n, 0], sem[8]))
        high_rest.append(start(rel_rows(RING + high_at), rel.at[n, 1], sem[9]))
        steps.append((low_moves, high_moves + moves, low_rest, high_rest))
        moves = []
    writes = []
    for n, (low_moves, high_moves, low_rest, high_rest) in enumerate(steps):
        for waits, lhs, rhs, place in (
            (low_moves, low_l.at[n], low_r.at[n], core), (high_moves, high_l.at[n], high_r, 1 - core),
        ):
            for move in waits:
                move.wait()
            whole = dot_tn(lhs[...], rhs[...]).astype(BF16)
            stage_a[n, place] = whole[:HEAD_ROWS]
            stage_b[n, place, :REST_ROWS] = whole[HEAD_ROWS:]
        writes.append(start(stage_a.at[n, 1], other_a.at[n], out_sems.at[4 * n]))
        writes.append(start(stage_a.at[n, 0], own_a.at[n], out_sems.at[4 * n + 1]))
        for waits, half, place in ((low_rest, 0, core), (high_rest, 1, 1 - core)):
            for move in waits:
                move.wait()
            value = dot_tn(left[n, half], right[n, half]).astype(BF16)
            stage_b[n, place, BLOCK.start : BLOCK.stop, :HALF] = value[: HALF // 2]
            stage_b[n, place, BLOCK.start : BLOCK.stop, HALF:] = value[HALF // 2 :]
            stage_b[n, place, BLOCK.stop :] = jnp.concatenate(
                [rel[n, half, 0] + rel[n, half, 1], jnp.zeros((B_ROWS - REL.stop, width), F32)], axis=0
            ).astype(BF16)
        writes.append(start(stage_b.at[n, 1], other_b.at[n], out_sems.at[4 * n + 2]))
        writes.append(start(stage_b.at[n, 0], own_b.at[n], out_sems.at[4 * n + 3]))
    for copy in writes:
        copy.wait()


def pieces(first, count, meta, me, ua, operands):
    rows, width = operands[0].shape

    def vm(*dims, dtype=BF16):
        return pltpu.VMEM((count, *dims), dtype)

    return pl.pallas_call(
        functools.partial(piece_body, first, count),
        out_shape=[shape(count, size, width) for size in (HEAD_ROWS, HEAD_ROWS, B_ROWS, B_ROWS)],
        in_specs=[SMEM_SPEC] + [ANY_SPEC] * (2 + len(operands)),
        out_specs=[ANY_SPEC] * 4,
        scratch_shapes=[
            vm(rows, HALF), vm(rows, width), vm(rows, HALF), pltpu.VMEM((rows, width), BF16),
            vm(2, rows, HALF), vm(2, rows, HALF), vm(2, 2, REL_PIECE, width, dtype=F32),
            vm(2, HEAD_ROWS, width), vm(2, B_ROWS, width),
            pltpu.SemaphoreType.DMA((10 * count + 1,)), pltpu.SemaphoreType.DMA((4 * count,)),
        ],
        compiler_params=params(),
        cost_estimate=cost(6 * rows * HALF * width * count, 4_000_000 * count),
    )(meta, me, ua, *operands)


def by_core(meta, own, other, low_f, high_f):
    low = meta[META_CORE] == 0

    @pl.when(low)
    def _low():
        low_f[...] = own[...].astype(F32)
        high_f[...] = other[...].astype(F32)

    @pl.when(~low)
    def _high():
        low_f[...] = other[...].astype(F32)
        high_f[...] = own[...].astype(F32)


def ffn_places(fi, fo, low_at, high_at, first, count):
    width = fo.shape[2]
    return (
        fi.at[0, pl.ds(pl.multiple_of((low_at % 2) * HALF + first, 8), count), lane_slice((low_at // 2) * width, width)],
        fo.at[0, pl.ds(pl.multiple_of(high_at * HALF + first, 8), count), :],
    )


def unpack_body(step, last, meta, own_a, other_a, own_b, other_b, *refs):
    if last:
        pos, rel_in = refs[0], refs[7]
        fi, fo, wq, wk, wv, wo, rel, w_rel, low_a, high_a, low_f, high_f, sems, rel_all, rel_sem = refs[-15:]
        rel_copy = pltpu.make_async_copy(rel_in, rel_all, rel_sem.at[0])
        rel_copy.start()
    else:
        fi, fo, wq, wk, wv, wo, rel, token, low_a, high_a, low_f, high_f, sems = refs[-13:]
        token[...] = jnp.zeros_like(token)
    low_at, high_at = meta[step], meta[RING + step]
    by_core(meta, own_a, other_a, low_a, high_a)
    low_to, high_to = ffn_places(fi, fo, low_at, high_at, 0, HEAD_ROWS)
    copies = [
        pltpu.make_async_copy(low_a, low_to, sems.at[8]),
        pltpu.make_async_copy(high_a, high_to, sems.at[9]),
    ]
    for copy in copies:
        copy.start()
    by_core(meta, own_b, other_b, low_f, high_f)
    low_to, high_to = ffn_places(fi, fo, low_at, high_at, HEAD_ROWS, REST_ROWS)
    rest = pl.ds(0, REST_ROWS)
    rel_part = pl.ds(REL.start, REL_PIECE)

    def rel_to(at):
        return rel.at[pl.ds(pl.multiple_of(at * REL_PIECE, 8), REL_PIECE), :]

    later = [
        pltpu.make_async_copy(low_f.at[rest], low_to, sems.at[0]),
        pltpu.make_async_copy(high_f.at[rest], high_to, sems.at[1]),
    ]
    if not last:
        later.append(pltpu.make_async_copy(low_f.at[rel_part], rel_to(low_at), sems.at[2]))
        later.append(pltpu.make_async_copy(high_f.at[rel_part], rel_to(RING + high_at), sems.at[3]))
    for copy in later:
        copy.start()

    def block_copies(src, at, dst, sem):
        inside = at % 4
        return [
            pltpu.make_async_copy(
                src.at[pl.ds(BLOCK.start, HALF // 2), pl.ds(part * HALF, HALF)],
                dst.at[
                    0,
                    pl.ds(pl.multiple_of((inside // 2) * HALF + part * (HALF // 2), 8), HALF // 2),
                    lane_slice((inside % 2) * HALF, HALF),
                ],
                sems.at[sem + part],
            )
            for part in range(2)
        ]

    for src, at, early, late, n in ((low_f, low_at, wq, wk, 4), (high_f, high_at, wv, wo, 6)):

        @pl.when(at < RING // 2)
        def _early(src=src, at=at, early=early, n=n):
            for copy in block_copies(src, at, early, n):
                copy.start()

        @pl.when(at >= RING // 2)
        def _late(src=src, at=at, late=late, n=n):
            for copy in block_copies(src, at, late, n):
                copy.start()

        later += block_copies(src, at, early, n)
    if last:
        rel_copy.wait()
        for src, at in ((low_f, low_at), (high_f, RING + high_at)):
            rel_all[pl.ds(pl.multiple_of(at * REL_PIECE, 8), REL_PIECE), :] = src[REL, :]
        w_rel[0] = dot_tn(pos[...], rel_all[...].astype(BF16))
    for copy in copies + later:
        copy.wait()


def unpack(step, meta, own_a, other_a, own_b, other_b, outs, earlier, pos):
    given = [v for v in outs if not isinstance(v, jax.ShapeDtypeStruct)]
    width = own_a.shape[1]
    last = pos is not None
    extra = shape(1, width, width, dtype=F32) if last else shape(8, LANES, dtype=F32)
    scratch = [
        *[pltpu.VMEM((HEAD_ROWS, width), F32)] * 2,
        *[pltpu.VMEM((B_ROWS, width), F32)] * 2,
        pltpu.SemaphoreType.DMA((10,)),
    ]
    if last:
        scratch += [pltpu.VMEM(pos.shape, F32), pltpu.SemaphoreType.DMA((1,))]
    front = [meta, own_a, other_a, own_b, other_b] + ([pos] if last else [])
    *results, token = pl.pallas_call(
        functools.partial(unpack_body, (step + RING - 1) % RING, last),
        out_shape=tuple(shape(*v.shape, dtype=v.dtype) for v in outs) + (extra,),
        in_specs=[SMEM_SPEC] + [VMEM_SPEC] * (len(front) - 1) + [ANY_SPEC] * (len(given) + len(earlier)),
        out_specs=tuple(ANY_SPEC for _ in outs) + (VMEM_SPEC,),
        input_output_aliases={len(front) + n: n for n in range(len(given))},
        scratch_shapes=scratch,
        compiler_params=params(),
        cost_estimate=cost(0, 8_000_000),
    )(*front, *given, *earlier)
    return results, token


def finish_small_body(small, mask, bc, bp, bs, seg, n1g, n1s, fib, fob, n2g, n2s, mask_out):
    heads, dim = bc.shape[0], bc.shape[2]
    width = heads * dim
    for head in range(heads):
        cols = slice(head * dim, (head + 1) * dim)
        bc[head] = small[0:1, cols]
        bp[head] = small[1:2, cols]
        bs[head] = small[2:3, cols]
        seg[head] = small[3:5, cols]
    n1g[...] = small[9:10, :]
    n1s[...] = small[10:11, :]
    fob[...] = small[11:12, :]
    n2g[...] = small[12:13, :]
    n2s[...] = small[13:14, :]
    for step in range(4):
        fib[:, step * width : (step + 1) * width] = small[16 + step : 17 + step, :]
    mask_out[...] = mask[...]


def ring_steps(count):
    cycle = [(z, 0) for z in range(4)] + [(z, 1) for z in (3, 2, 1, 0)]
    steps = []
    for index in range(count):
        base, inside = index - index % GROUP, index % GROUP
        at = cycle.index((inside // 4, (inside // 2) % 2))
        z, y = cycle[(at + (1 if inside % 2 == 0 else -1)) % RING]
        steps.append((index, base + (z * 2 + y) * 2 + inside % 2))
    return steps


SECTION, DP = "section", "dp"


def swapped(value, axis, bit):
    count = lax.axis_size(axis)
    return lax.ppermute(value, axis, [(index, index ^ bit) for index in range(count)])


def position_table(total_rows, width_model, mem_rows, seg_rows):
    row_ids = np.arange(total_rows, dtype=np.float32)
    distance = np.float32(mem_rows + seg_rows - 1) - row_ids
    power = np.arange(0, width_model, 2, dtype=np.float32) / np.float32(width_model)
    freqs = np.float32(1.0) / np.power(np.float32(10000.0), power)
    angles = distance[:, None] * freqs[None, :]
    return np.concatenate([np.sin(angles), np.cos(angles)], axis=1).astype(np.float32)


def scratches(seg_rows, mem_rows, width, ff, heads):
    rows, key_rows, rel_rows = 2 * seg_rows, mem_rows + seg_rows, mem_rows + 2 * seg_rows
    vm, dma = pltpu.VMEM, pltpu.SemaphoreType.DMA
    vrow_b, vrow_f, square, wide = vm((rows, width), BF16), vm((rows, width), F32), vm((width, width), BF16), vm((rows, ff), BF16)
    weights_f = dict(fi=vm((width, ff), BF16), fo=vm((ff, width), BF16))
    weights_a = dict(wk=square, wq=square, wv=square, wo=square, rel=vm((rel_rows, width), BF16))
    probs_scratch = vm((heads, rows, key_rows), BF16)
    forward_scratch = dict(
        joined=vrow_b, stream=vrow_b, qc=vrow_b, qp=vrow_b, qs=vrow_b, k=vrow_b, v=vrow_b, mixed=vrow_b,
        midb=vrow_b, out=vrow_b, p=probs_scratch,
        pos=vm((heads // 2, 2 * rows, key_rows), F32),
        bias=vm((2, seg_rows, seg_rows), F32),
        mid_in=vrow_f, outer=vrow_f, act=wide, slope=wide,
        sem_in=dma((10,)),
        sem_first=dma((1,)),
        sem_out=dma((40,)),
        **weights_f, **weights_a,
    )
    backward_scratch = dict(
        outer=vrow_f, mid_in=vrow_f, cot=vrow_b, returned=vrow_b, e=vrow_b, ab=vrow_b, a=vrow_f, acc=vrow_f,
        u=wide, slope=wide, x=vrow_b, k=vrow_b, v=vrow_b, qc=vrow_b, qp=vrow_b, qs=vrow_b, qpf=vrow_b, dk=vrow_b,
        dv=vrow_b, dqb=vrow_b, out=vrow_b, p=probs_scratch, dq=vrow_f, dqp=vrow_f,
        drel=vm((rel_rows, width), F32),
        sums_t=vm((16, width), F32),
        sums=vm((8, width), F32),
        sem_tail=dma((1 + 3 * (ff // width),)),
        sem_first=dma((4,)),
        sem_head=dma((11,)),
        sem_out=dma((14,)),
        **weights_f, **weights_a,
    )
    return forward_scratch, backward_scratch


def shards(
    content_in, memory, mask_embed, doc_ids, orders, targets, slot_used,
    w_query, w_key, w_value, w_out, w_rel, bias_content, bias_position, bias_segment, seg_embed,
    norm1_gain, norm1_shift, ffn_in, ffn_in_bias, ffn_out, ffn_out_bias, norm2_gain, norm2_shift,
    content_cot, query_cot,
):
    slots, seg_rows, width = content_in.shape
    mem_rows = memory.shape[2]
    heads, dim = bias_content.shape[1:]
    ff = ffn_in.shape[2]
    key_rows, rows = mem_rows + seg_rows, 2 * seg_rows
    rel_rows = key_rows + seg_rows
    section = lax.axis_index(SECTION).astype(jnp.int32)
    dp = lax.axis_index(DP).astype(jnp.int32)
    dp_count = lax.axis_size(DP)
    inside = dp % GROUP
    at = jnp.where((inside // 2) % 2 == 0, inside // 4, RING - 1 - inside // 4)
    lane = jnp.arange(2 * RING + 2, dtype=jnp.int32)
    meta = jnp.where(
        lane < RING,
        (at - lane) & (RING - 1),
        jnp.where(
            lane < 2 * RING,
            (-at - lane) & (RING - 1),
            jnp.where(lane == META_CORE, dp % 2, section),
        ),
    )
    pos_b = jnp.asarray(position_table(rel_rows, width, mem_rows, seg_rows)).astype(BF16)
    small, rel = pl.pallas_call(
        prepare_body,
        out_shape=(shape(SMALL_ROWS, width, dtype=F32), shape(rel_rows, width)),
        compiler_params=params(),
    )(
        bias_content, bias_position, bias_segment,
        jnp.transpose(seg_embed[0], (1, 0, 2)), norm1_gain, norm1_shift, ffn_out_bias, norm2_gain,
        norm2_shift, mask_embed.reshape(1, width), ffn_in_bias, pos_b, w_rel,
    )

    row_b, row_f = shape(slots, rows, width), shape(slots, rows, width, dtype=F32)
    kept = dict(
        joined=row_b, stream=row_b, qc=row_b, qp=row_b, qs=row_b, k=row_b, v=row_b, mixed=row_b,
        p=shape(slots, heads, rows, key_rows),
        mid_in=row_f,
        outer=row_f,
        slope=shape(slots, rows, ff),
        me=shape(2, slots, rows, width),
        ua=shape(2, slots, rows, ff),
        content_out=shape(1, slots, seg_rows, width),
        query_out=shape(1, slots, seg_rows, width),
    )
    forward_scratch, backward_scratch = scratches(seg_rows, mem_rows, width, ff, heads)
    common = dict(meta=(SMEM_SPEC, meta), slot_used=(SMEM_SPEC, slot_used), **in_vmem(small=small))
    ids = in_vmem(docs=doc_ids, orders=orders, targets=targets)
    weights_attention = in_hbm(w_key=w_key, w_query=w_query, w_value=w_value, w_out=w_out, rel=rel)
    weights_ffn = in_hbm(ffn_in=ffn_in, ffn_out=ffn_out)
    sent = {}
    for call in range(4):
        layer, slot = call // 2, call % 2
        source = in_hbm(content_in=content_in) if layer == 0 else in_hbm(arrived=sent[slot])
        inputs = common | ids | in_hbm(memory=memory) | weights_attention | weights_ffn | source
        fresh = dict(sent=shape(rows, width)) if layer == 0 else {}
        kept, new = call_kernel(forward_body, layer, slot, inputs, kept, fresh, forward_scratch)
        if layer == 0:
            sent[slot] = lax.ppermute(new.popitem()[1], SECTION, [(0, 1)])
    kept = types.SimpleNamespace(**kept)

    grads = dict(
        me=kept.me, ua=kept.ua, ab=row_b, dk=row_b, dv=row_b, dq=row_b,
        drel=shape(slots, rel_rows, width, dtype=F32),
        input_grad=shape(1, slots, seg_rows, width),
        sums_tail=shape(slots, 16, width, dtype=F32),
        sums_head=shape(slots, 8, width, dtype=F32),
    )
    flat = lambda v: v.reshape(v.shape[:-3] + (slots * rows, v.shape[-1]))
    returned = {}
    for call in range(4):
        layer, slot = 1 - call // 2, 1 - call % 2
        inputs = common | in_vmem(docs=doc_ids) | weights_attention | weights_ffn | in_hbm(
            outer=kept.outer, slope=kept.slope, mid_in=kept.mid_in, content_cot=content_cot, query_cot=query_cot,
            p=kept.p, k=kept.k, v=kept.v, qc=kept.qc, qp=kept.qp, qs=kept.qs,
        )
        if layer == 0:
            inputs |= in_hbm(returned=returned[slot])
        fresh = dict(sent=shape(rows, width)) if layer == 1 else {}
        grads, new = call_kernel(backward_body, layer, slot, inputs, grads, fresh, backward_scratch)
        if layer == 1:
            returned[slot] = lax.ppermute(new.popitem()[1], SECTION, [(1, 0)])
    grads = types.SimpleNamespace(**grads)

    me, ua = flat(grads.me), flat(grads.ua)
    operands = [flat(v) for v in (kept.stream, kept.joined, kept.mixed, grads.dq, grads.dk, grads.dv, grads.ab)]
    operands.append(grads.drel)
    own, others = {}, {}

    def add(ring, step, came=None):
        total = own[ring, step].astype(F32) + others[ring, step].astype(F32)
        return (total if came is None else total + came.astype(F32)).astype(BF16)

    def form(first, count, meta):
        formed = pieces(first, count, meta, me, ua, operands)
        for ring in range(2):
            handed = swapped(formed[2 * ring + 1], DP, 1)
            for n in range(count):
                own[ring, first + n] = formed[2 * ring][n]
                others[ring, first + n] = handed[n]

    form(0, 1, meta)
    meta, own[0, 0] = lax.optimization_barrier((meta, own[0, 0]))
    form(1, 1, meta)
    later = {1: (2, 2), 2: (4, 2), 4: (6, 2)}
    acc = [add(0, 0), add(1, 0)]

    sums = jnp.concatenate(
        [grads.sums_head[0] + grads.sums_head[1], grads.sums_tail[0] + grads.sums_tail[1]], axis=0
    )
    row = lax.broadcasted_iota(jnp.int32, sums.shape, 0)
    sums = jnp.where((row == 5) & (section != 0), 0.0, sums)
    bits = [1 << n for n in range(dp_count.bit_length() - 1)]

    steps = ring_steps(dp_count)
    for step in range(1, RING):
        if step in later:
            meta, acc[0] = lax.optimization_barrier((meta, acc[0]))
            form(*later[step], meta)
        came = [lax.ppermute(acc[ring], DP, steps) for ring in range(2)]
        moving = swapped(sums, DP, bits.pop(0)) if bits else None
        acc = [add(ring, step, came[ring]) for ring in range(2)]
        if moving is not None:
            sums = sums + moving
            sums, acc[0] = lax.optimization_barrier((sums, acc[0]))
    for bit in bits:
        sums = sums + swapped(sums, DP, bit)
    mask_total = sums[5:6, :]
    mask_total = mask_total + swapped(mask_total, SECTION, 1)
    acc_a, acc_b = acc
    bit = GROUP
    while bit < dp_count:
        acc_a = (acc_a.astype(F32) + swapped(acc_a, DP, bit).astype(F32)).astype(BF16)
        acc_b = (acc_b.astype(F32) + swapped(acc_b, DP, bit).astype(F32)).astype(BF16)
        bit *= 2
    ffn_outs = [shape(1, width, ff, dtype=F32), shape(1, ff, width, dtype=F32)]
    rest_outs = [shape(1, width, width, dtype=F32) for _ in range(4)] + [shape(rel_rows, width, dtype=F32)]
    head_shape = shape(heads, 1, dim, dtype=F32)
    row_shape = shape(1, width, dtype=F32)
    (
        grad_bc, grad_bp, grad_bs, grad_seg, grad_n1g, grad_n1s, grad_fib, grad_fob, grad_n2g, grad_n2s, mask_grad,
    ) = pl.pallas_call(
        finish_small_body,
        out_shape=(
            head_shape, head_shape, head_shape, shape(heads, 2, dim, dtype=F32), row_shape, row_shape,
            shape(1, ff, dtype=F32), row_shape, row_shape, row_shape, row_shape,
        ),
        compiler_params=params(),
    )(sums, mask_total)
    mask_grad = mask_grad.reshape(width)
    tokens = []
    outs = ffn_outs + rest_outs
    for step in range(RING):
        before_a, before_b = [], []
        if step:
            if step > 1:
                acc_a, *before_a = lax.optimization_barrier((acc_a, tokens[step - 2]))
                acc_b, *before_b = lax.optimization_barrier((acc_b, tokens[step - 2]))
            if step == 3:
                mask_grad, acc_a = lax.optimization_barrier((mask_grad, acc_a))
            acc_a = lax.ppermute(acc_a, DP, steps)
            acc_b = lax.ppermute(acc_b, DP, steps)
        outs, token = unpack(
            step, meta, acc_a, swapped(acc_a, DP, 1), acc_b, swapped(acc_b, DP, 1), outs, before_a + before_b,
            pos_b if step == RING - 1 else None,
        )
        tokens.append(token)
    ffn_outs, rest_outs = outs[:2], outs[2:]
    grad_ffn_in, grad_ffn_out = ffn_outs
    grad_w_query, grad_w_key, grad_w_value, grad_w_out, grad_rel = rest_outs
    grad_w_rel = tokens[-1]
    one_layer = lambda v: v.reshape(1, heads, dim)
    return (
        kept.content_out, kept.query_out, grads.input_grad, mask_grad,
        grad_w_query, grad_w_key, grad_w_value, grad_w_out, grad_w_rel,
        one_layer(grad_bc), one_layer(grad_bp), one_layer(grad_bs), jnp.transpose(grad_seg, (1, 0, 2))[None],
        grad_n1g, grad_n1s, grad_ffn_in, grad_fib, grad_ffn_out, grad_fob, grad_n2g, grad_n2s,
    )


def solution(mesh):
    two, three, four = P(SECTION, None), P(SECTION, None, None), P(SECTION, None, None, None)
    rows = P(SECTION, DP, None, None)
    return jax.shard_map(
        shards,
        mesh=mesh,
        in_specs=(
            P(DP, None, None), rows, P(), P(DP, None), P(DP, None), P(DP, None), P(DP), *[three] * 8, four,
            two, two, three, two, three, two, two, two, rows, rows,
        ),
        out_specs=(
            rows, rows, rows, P(), *[three] * 8, four, two, two, three, two, three, two, two, two,
        ),
        check_vma=False,
    )
```

```python
import functools
import types

import jax
import jax.numpy as jnp
import numpy as np
from jax import lax
from jax.experimental import pallas as pl
from jax.experimental.pallas import tpu as pltpu
from jax.sharding import PartitionSpec as P

BF16 = jnp.bfloat16
F32 = jnp.float32
NEG_FILL = -1e30
NORM_EPS = 1e-05
GELU_A = 0.7978845608028654
GELU_B = 0.044715
VMEM_LIMIT = 60 * 1024 * 1024
LANES = 128
LAYER_FLOPS = 9_000_000_000
RING = 8
META_CORE, META_SECTION = 2 * RING, 2 * RING + 1

ROW_BC, ROW_BP, ROW_BS, ROW_SEG0, ROW_SEG1 = 0, 1, 2, 3, 4
ROW_N1G, ROW_N1S, ROW_FOB, ROW_N2G, ROW_N2S, ROW_MASK, ROW_FIB = 5, 6, 7, 8, 9, 10, 11
SMALL_ROWS = 16


def dot_nn(left, right):
    return jnp.dot(left, right, preferred_element_type=F32)


def dot_nt(left, right):
    return lax.dot_general(left, right, (((1,), (1,)), ((), ())), preferred_element_type=F32)


def dot_tn(left, right):
    return lax.dot_general(left, right, (((0,), (0,)), ((), ())), preferred_element_type=F32)


def col_sum(block):
    return jnp.sum(block, axis=0, keepdims=True)


def norm_parts(rows):
    center = jnp.mean(rows, axis=-1, keepdims=True)
    offset = rows - center
    spread = jnp.mean(offset * offset, axis=-1, keepdims=True)
    scale = lax.rsqrt(spread + NORM_EPS)
    return offset * scale, scale


def norm_back(grad, unit, scale, gain):
    inner = grad * gain
    mean_inner = jnp.mean(inner, axis=-1, keepdims=True)
    mean_cross = jnp.mean(inner * unit, axis=-1, keepdims=True)
    return (inner - mean_inner - unit * mean_cross) * scale


def half_masks():
    lane = lax.broadcasted_iota(jnp.int32, (1, LANES), 1)
    low = lane < LANES // 2
    return low, low.astype(F32).astype(BF16), (~low).astype(F32).astype(BF16)


def stack_heads(block, low_b, high_b):
    return jnp.concatenate([block * low_b, block * high_b], axis=0)


def copy_in(pairs, sems):
    copies = [
        pltpu.make_async_copy(src, dst, sems.at[n]) for n, (src, dst) in enumerate(pairs)
    ]
    for copy in copies:
        copy.start()
    return copies


def name_refs(names_in, names_out, names_scratch, refs):
    groups, start = [], 0
    for names in (names_in, names_out, names_scratch):
        groups.append(types.SimpleNamespace(**dict(zip(names, refs[start : start + len(names)]))))
        start += len(names)
    return groups


def forward_body(section, slot, names_in, names_out, names_scratch, *refs):
    r, o, s = name_refs(names_in, names_out, names_scratch, refs)
    meta = r.meta
    seg_rows, width = s.stream.shape[0] // 2, s.stream.shape[1]
    key_rows = s.joined.shape[0]
    pairs_count = width // LANES
    ff = s.act.shape[1]
    score_scale = 0.125

    @pl.when(meta[META_SECTION] == section)
    def _run():
        sem_in, sem_out = s.sem_in, s.sem_out
        mem_rows = key_rows - seg_rows
        x_src = r.content_in.at[slot] if section == 0 else r.arrived.at[pl.ds(0, seg_rows)]
        loads = [
            (r.memory.at[0, slot], s.joined.at[pl.ds(0, mem_rows)]),
            (x_src, s.joined.at[pl.ds(mem_rows, seg_rows)]),
            (x_src, s.stream.at[pl.ds(0, seg_rows)]),
            (r.w_key.at[0], s.wk),
            (r.w_query.at[0], s.wq),
            (r.rel, s.rel),
            (r.w_value.at[0], s.wv),
            (r.w_out.at[0], s.wo),
            (r.ffn_in.at[0], s.fi),
            (r.ffn_out.at[0], s.fo),
        ]
        moves = []
        if section == 1:
            query_rows = pl.ds(seg_rows, seg_rows)
            moves = copy_in([(r.arrived.at[query_rows], s.stream.at[query_rows])], s.sem_first)
        moves = copy_in(loads, sem_in) + moves
        stores = []

        def store(src, dst):
            copy = pltpu.make_async_copy(src, dst, sem_out.at[len(stores)])
            copy.start()
            stores.append(copy)

        small = r.small
        used = (r.slot_used[slot] > 0).astype(jnp.int32).astype(F32)
        if section == 0:
            s.stream[seg_rows:, :] = jnp.broadcast_to(
                small[ROW_MASK : ROW_MASK + 1, :], (seg_rows, width)
            ).astype(BF16)
        square = (seg_rows, seg_rows)
        doc = jnp.broadcast_to(r.docs[slot : slot + 1, :].astype(F32), square)
        order = jnp.broadcast_to(r.orders[slot : slot + 1, :].astype(F32), square)
        target = jnp.broadcast_to(r.targets[slot : slot + 1, :].astype(F32), square)
        same = doc == doc.T
        visible = same & ((target == 0.0) | (order <= order.T))
        row_id = lax.broadcasted_iota(jnp.int32, square, 0)
        col_id = lax.broadcasted_iota(jnp.int32, square, 1)
        s.bias[0] = jnp.where(visible, 0.0, NEG_FILL)
        s.bias[1] = jnp.where(visible & (row_id != col_id), 0.0, NEG_FILL)

        for n in (0, 1, 3):
            moves[n].wait()
        s.k[...] = dot_nn(s.joined[...], s.wk[...]).astype(BF16)
        store(s.k, o.k.at[slot])
        store(s.joined, o.joined.at[slot])
        moves[2].wait()
        if section == 1:
            moves[10].wait()
        store(s.stream, o.stream.at[slot])
        moves[4].wait()
        queries = dot_nn(s.stream[...], s.wq[...])
        for block, kept, row in ((s.qc, o.qc, ROW_BC), (s.qp, o.qp, ROW_BP), (s.qs, o.qs, ROW_BS)):
            with_bias = (queries + small[row : row + 1, :]).astype(BF16)
            block[...] = (with_bias.astype(F32) * score_scale).astype(BF16)
            store(block, kept.at[slot])
        moves[6].wait()
        s.v[...] = dot_nn(s.joined[...], s.wv[...]).astype(BF16)
        store(s.v, o.v.at[slot])
        moves[5].wait()

        low, low_b, high_b = half_masks()
        bias_by_stream = [s.bias[0], s.bias[1]]
        inside = col_id <= row_id
        for pair in range(pairs_count):
            sl = slice(pair * LANES, (pair + 1) * LANES)
            position = dot_nt(stack_heads(s.qp[:, sl], low_b, high_b), s.rel[:, sl])
            for part in range(4):
                base = part * seg_rows
                turned = [
                    pltpu.roll(
                        position[base : base + seg_rows, n * LANES : (n + 1) * LANES],
                        1, axis=1, stride=1, stride_axis=0,
                    )
                    for n in range(3)
                ]
                rolled = jnp.concatenate(
                    [jnp.where(inside, turned[n], turned[n + 1]) for n in range(2)], axis=1
                )
                s.pos[pair, base : base + seg_rows, :] = rolled
        for pair in range(pairs_count):
            sl = slice(pair * LANES, (pair + 1) * LANES)
            content = dot_nt(stack_heads(s.qc[:, sl], low_b, high_b), s.k[:, sl])
            segments = jnp.concatenate(
                [
                    jnp.broadcast_to(small[row : row + 1, sl].astype(BF16) * mask, (LANES, LANES))
                    for mask in (low_b, high_b)
                    for row in (ROW_SEG0, ROW_SEG1)
                ],
                axis=0,
            )
            pieces_wide = dot_nt(s.qs[:, sl], segments)
            probs_pair = []
            for head in range(2):
                probs_streams = []
                for stream in range(2):
                    base = (2 * head + stream) * seg_rows
                    rows = slice(stream * seg_rows, (stream + 1) * seg_rows)
                    same_part = pieces_wide[rows, 2 * head * LANES : (2 * head + 1) * LANES]
                    other_part = pieces_wide[rows, (2 * head + 1) * LANES : (2 * head + 2) * LANES]
                    body = content[base : base + seg_rows, :] + s.pos[pair, base : base + seg_rows, :]
                    left = body[:, :mem_rows] + other_part
                    right = body[:, mem_rows:] + jnp.where(same, same_part, other_part) + bias_by_stream[stream]
                    peak = jnp.max(jnp.maximum(left, right), axis=-1, keepdims=True)
                    left = jnp.exp(left - peak)
                    right = jnp.exp(right - peak)
                    total = jnp.sum(left + right, axis=-1, keepdims=True)
                    inverse = 1.0 / total
                    probs_streams.append(
                        jnp.concatenate([left * inverse, right * inverse], axis=1).astype(BF16)
                    )
                probs = jnp.concatenate(probs_streams, axis=0)
                s.p[2 * pair + head] = probs
                store(s.p.at[2 * pair + head], o.p.at[slot, 2 * pair + head])
                probs_pair.append(probs)
            mixed = dot_nn(
                jnp.concatenate(probs_pair, axis=1), stack_heads(s.v[:, sl], low_b, high_b)
            )
            s.mixed[:, sl] = mixed.astype(BF16)
        store(s.mixed, o.mixed.at[slot])

        moves[7].wait()
        middle_in = dot_nn(s.mixed[...], s.wo[...]) + s.stream[...].astype(F32)
        s.mid_in[...] = middle_in
        store(s.mid_in, o.mid_in.at[slot])
        unit, _ = norm_parts(middle_in)
        middle = unit * small[ROW_N1G : ROW_N1G + 1, :] + small[ROW_N1S : ROW_N1S + 1, :]
        s.midb[...] = middle.astype(BF16)
        store(s.midb, o.me.at[0, slot])
        s.outer[...] = middle + small[ROW_FOB : ROW_FOB + 1, :]
        moves[8].wait()
        moves[9].wait()
        for step in range(ff // width):
            cols = slice(step * width, (step + 1) * width)
            inner = (
                dot_nn(s.midb[...], s.fi[:, cols])
                + small[ROW_FIB + step : ROW_FIB + step + 1, :]
            )
            square_in = inner * inner
            wave = jnp.tanh(GELU_A * inner * (1.0 + GELU_B * square_in))
            half = 0.5 * (1.0 + wave)
            active = (inner * half).astype(BF16)
            slope = half + (0.5 * GELU_A) * inner * (1.0 - wave * wave) * (1.0 + 3.0 * GELU_B * square_in)
            s.act[:, cols] = active
            s.slope[:, cols] = slope.astype(BF16)
            part = pl.ds(step * width, width)
            store(s.act.at[:, part], o.ua.at[1, slot, :, part])
            store(s.slope.at[:, part], o.slope.at[slot, :, part])
            s.outer[...] += dot_nn(active, s.fo[cols, :])
        store(s.outer, o.outer.at[slot])
        unit, _ = norm_parts(s.outer[...])
        result = unit * small[ROW_N2G : ROW_N2G + 1, :] + small[ROW_N2S : ROW_N2S + 1, :]
        s.out[...] = (result * used).astype(BF16)
        store(s.out.at[pl.ds(0, seg_rows)], o.content_out.at[0, slot])
        store(s.out.at[pl.ds(seg_rows, seg_rows)], o.query_out.at[0, slot])
        if section == 0:
            store(s.out, o.sent)
        for copy in stores:
            copy.wait()


def backward_body(section, slot, names_in, names_out, names_scratch, *refs):
    r, o, s = name_refs(names_in, names_out, names_scratch, refs)
    meta = r.meta
    rows, width = s.a.shape
    seg_rows = rows // 2
    ff = s.slope.shape[1]
    key_rows = s.k.shape[0]
    mem_rows = key_rows - seg_rows
    pairs_count = width // LANES
    score_scale = 0.125

    @pl.when(meta[META_SECTION] == section)
    def _run():
        first_loads = [
            (r.content_cot.at[0, slot], s.cot.at[pl.ds(0, seg_rows)]),
            (r.query_cot.at[0, slot], s.cot.at[pl.ds(seg_rows, seg_rows)]),
            (r.outer.at[slot], s.outer),
        ]
        if section == 0:
            first_loads.append((r.returned, s.returned))
        first = copy_in(first_loads, s.sem_first)
        loads = []
        for step in range(ff // width):
            part = pl.ds(step * width, width)
            loads.append((r.ffn_out.at[0, part], s.fo.at[part]))
            loads.append((r.slope.at[slot, :, part], s.slope.at[:, part]))
            loads.append((r.ffn_in.at[0, :, part], s.fi.at[:, part]))
        loads.append((r.mid_in.at[slot], s.mid_in))
        head_loads = [
            (r.w_out.at[0], s.wo),
            (r.v.at[slot], s.v),
            (r.p.at[slot], s.p),
            (r.k.at[slot], s.k),
            (r.qc.at[slot], s.qc),
            (r.qp.at[slot], s.qp),
            (r.qs.at[slot], s.qs),
            (r.rel, s.rel),
            (r.w_query.at[0], s.wq),
            (r.w_key.at[0], s.wk),
            (r.w_value.at[0], s.wv),
        ]
        stores = []

        def store(src, dst):
            copy = pltpu.make_async_copy(src, dst, s.sem_out.at[len(stores)])
            copy.start()
            stores.append(copy)

        small = r.small
        used = (r.slot_used[slot] > 0).astype(jnp.int32).astype(F32)
        for move in first:
            move.wait()
        moves = copy_in(loads, s.sem_tail)
        grad = s.cot[...].astype(F32) * used
        if section == 0:
            grad = grad + s.returned[...].astype(F32)
        unit, scale = norm_parts(s.outer[...])
        out = s.sums_t
        out[...] = jnp.zeros_like(out)
        out[4:5, :] = col_sum(grad * unit)
        out[5:6, :] = col_sum(grad)
        grad_outer = norm_back(grad, unit, scale, small[ROW_N2G : ROW_N2G + 1, :])
        s.e[...] = grad_outer.astype(BF16)
        store(s.e, o.me.at[1, slot])
        out[3:4, :] = col_sum(s.e[...].astype(F32))
        s.acc[...] = grad_outer
        for step in range(ff // width):
            for move in moves[3 * step : 3 * step + 3]:
                move.wait()
            cols = slice(step * width, (step + 1) * width)
            if step == 1:
                head_moves = copy_in(head_loads, s.sem_head)
            grad_active = dot_nt(s.e[...], s.fo[cols, :])
            inner_b = (s.slope[:, cols].astype(F32) * grad_active).astype(BF16)
            s.u[:, cols] = inner_b
            out[8 + step : 9 + step, :] = col_sum(inner_b.astype(F32))
            s.acc[...] += dot_nt(inner_b, s.fi[:, cols])
        store(s.u, o.ua.at[0, slot])
        moves[-1].wait()
        unit, scale = norm_parts(s.mid_in[...])
        grad = s.acc[...]
        out[1:2, :] = col_sum(grad * unit)
        out[2:3, :] = col_sum(grad)
        s.a[...] = norm_back(grad, unit, scale, small[ROW_N1G : ROW_N1G + 1, :])
        s.ab[...] = s.a[...].astype(BF16)
        store(s.ab, o.ab.at[slot])
        store(s.sums_t, o.sums.at[slot, pl.ds(8, 16)])

        square = (seg_rows, seg_rows)
        doc = jnp.broadcast_to(r.docs[slot : slot + 1, :].astype(F32), square)
        same_one = (doc == doc.T).astype(F32)
        same = jnp.concatenate([same_one, same_one], axis=0)
        flip_rows = lax.broadcasted_iota(jnp.int32, (rows, rows), 0)
        flip_cols = lax.broadcasted_iota(jnp.int32, (rows, rows), 1)
        flipped_to = jnp.where(flip_rows < seg_rows, seg_rows - 1, rows + seg_rows - 1) - flip_rows
        flip = (flip_cols == flipped_to).astype(F32).astype(BF16)
        out = s.sums
        out[...] = jnp.zeros_like(out)
        head_moves[0].wait()
        s.x[...] = dot_nt(s.ab[...], s.wo[...]).astype(BF16)
        for n in (1, 2, 3, 4, 5, 6, 7):
            head_moves[n].wait()
        s.qpf[...] = dot_nn(flip, s.qp[...]).astype(BF16)

        low, low_b, high_b = half_masks()
        past = lax.broadcasted_iota(jnp.int32, square, 1) >= lax.broadcasted_iota(jnp.int32, square, 0)
        for pair in range(pairs_count):
            sl = slice(pair * LANES, (pair + 1) * LANES)
            grads_mixed = stack_heads(s.x[:, sl], low_b, high_b)
            grad_probs = dot_nt(grads_mixed, s.v[:, sl])
            scores_b = []
            same_sums, other_sums = [], []
            for head in range(2):
                probs = s.p[2 * pair + head].astype(F32)
                product = probs * grad_probs[head * rows : (head + 1) * rows, :]
                delta = jnp.sum(product, axis=-1, keepdims=True)
                rounded = (product - probs * delta).astype(BF16)
                scores_b.append(rounded)
                wide = rounded.astype(F32)
                right = wide[:, mem_rows:] * same
                same_sum = jnp.sum(right, axis=-1, keepdims=True)
                same_sums.append(same_sum)
                other_sums.append(
                    jnp.sum(wide[:, :mem_rows] + (wide[:, mem_rows:] - right), axis=-1, keepdims=True)
                )
            stacked = jnp.concatenate(scores_b, axis=0)
            beside = jnp.concatenate(scores_b, axis=1)
            probs_stacked = jnp.concatenate([s.p[2 * pair], s.p[2 * pair + 1]], axis=0)
            s.dv[:, sl] = dot_tn(probs_stacked, grads_mixed).astype(BF16)
            s.dk[:, sl] = dot_tn(stacked, stack_heads(s.qc[:, sl], low_b, high_b)).astype(BF16)
            grad_content = dot_nn(beside, stack_heads(s.k[:, sl], low_b, high_b)) * score_scale
            same_sel = jnp.where(low, same_sums[0], same_sums[1])
            other_sel = jnp.where(low, other_sums[0], other_sums[1])
            seg0 = small[ROW_SEG0 : ROW_SEG0 + 1, sl]
            seg1 = small[ROW_SEG1 : ROW_SEG1 + 1, sl]
            grad_segment = (same_sel * seg0 + other_sel * seg1) * score_scale
            qs = s.qs[:, sl].astype(F32)
            out[0:1, sl] = col_sum(grad_content)
            out[2:3, sl] = col_sum(grad_segment)
            out[3:4, sl] = col_sum(same_sel * qs)
            out[4:5, sl] = col_sum(other_sel * qs)
            s.dq[:, sl] = grad_content + grad_segment
            turned = dot_nn(flip, beside)
            shifted_heads = []
            for head in range(2):
                parts = []
                for stream in range(2):
                    blocks = [
                        pltpu.roll(
                            turned[
                                stream * seg_rows : (stream + 1) * seg_rows,
                                head * key_rows + n * LANES : head * key_rows + (n + 1) * LANES,
                            ],
                            0, axis=1, stride=1, stride_axis=0,
                        )
                        for n in range(2)
                    ]
                    blocks = [
                        jnp.where(past, blocks[0], 0.0),
                        jnp.where(past, blocks[1], blocks[0]),
                        jnp.where(past, 0.0, blocks[1]),
                    ]
                    parts.append(jnp.concatenate(blocks, axis=1).astype(BF16))
                shifted_heads.append(jnp.concatenate(parts, axis=0))
            grad_position = (
                dot_nn(
                    jnp.concatenate(shifted_heads, axis=1),
                    stack_heads(s.rel[:, sl], low_b, high_b),
                )
                * score_scale
            )
            out[1:2, sl] = col_sum(grad_position)
            s.dqp[:, sl] = grad_position
            s.drel[:, sl] = dot_tn(
                jnp.concatenate(shifted_heads, axis=0),
                stack_heads(s.qpf[:, sl], low_b, high_b),
            )
        store(s.dk, o.dk.at[slot])
        store(s.dv, o.dv.at[slot])
        store(s.drel, o.drel.at[slot])
        grad_position = s.dqp[...]
        position_high = grad_position.astype(BF16)
        position_low = (grad_position - position_high.astype(F32)).astype(BF16)
        grad_queries = s.dq[...] + dot_nn(flip, position_high) + dot_nn(flip, position_low)
        s.dqb[...] = grad_queries.astype(BF16)
        store(s.dqb, o.dq.at[slot])
        for n in (8, 9, 10):
            head_moves[n].wait()
        grad_rows = s.a[...] + dot_nt(s.dqb[...], s.wq[...])
        grad_content = (
            grad_rows[:seg_rows, :]
            + dot_nt(s.dk[mem_rows:, :], s.wk[...])
            + dot_nt(s.dv[mem_rows:, :], s.wv[...])
        )
        grad_query = grad_rows[seg_rows:, :]
        s.out[:seg_rows, :] = grad_content.astype(BF16)
        s.out[seg_rows:, :] = grad_query.astype(BF16)
        store(s.out.at[pl.ds(0, seg_rows)], o.input_grad.at[0, slot])
        if section == 1:
            store(s.out, o.sent)
        if section == 0:
            out[5:6, :] = col_sum(grad_query)
        store(s.sums, o.sums.at[slot, pl.ds(0, 8)])
        for copy in stores:
            copy.wait()


ANY_SPEC = pl.BlockSpec(memory_space=pltpu.HBM)
SMEM_SPEC = pl.BlockSpec(memory_space=pltpu.SMEM)
VMEM_SPEC = pl.BlockSpec(memory_space=pltpu.VMEM)


def call_kernel(body, section, slot, inputs, carried, fresh, scratch):
    names_in = list(inputs)
    arrays = [inputs[n][1] for n in names_in]
    specs = [inputs[n][0] for n in names_in]
    aliases = {}
    names_out = list(carried) + list(fresh)
    out_shapes = []
    for position, key in enumerate(carried):
        value = carried[key]
        out_shapes.append(jax.ShapeDtypeStruct(value.shape, value.dtype))
        if not isinstance(value, jax.ShapeDtypeStruct):
            aliases[len(arrays)] = position
            arrays.append(value)
            specs.append(ANY_SPEC)
            names_in.append(key + "_")
    out_shapes += [fresh[key] for key in fresh]
    results = pl.pallas_call(
        functools.partial(body, section, slot, names_in, names_out, list(scratch)),
        out_shape=tuple(out_shapes),
        in_specs=specs,
        out_specs=tuple(ANY_SPEC for _ in out_shapes),
        scratch_shapes=list(scratch.values()),
        input_output_aliases=aliases,
        compiler_params=pltpu.CompilerParams(vmem_limit_bytes=VMEM_LIMIT),
        cost_estimate=pl.CostEstimate(flops=LAYER_FLOPS, bytes_accessed=20_000_000, transcendentals=0),
    )(*arrays)
    named = dict(zip(names_out, results))
    return {k: named[k] for k in carried}, {k: named[k] for k in fresh}


def in_hbm(**arrays):
    return {key: (ANY_SPEC, value) for key, value in arrays.items()}


def in_vmem(**arrays):
    return {key: (VMEM_SPEC, value) for key, value in arrays.items()}


def params():
    return pltpu.CompilerParams(vmem_limit_bytes=VMEM_LIMIT)


def cost(flops, moved):
    return pl.CostEstimate(flops=flops, bytes_accessed=moved, transcendentals=0)


def shape(*dims, dtype=BF16):
    return jax.ShapeDtypeStruct(dims, dtype)


def prepare_body(bc, bp, bs, seg, n1g, n1s, fob, n2g, n2s, mask, fib, pos, w_rel, small, rel):
    heads, dim = bc.shape[1:]
    width = heads * dim
    wide = [(row, value[0].astype(F32)) for row, value in ((ROW_BC, bc), (ROW_BP, bp), (ROW_BS, bs))]
    for head in range(heads):
        cols = slice(head * dim, (head + 1) * dim)
        for row, value in wide:
            small[row : row + 1, cols] = value[head : head + 1, :]
        small[ROW_SEG0 : ROW_SEG1 + 1, cols] = seg[head].astype(F32)
    for row, value in (
        (ROW_N1G, n1g), (ROW_N1S, n1s), (ROW_FOB, fob), (ROW_N2G, n2g), (ROW_N2S, n2s),
    ):
        small[row : row + 1, :] = value[...].astype(F32)
    small[ROW_MASK : ROW_MASK + 1, :] = mask[...].astype(F32).reshape(1, width)
    for step in range(4):
        small[ROW_FIB + step : ROW_FIB + step + 1, :] = fib[:, step * width : (step + 1) * width].astype(F32)
    small[SMALL_ROWS - 1 : SMALL_ROWS, :] = jnp.zeros((1, width), F32)
    rel[...] = dot_nn(pos[...], w_rel[0]).astype(BF16)


GROUP = 16
SUM_ROWS = 24
MASK_ROW = 5
HALF = 384
HEAD_ROWS = 320
REST_ROWS = HALF - HEAD_ROWS
REL_PIECE = 24
BLOCK = slice(REST_ROWS, REST_ROWS + HALF // 2)
REL = slice(BLOCK.stop, BLOCK.stop + REL_PIECE)
B_ROWS = BLOCK.stop + 32


def lane_slice(start, size):
    return pl.ds(pl.multiple_of(start, LANES), size)


def block_rows(index, size):
    return pl.ds(pl.multiple_of(index * size, size), size)


def piece_body(first, count, meta, me, ua, stream, joined, mixed, dq, dk, dv, ab, drel, sums, *refs):
    own_a, other_a, own_b, other_b = refs[:4]
    low_l, low_r, high_l, high_r, left, right, rel, stage_a, stage_b, small, sems, out_sems = refs[4:]
    core = meta[META_CORE]
    width = low_r.shape[2]

    def start(src, dst, sem):
        copy = pltpu.make_async_copy(src, dst, sem)
        copy.start()
        return copy

    def rel_rows(at):
        return drel.at[:, pl.ds(pl.multiple_of(at * REL_PIECE, 8), REL_PIECE), :]

    def fetch(at, early, late, to_left, to_right, sem):
        inside = at % 4
        rows_at, cols_at = block_rows(inside // 2, HALF), block_rows(inside % 2, HALF)

        @pl.when(at < RING // 2)
        def _early():
            start(early[0].at[:, rows_at], to_left, sem[0])
            start(early[1].at[:, cols_at], to_right, sem[1])

        @pl.when(at >= RING // 2)
        def _late():
            start(late[0].at[:, rows_at], to_left, sem[0])
            start(late[1].at[:, cols_at], to_right, sem[1])

        return [
            pltpu.make_async_copy(early[0].at[:, rows_at], to_left, sem[0]),
            pltpu.make_async_copy(early[1].at[:, cols_at], to_right, sem[1]),
        ]

    moves = [start(me.at[1], high_r, sems.at[10 * count]), start(sums, small, sems.at[10 * count + 1])]
    steps = []
    for n in range(count):
        low_at, high_at = meta[first + n], meta[RING + first + n]
        sem = [sems.at[10 * n + k] for k in range(10)]
        low_moves = [
            start(me.at[0, :, block_rows(low_at % 2, HALF)], low_l.at[n], sem[0]),
            start(ua.at[0, :, block_rows(low_at // 2, width)], low_r.at[n], sem[1]),
        ]
        high_moves = [start(ua.at[1, :, block_rows(high_at, HALF)], high_l.at[n], sem[2])]
        low_rest = fetch(low_at, (stream, dq), (joined, dk), left.at[n, 0], right.at[n, 0], sem[4:6])
        high_rest = fetch(high_at, (joined, dv), (mixed, ab), left.at[n, 1], right.at[n, 1], sem[6:8])
        low_rest.append(start(rel_rows(low_at), rel.at[n, 0], sem[8]))
        high_rest.append(start(rel_rows(RING + high_at), rel.at[n, 1], sem[9]))
        steps.append((low_moves, high_moves + moves, low_rest, high_rest, 2 * low_at, 2 * high_at + 1))
        moves = []
    writes = []
    for n, (low_moves, high_moves, low_rest, high_rest, low_row, high_row) in enumerate(steps):
        for waits, lhs, rhs, place in (
            (low_moves, low_l.at[n], low_r.at[n], core), (high_moves, high_l.at[n], high_r, 1 - core),
        ):
            for move in waits:
                move.wait()
            whole = dot_tn(lhs[...], rhs[...]).astype(BF16)
            stage_a[n, place] = whole[:HEAD_ROWS]
            stage_b[n, place, :REST_ROWS] = whole[HEAD_ROWS:]
        writes.append(start(stage_a.at[n, 1], other_a.at[n], out_sems.at[4 * n]))
        writes.append(start(stage_a.at[n, 0], own_a.at[n], out_sems.at[4 * n + 1]))
        for waits, half, place, row in ((low_rest, 0, core, low_row), (high_rest, 1, 1 - core, high_row)):
            for move in waits:
                move.wait()
            value = dot_tn(left[n, half], right[n, half]).astype(BF16)
            stage_b[n, place, BLOCK.start : BLOCK.stop, :HALF] = value[: HALF // 2]
            stage_b[n, place, BLOCK.start : BLOCK.stop, HALF:] = value[HALF // 2 :]
            rows = [
                small[0, pl.ds(at, 1), :] + small[1, pl.ds(at, 1), :]
                for at in (row, jnp.minimum(row + 2 * RING, SUM_ROWS - 1))
            ]
            blank = jnp.zeros((B_ROWS - REL.stop - 2, width), F32)
            stage_b[n, place, BLOCK.stop :] = jnp.concatenate(
                [rel[n, half, 0] + rel[n, half, 1], *rows, blank], axis=0
            ).astype(BF16)
        writes.append(start(stage_b.at[n, 1], other_b.at[n], out_sems.at[4 * n + 2]))
        writes.append(start(stage_b.at[n, 0], own_b.at[n], out_sems.at[4 * n + 3]))
    for copy in writes:
        copy.wait()


def pieces(first, count, meta, me, ua, operands):
    rows, width = operands[0].shape

    def vm(*dims, dtype=BF16):
        return pltpu.VMEM((count, *dims), dtype)

    return pl.pallas_call(
        functools.partial(piece_body, first, count),
        out_shape=[shape(count, size, width) for size in (HEAD_ROWS, HEAD_ROWS, B_ROWS, B_ROWS)],
        in_specs=[SMEM_SPEC] + [ANY_SPEC] * (2 + len(operands)),
        out_specs=[ANY_SPEC] * 4,
        scratch_shapes=[
            vm(rows, HALF), vm(rows, width), vm(rows, HALF), pltpu.VMEM((rows, width), BF16),
            vm(2, rows, HALF), vm(2, rows, HALF), vm(2, 2, REL_PIECE, width, dtype=F32),
            vm(2, HEAD_ROWS, width), vm(2, B_ROWS, width), pltpu.VMEM(operands[-1].shape, F32),
            pltpu.SemaphoreType.DMA((10 * count + 2,)), pltpu.SemaphoreType.DMA((4 * count,)),
        ],
        compiler_params=params(),
        cost_estimate=cost(6 * rows * HALF * width * count, 4_000_000 * count),
    )(meta, me, ua, *operands)


def by_core(meta, own, other, low_f, high_f):
    low = meta[META_CORE] == 0

    @pl.when(low)
    def _low():
        low_f[...] = own[...].astype(F32)
        high_f[...] = other[...].astype(F32)

    @pl.when(~low)
    def _high():
        low_f[...] = other[...].astype(F32)
        high_f[...] = own[...].astype(F32)


def ffn_places(fi, fo, low_at, high_at, first, count):
    width = fo.shape[2]
    return (
        fi.at[0, pl.ds(pl.multiple_of((low_at % 2) * HALF + first, 8), count), lane_slice((low_at // 2) * width, width)],
        fo.at[0, pl.ds(pl.multiple_of(high_at * HALF + first, 8), count), :],
    )


def finish_small(gathered, bc, bp, bs, seg, n1g, n1s, fib, fob, n2g, n2s, mask_out):
    def row(at):
        place = 8 * (at % (2 * RING)) + at // (2 * RING)
        return gathered[place : place + 1, :]

    heads, dim = bc.shape[0], bc.shape[2]
    width = heads * dim
    rows = [row(at) for at in range(5)]
    for head in range(heads):
        cols = slice(head * dim, (head + 1) * dim)
        bc[head] = rows[0][:, cols]
        bp[head] = rows[1][:, cols]
        bs[head] = rows[2][:, cols]
        seg[head, 0:1, :] = rows[3][:, cols]
        seg[head, 1:2, :] = rows[4][:, cols]
    mask_out[...] = row(MASK_ROW).reshape(width)
    for out, at in ((n1g, 9), (n1s, 10), (fob, 11), (n2g, 12), (n2s, 13)):
        out[...] = row(at)
    for step in range(4):
        fib[:, step * width : (step + 1) * width] = row(16 + step)


def unpack_body(step, last, meta, own_a, other_a, own_b, other_b, *refs):
    if last:
        pos, rel_in, small_in = refs[0], refs[7], refs[8]
        *small_outs, low_a, high_a, low_f, high_f, sems, rel_all, small_all, rel_sem = refs[-19:]
        fi, fo, wq, wk, wv, wo, rel, small, w_rel = refs[-28:-19]
        rel_copies = [
            pltpu.make_async_copy(rel_in, rel_all, rel_sem.at[0]),
            pltpu.make_async_copy(small_in, small_all, rel_sem.at[1]),
        ]
        for copy in rel_copies:
            copy.start()
    else:
        fi, fo, wq, wk, wv, wo, rel, small, token, low_a, high_a, low_f, high_f, sems = refs[-14:]
        token[...] = jnp.zeros_like(token)
    low_at, high_at = meta[step], meta[RING + step]
    by_core(meta, own_a, other_a, low_a, high_a)
    low_to, high_to = ffn_places(fi, fo, low_at, high_at, 0, HEAD_ROWS)
    copies = [
        pltpu.make_async_copy(low_a, low_to, sems.at[8]),
        pltpu.make_async_copy(high_a, high_to, sems.at[9]),
    ]
    for copy in copies:
        copy.start()
    by_core(meta, own_b, other_b, low_f, high_f)
    low_to, high_to = ffn_places(fi, fo, low_at, high_at, HEAD_ROWS, REST_ROWS)
    rest = pl.ds(0, REST_ROWS)
    rel_part = pl.ds(REL.start, REL_PIECE)

    def rel_to(at):
        return rel.at[pl.ds(pl.multiple_of(at * REL_PIECE, 8), REL_PIECE), :]

    later = [
        pltpu.make_async_copy(low_f.at[rest], low_to, sems.at[0]),
        pltpu.make_async_copy(high_f.at[rest], high_to, sems.at[1]),
    ]
    blocks = ((low_f, low_at, 2 * low_at, 0), (high_f, RING + high_at, 2 * high_at + 1, 1))
    small_part = pl.ds(REL.stop, 8)
    if not last:
        for src, at, row, n in blocks:
            later.append(pltpu.make_async_copy(src.at[rel_part], rel_to(at), sems.at[2 + n]))
            later.append(
                pltpu.make_async_copy(src.at[small_part], small.at[pl.ds(pl.multiple_of(8 * row, 8), 8), :], sems.at[10 + n])
            )
    for copy in later:
        copy.start()

    def block_copies(src, at, dst, sem):
        inside = at % 4
        return [
            pltpu.make_async_copy(
                src.at[pl.ds(BLOCK.start, HALF // 2), pl.ds(part * HALF, HALF)],
                dst.at[
                    0,
                    pl.ds(pl.multiple_of((inside // 2) * HALF + part * (HALF // 2), 8), HALF // 2),
                    lane_slice((inside % 2) * HALF, HALF),
                ],
                sems.at[sem + part],
            )
            for part in range(2)
        ]

    for src, at, early, late, n in ((low_f, low_at, wq, wk, 4), (high_f, high_at, wv, wo, 6)):

        @pl.when(at < RING // 2)
        def _early(src=src, at=at, early=early, n=n):
            for copy in block_copies(src, at, early, n):
                copy.start()

        @pl.when(at >= RING // 2)
        def _late(src=src, at=at, late=late, n=n):
            for copy in block_copies(src, at, late, n):
                copy.start()

        later += block_copies(src, at, early, n)
    if last:
        for copy in rel_copies:
            copy.wait()
        for src, at, row, _ in blocks:
            rel_all[pl.ds(pl.multiple_of(at * REL_PIECE, 8), REL_PIECE), :] = src[REL, :]
            small_all[pl.ds(pl.multiple_of(8 * row, 8), 8), :] = src[REL.stop :, :]
        w_rel[0] = dot_tn(pos[...], rel_all[...].astype(BF16))
        finish_small(small_all, *small_outs)
    for copy in copies + later:
        copy.wait()


def unpack(step, meta, own_a, other_a, own_b, other_b, outs, earlier, pos, heads):
    given = [v for v in outs if not isinstance(v, jax.ShapeDtypeStruct)]
    width, ff = own_a.shape[1], outs[0].shape[2]
    last = pos is not None

    def f32(*dims):
        return shape(*dims, dtype=F32)

    extra = [f32(8, LANES)]
    scratch = [
        *[pltpu.VMEM((HEAD_ROWS, width), F32)] * 2,
        *[pltpu.VMEM((B_ROWS, width), F32)] * 2,
        pltpu.SemaphoreType.DMA((12,)),
    ]
    if last:
        by_head, line = f32(heads, 1, width // heads), f32(1, width)
        extra = [
            f32(1, width, width), by_head, by_head, by_head, f32(heads, 2, width // heads), line, line, f32(1, ff),
            line, line, line, f32(width),
        ]
        scratch += [
            pltpu.VMEM(pos.shape, F32), pltpu.VMEM((16 * RING, width), F32), pltpu.SemaphoreType.DMA((2,)),
        ]
    front = [meta, own_a, other_a, own_b, other_b] + ([pos] if last else [])
    results = pl.pallas_call(
        functools.partial(unpack_body, (step + RING - 1) % RING, last),
        out_shape=tuple(shape(*v.shape, dtype=v.dtype) for v in outs) + tuple(extra),
        in_specs=[SMEM_SPEC] + [VMEM_SPEC] * (len(front) - 1) + [ANY_SPEC] * (len(given) + len(earlier)),
        out_specs=tuple(ANY_SPEC for _ in outs) + (VMEM_SPEC,) * len(extra),
        input_output_aliases={len(front) + n: n for n in range(len(given))},
        scratch_shapes=scratch,
        compiler_params=params(),
        cost_estimate=cost(0, 8_000_000),
    )(*front, *given, *earlier)
    results, token = results[: len(outs)], results[len(outs) :]
    if not last:
        token = token[0]
    return results, token


def ring_steps(count):
    cycle = [(z, 0) for z in range(4)] + [(z, 1) for z in (3, 2, 1, 0)]
    steps = []
    for index in range(count):
        base, inside = index - index % GROUP, index % GROUP
        at = cycle.index((inside // 4, (inside // 2) % 2))
        z, y = cycle[(at + (1 if inside % 2 == 0 else -1)) % RING]
        steps.append((index, base + (z * 2 + y) * 2 + inside % 2))
    return steps


SECTION, DP = "section", "dp"


def swapped(value, axis, bit):
    count = lax.axis_size(axis)
    return lax.ppermute(value, axis, [(index, index ^ bit) for index in range(count)])


def position_table(total_rows, width_model, mem_rows, seg_rows):
    row_ids = np.arange(total_rows, dtype=np.float32)
    distance = np.float32(mem_rows + seg_rows - 1) - row_ids
    power = np.arange(0, width_model, 2, dtype=np.float32) / np.float32(width_model)
    freqs = np.float32(1.0) / np.power(np.float32(10000.0), power)
    angles = distance[:, None] * freqs[None, :]
    return np.concatenate([np.sin(angles), np.cos(angles)], axis=1).astype(np.float32)


def scratches(seg_rows, mem_rows, width, ff, heads):
    rows, key_rows, rel_rows = 2 * seg_rows, mem_rows + seg_rows, mem_rows + 2 * seg_rows
    vm, dma = pltpu.VMEM, pltpu.SemaphoreType.DMA
    vrow_b, vrow_f, square, wide = vm((rows, width), BF16), vm((rows, width), F32), vm((width, width), BF16), vm((rows, ff), BF16)
    weights_f = dict(fi=vm((width, ff), BF16), fo=vm((ff, width), BF16))
    weights_a = dict(wk=square, wq=square, wv=square, wo=square, rel=vm((rel_rows, width), BF16))
    probs_scratch = vm((heads, rows, key_rows), BF16)
    forward_scratch = dict(
        joined=vrow_b, stream=vrow_b, qc=vrow_b, qp=vrow_b, qs=vrow_b, k=vrow_b, v=vrow_b, mixed=vrow_b,
        midb=vrow_b, out=vrow_b, p=probs_scratch,
        pos=vm((heads // 2, 2 * rows, key_rows), F32),
        bias=vm((2, seg_rows, seg_rows), F32),
        mid_in=vrow_f, outer=vrow_f, act=wide, slope=wide,
        sem_in=dma((10,)),
        sem_first=dma((1,)),
        sem_out=dma((40,)),
        **weights_f, **weights_a,
    )
    backward_scratch = dict(
        outer=vrow_f, mid_in=vrow_f, cot=vrow_b, returned=vrow_b, e=vrow_b, ab=vrow_b, a=vrow_f, acc=vrow_f,
        u=wide, slope=wide, x=vrow_b, k=vrow_b, v=vrow_b, qc=vrow_b, qp=vrow_b, qs=vrow_b, qpf=vrow_b, dk=vrow_b,
        dv=vrow_b, dqb=vrow_b, out=vrow_b, p=probs_scratch, dq=vrow_f, dqp=vrow_f,
        drel=vm((rel_rows, width), F32),
        sums_t=vm((16, width), F32),
        sums=vm((8, width), F32),
        sem_tail=dma((1 + 3 * (ff // width),)),
        sem_first=dma((4,)),
        sem_head=dma((11,)),
        sem_out=dma((14,)),
        **weights_f, **weights_a,
    )
    return forward_scratch, backward_scratch


def shards(
    content_in, memory, mask_embed, doc_ids, orders, targets, slot_used,
    w_query, w_key, w_value, w_out, w_rel, bias_content, bias_position, bias_segment, seg_embed,
    norm1_gain, norm1_shift, ffn_in, ffn_in_bias, ffn_out, ffn_out_bias, norm2_gain, norm2_shift,
    content_cot, query_cot,
):
    slots, seg_rows, width = content_in.shape
    mem_rows = memory.shape[2]
    heads, dim = bias_content.shape[1:]
    ff = ffn_in.shape[2]
    key_rows, rows = mem_rows + seg_rows, 2 * seg_rows
    rel_rows = key_rows + seg_rows
    section = lax.axis_index(SECTION).astype(jnp.int32)
    dp = lax.axis_index(DP).astype(jnp.int32)
    dp_count = lax.axis_size(DP)
    inside = dp % GROUP
    at = jnp.where((inside // 2) % 2 == 0, inside // 4, RING - 1 - inside // 4)
    lane = jnp.arange(2 * RING + 2, dtype=jnp.int32)
    meta = jnp.where(
        lane < RING,
        (at - lane) & (RING - 1),
        jnp.where(
            lane < 2 * RING,
            (-at - lane) & (RING - 1),
            jnp.where(lane == META_CORE, dp % 2, section),
        ),
    )
    pos_b = jnp.asarray(position_table(rel_rows, width, mem_rows, seg_rows)).astype(BF16)
    small, rel = pl.pallas_call(
        prepare_body,
        out_shape=(shape(SMALL_ROWS, width, dtype=F32), shape(rel_rows, width)),
        compiler_params=params(),
    )(
        bias_content, bias_position, bias_segment,
        jnp.transpose(seg_embed[0], (1, 0, 2)), norm1_gain, norm1_shift, ffn_out_bias, norm2_gain,
        norm2_shift, mask_embed, ffn_in_bias, pos_b, w_rel,
    )

    row_b, row_f = shape(slots, rows, width), shape(slots, rows, width, dtype=F32)
    kept = dict(
        joined=row_b, stream=row_b, qc=row_b, qp=row_b, qs=row_b, k=row_b, v=row_b, mixed=row_b,
        p=shape(slots, heads, rows, key_rows),
        mid_in=row_f,
        outer=row_f,
        slope=shape(slots, rows, ff),
        me=shape(2, slots, rows, width),
        ua=shape(2, slots, rows, ff),
        content_out=shape(1, slots, seg_rows, width),
        query_out=shape(1, slots, seg_rows, width),
    )
    forward_scratch, backward_scratch = scratches(seg_rows, mem_rows, width, ff, heads)
    common = dict(meta=(SMEM_SPEC, meta), slot_used=(SMEM_SPEC, slot_used), **in_vmem(small=small))
    ids = in_vmem(docs=doc_ids, orders=orders, targets=targets)
    weights_attention = in_hbm(w_key=w_key, w_query=w_query, w_value=w_value, w_out=w_out, rel=rel)
    weights_ffn = in_hbm(ffn_in=ffn_in, ffn_out=ffn_out)
    sent = {}
    for call in range(4):
        layer, slot = call // 2, call % 2
        source = in_hbm(content_in=content_in) if layer == 0 else in_hbm(arrived=sent[slot])
        inputs = common | ids | in_hbm(memory=memory) | weights_attention | weights_ffn | source
        fresh = dict(sent=shape(rows, width)) if layer == 0 else {}
        kept, new = call_kernel(forward_body, layer, slot, inputs, kept, fresh, forward_scratch)
        if layer == 0:
            sent[slot] = lax.ppermute(new.popitem()[1], SECTION, [(0, 1)])
    kept = types.SimpleNamespace(**kept)

    grads = dict(
        me=kept.me, ua=kept.ua, ab=row_b, dk=row_b, dv=row_b, dq=row_b,
        drel=shape(slots, rel_rows, width, dtype=F32),
        input_grad=shape(1, slots, seg_rows, width),
        sums=shape(slots, SUM_ROWS, width, dtype=F32),
    )
    flat = lambda v: v.reshape(v.shape[:-3] + (slots * rows, v.shape[-1]))
    returned = {}
    for call in range(4):
        layer, slot = 1 - call // 2, 1 - call % 2
        inputs = common | in_vmem(docs=doc_ids) | weights_attention | weights_ffn | in_hbm(
            outer=kept.outer, slope=kept.slope, mid_in=kept.mid_in, content_cot=content_cot, query_cot=query_cot,
            p=kept.p, k=kept.k, v=kept.v, qc=kept.qc, qp=kept.qp, qs=kept.qs,
        )
        if layer == 0:
            inputs |= in_hbm(returned=returned[slot])
        fresh = dict(sent=shape(rows, width)) if layer == 1 else {}
        grads, new = call_kernel(backward_body, layer, slot, inputs, grads, fresh, backward_scratch)
        if layer == 1:
            returned[slot] = lax.ppermute(new.popitem()[1], SECTION, [(1, 0)])
    grads = types.SimpleNamespace(**grads)

    me, ua = flat(grads.me), flat(grads.ua)
    operands = [flat(v) for v in (kept.stream, kept.joined, kept.mixed, grads.dq, grads.dk, grads.dv, grads.ab)]
    operands += [grads.drel, grads.sums]
    own, others = {}, {}

    def add(ring, step, came=None):
        total = own[ring, step].astype(F32) + others[ring, step].astype(F32)
        return (total if came is None else total + came.astype(F32)).astype(BF16)

    def form(first, count, meta):
        formed = pieces(first, count, meta, me, ua, operands)
        for ring in range(2):
            handed = swapped(formed[2 * ring + 1], DP, 1)
            for n in range(count):
                own[ring, first + n] = formed[2 * ring][n]
                others[ring, first + n] = handed[n]

    form(0, 1, meta)
    meta, own[0, 0] = lax.optimization_barrier((meta, own[0, 0]))
    form(1, 1, meta)
    later = {1: (2, 2), 2: (4, 2), 4: (6, 2)}
    acc = [add(0, 0), add(1, 0)]

    steps = ring_steps(dp_count)
    for step in range(1, RING):
        if step in later:
            meta, *acc = lax.optimization_barrier((meta, *acc))
            form(*later[step], meta)
        came = [lax.ppermute(acc[ring], DP, steps) for ring in range(2)]
        acc = [add(ring, step, came[ring]) for ring in range(2)]
    acc_a, acc_b = acc
    bit = GROUP
    while bit < dp_count:
        acc_a = (acc_a.astype(F32) + swapped(acc_a, DP, bit).astype(F32)).astype(BF16)
        acc_b = (acc_b.astype(F32) + swapped(acc_b, DP, bit).astype(F32)).astype(BF16)
        bit *= 2
    spare = lax.slice_in_dim(acc_b, REL.stop, B_ROWS, axis=0)
    came = swapped(spare, SECTION, 1)
    holds = (meta[META_CORE] == MASK_ROW % 2) & (meta[2 * RING - 1] == MASK_ROW // 2)
    row = lax.broadcasted_iota(jnp.int32, spare.shape, 0)
    spare = jnp.where(holds & (row == 0), (spare.astype(F32) + came.astype(F32)).astype(BF16), spare)
    acc_b = lax.dynamic_update_slice_in_dim(acc_b, spare, REL.stop, axis=0)
    ffn_outs = [shape(1, width, ff, dtype=F32), shape(1, ff, width, dtype=F32)]
    rest_outs = [shape(1, width, width, dtype=F32) for _ in range(4)] + [shape(rel_rows, width, dtype=F32)]
    rest_outs.append(shape(16 * RING, width, dtype=F32))
    tokens = []
    outs = ffn_outs + rest_outs
    for step in range(RING):
        if step:
            acc_a = lax.ppermute(acc_a, DP, steps)
            acc_b = lax.ppermute(acc_b, DP, steps)
        handed_a, handed_b, before = acc_a, acc_b, []
        if step > 1:
            handed_a, before_a = lax.optimization_barrier((acc_a, tokens[step - 2]))
            before.append(before_a)
        if step:
            handed_b, before_b = lax.optimization_barrier((acc_b, tokens[step - 1]))
            before.append(before_b)
        outs, token = unpack(
            step, meta, acc_a, swapped(handed_a, DP, 1), acc_b, swapped(handed_b, DP, 1), outs, before,
            pos_b if step == RING - 1 else None, heads,
        )
        tokens.append(token)
    ffn_outs, rest_outs = outs[:2], outs[2:]
    (
        grad_w_rel, grad_bc, grad_bp, grad_bs, grad_seg, grad_n1g, grad_n1s, grad_fib, grad_fob, grad_n2g, grad_n2s,
        mask_grad,
    ) = tokens[-1]
    grad_ffn_in, grad_ffn_out = ffn_outs
    grad_w_query, grad_w_key, grad_w_value, grad_w_out = rest_outs[:4]
    one_layer = lambda v: v.reshape(1, heads, dim)
    return (
        kept.content_out, kept.query_out, grads.input_grad, mask_grad,
        grad_w_query, grad_w_key, grad_w_value, grad_w_out, grad_w_rel,
        one_layer(grad_bc), one_layer(grad_bp), one_layer(grad_bs), jnp.transpose(grad_seg, (1, 0, 2))[None],
        grad_n1g, grad_n1s, grad_ffn_in, grad_fib, grad_ffn_out, grad_fob, grad_n2g, grad_n2s,
    )


def solution(mesh):
    two, three, four = P(SECTION, None), P(SECTION, None, None), P(SECTION, None, None, None)
    rows = P(SECTION, DP, None, None)
    return jax.shard_map(
        shards,
        mesh=mesh,
        in_specs=(
            P(DP, None, None), rows, P(), P(DP, None), P(DP, None), P(DP, None), P(DP), *[three] * 8, four,
            two, two, three, two, three, two, two, two, rows, rows,
        ),
        out_specs=(
            rows, rows, rows, P(), *[three] * 8, four, two, two, three, two, three, two, two, two,
        ),
        check_vma=False,
    )
```

```python
import functools
import types

import jax
import jax.numpy as jnp
import numpy as np
from jax import lax
from jax.experimental import pallas as pl
from jax.experimental.pallas import tpu as pltpu
from jax.sharding import PartitionSpec as P

BF16 = jnp.bfloat16
F32 = jnp.float32
NEG_FILL = -1e30
NORM_EPS = 1e-05
GELU_A = 0.7978845608028654
GELU_B = 0.044715
VMEM_LIMIT = 60 * 1024 * 1024
LANES = 128
LAYER_FLOPS = 9_000_000_000
RING = 8
META_CORE, META_SECTION = 2 * RING, 2 * RING + 1

ROW_BC, ROW_BP, ROW_BS, ROW_SEG0, ROW_SEG1 = 0, 1, 2, 3, 4
ROW_N1G, ROW_N1S, ROW_FOB, ROW_N2G, ROW_N2S, ROW_MASK, ROW_FIB = 5, 6, 7, 8, 9, 10, 11
SMALL_ROWS = 16


def dot_nn(left, right):
    return jnp.dot(left, right, preferred_element_type=F32)


def dot_nt(left, right):
    return lax.dot_general(left, right, (((1,), (1,)), ((), ())), preferred_element_type=F32)


def dot_tn(left, right):
    return lax.dot_general(left, right, (((0,), (0,)), ((), ())), preferred_element_type=F32)


def col_sum(block):
    return jnp.sum(block, axis=0, keepdims=True)


def norm_parts(rows):
    center = jnp.mean(rows, axis=-1, keepdims=True)
    offset = rows - center
    spread = jnp.mean(offset * offset, axis=-1, keepdims=True)
    scale = lax.rsqrt(spread + NORM_EPS)
    return offset * scale, scale


def norm_back(grad, unit, scale, gain):
    inner = grad * gain
    mean_inner = jnp.mean(inner, axis=-1, keepdims=True)
    mean_cross = jnp.mean(inner * unit, axis=-1, keepdims=True)
    return (inner - mean_inner - unit * mean_cross) * scale


def half_masks():
    lane = lax.broadcasted_iota(jnp.int32, (1, LANES), 1)
    low = lane < LANES // 2
    return low, low.astype(F32).astype(BF16), (~low).astype(F32).astype(BF16)


def stack_heads(block, low_b, high_b):
    return jnp.concatenate([block * low_b, block * high_b], axis=0)


def copy_in(pairs, sems):
    copies = [
        pltpu.make_async_copy(src, dst, sems.at[n]) for n, (src, dst) in enumerate(pairs)
    ]
    for copy in copies:
        copy.start()
    return copies


def name_refs(names_in, names_out, names_scratch, refs):
    groups, start = [], 0
    for names in (names_in, names_out, names_scratch):
        groups.append(types.SimpleNamespace(**dict(zip(names, refs[start : start + len(names)]))))
        start += len(names)
    return groups


def forward_body(section, slot, names_in, names_out, names_scratch, *refs):
    r, o, s = name_refs(names_in, names_out, names_scratch, refs)
    meta = r.meta
    seg_rows, width = s.stream.shape[0] // 2, s.stream.shape[1]
    key_rows = s.joined.shape[0]
    pairs_count = width // LANES
    ff = s.act.shape[1]
    score_scale = 0.125

    @pl.when(meta[META_SECTION] == section)
    def _run():
        sem_in, sem_out = s.sem_in, s.sem_out
        mem_rows = key_rows - seg_rows
        x_src = r.content_in.at[slot] if section == 0 else r.arrived.at[pl.ds(0, seg_rows)]
        loads = [
            (r.memory.at[0, slot], s.joined.at[pl.ds(0, mem_rows)]),
            (x_src, s.joined.at[pl.ds(mem_rows, seg_rows)]),
            (x_src, s.stream.at[pl.ds(0, seg_rows)]),
            (r.w_key.at[0], s.wk),
            (r.w_query.at[0], s.wq),
            (r.rel, s.rel),
            (r.w_value.at[0], s.wv),
            (r.w_out.at[0], s.wo),
            (r.ffn_in.at[0], s.fi),
            (r.ffn_out.at[0], s.fo),
        ]
        moves = []
        if section == 1:
            query_rows = pl.ds(seg_rows, seg_rows)
            moves = copy_in([(r.arrived.at[query_rows], s.stream.at[query_rows])], s.sem_first)
        moves = copy_in(loads, sem_in) + moves
        stores = []

        def store(src, dst):
            copy = pltpu.make_async_copy(src, dst, sem_out.at[len(stores)])
            copy.start()
            stores.append(copy)

        small = r.small
        used = (r.slot_used[slot] > 0).astype(jnp.int32).astype(F32)
        if section == 0:
            s.stream[seg_rows:, :] = jnp.broadcast_to(
                small[ROW_MASK : ROW_MASK + 1, :], (seg_rows, width)
            ).astype(BF16)
        square = (seg_rows, seg_rows)
        doc = jnp.broadcast_to(r.docs[slot : slot + 1, :].astype(F32), square)
        order = jnp.broadcast_to(r.orders[slot : slot + 1, :].astype(F32), square)
        target = jnp.broadcast_to(r.targets[slot : slot + 1, :].astype(F32), square)
        same = doc == doc.T
        visible = same & ((target == 0.0) | (order <= order.T))
        row_id = lax.broadcasted_iota(jnp.int32, square, 0)
        col_id = lax.broadcasted_iota(jnp.int32, square, 1)
        s.bias[0] = jnp.where(visible, 0.0, NEG_FILL)
        s.bias[1] = jnp.where(visible & (row_id != col_id), 0.0, NEG_FILL)

        for n in (0, 1, 3):
            moves[n].wait()
        s.k[...] = dot_nn(s.joined[...], s.wk[...]).astype(BF16)
        store(s.k, o.k.at[slot])
        store(s.joined, o.joined.at[slot])
        moves[2].wait()
        if section == 1:
            moves[10].wait()
        store(s.stream, o.stream.at[slot])
        moves[4].wait()
        queries = dot_nn(s.stream[...], s.wq[...])
        for block, kept, row in ((s.qc, o.qc, ROW_BC), (s.qp, o.qp, ROW_BP), (s.qs, o.qs, ROW_BS)):
            with_bias = (queries + small[row : row + 1, :]).astype(BF16)
            block[...] = (with_bias.astype(F32) * score_scale).astype(BF16)
            store(block, kept.at[slot])
        moves[6].wait()
        s.v[...] = dot_nn(s.joined[...], s.wv[...]).astype(BF16)
        store(s.v, o.v.at[slot])
        moves[5].wait()

        low, low_b, high_b = half_masks()
        bias_by_stream = [s.bias[0], s.bias[1]]
        inside = col_id <= row_id
        for pair in range(pairs_count):
            sl = slice(pair * LANES, (pair + 1) * LANES)
            position = dot_nt(stack_heads(s.qp[:, sl], low_b, high_b), s.rel[:, sl])
            for part in range(4):
                base = part * seg_rows
                turned = [
                    pltpu.roll(
                        position[base : base + seg_rows, n * LANES : (n + 1) * LANES],
                        1, axis=1, stride=1, stride_axis=0,
                    )
                    for n in range(3)
                ]
                rolled = jnp.concatenate(
                    [jnp.where(inside, turned[n], turned[n + 1]) for n in range(2)], axis=1
                )
                s.pos[pair, base : base + seg_rows, :] = rolled
        for pair in range(pairs_count):
            sl = slice(pair * LANES, (pair + 1) * LANES)
            content = dot_nt(stack_heads(s.qc[:, sl], low_b, high_b), s.k[:, sl])
            segments = jnp.concatenate(
                [
                    jnp.broadcast_to(small[row : row + 1, sl].astype(BF16) * mask, (LANES, LANES))
                    for mask in (low_b, high_b)
                    for row in (ROW_SEG0, ROW_SEG1)
                ],
                axis=0,
            )
            pieces_wide = dot_nt(s.qs[:, sl], segments)
            probs_pair = []
            for head in range(2):
                probs_streams = []
                for stream in range(2):
                    base = (2 * head + stream) * seg_rows
                    rows = slice(stream * seg_rows, (stream + 1) * seg_rows)
                    same_part = pieces_wide[rows, 2 * head * LANES : (2 * head + 1) * LANES]
                    other_part = pieces_wide[rows, (2 * head + 1) * LANES : (2 * head + 2) * LANES]
                    body = content[base : base + seg_rows, :] + s.pos[pair, base : base + seg_rows, :]
                    left = body[:, :mem_rows] + other_part
                    right = body[:, mem_rows:] + jnp.where(same, same_part, other_part) + bias_by_stream[stream]
                    peak = jnp.max(jnp.maximum(left, right), axis=-1, keepdims=True)
                    left = jnp.exp(left - peak)
                    right = jnp.exp(right - peak)
                    total = jnp.sum(left + right, axis=-1, keepdims=True)
                    inverse = 1.0 / total
                    probs_streams.append(
                        jnp.concatenate([left * inverse, right * inverse], axis=1).astype(BF16)
                    )
                probs = jnp.concatenate(probs_streams, axis=0)
                s.p[2 * pair + head] = probs
                store(s.p.at[2 * pair + head], o.p.at[slot, 2 * pair + head])
                probs_pair.append(probs)
            mixed = dot_nn(
                jnp.concatenate(probs_pair, axis=1), stack_heads(s.v[:, sl], low_b, high_b)
            )
            s.mixed[:, sl] = mixed.astype(BF16)
        store(s.mixed, o.mixed.at[slot])

        moves[7].wait()
        middle_in = dot_nn(s.mixed[...], s.wo[...]) + s.stream[...].astype(F32)
        s.mid_in[...] = middle_in
        store(s.mid_in, o.mid_in.at[slot])
        unit, _ = norm_parts(middle_in)
        middle = unit * small[ROW_N1G : ROW_N1G + 1, :] + small[ROW_N1S : ROW_N1S + 1, :]
        s.midb[...] = middle.astype(BF16)
        store(s.midb, o.me.at[0, slot])
        s.outer[...] = middle + small[ROW_FOB : ROW_FOB + 1, :]
        moves[8].wait()
        moves[9].wait()
        for step in range(ff // width):
            cols = slice(step * width, (step + 1) * width)
            inner = (
                dot_nn(s.midb[...], s.fi[:, cols])
                + small[ROW_FIB + step : ROW_FIB + step + 1, :]
            )
            square_in = inner * inner
            wave = jnp.tanh(GELU_A * inner * (1.0 + GELU_B * square_in))
            half = 0.5 * (1.0 + wave)
            active = (inner * half).astype(BF16)
            slope = half + (0.5 * GELU_A) * inner * (1.0 - wave * wave) * (1.0 + 3.0 * GELU_B * square_in)
            s.act[:, cols] = active
            s.slope[:, cols] = slope.astype(BF16)
            part = pl.ds(step * width, width)
            store(s.act.at[:, part], o.ua.at[1, slot, :, part])
            store(s.slope.at[:, part], o.slope.at[slot, :, part])
            s.outer[...] += dot_nn(active, s.fo[cols, :])
        store(s.outer, o.outer.at[slot])
        unit, _ = norm_parts(s.outer[...])
        result = unit * small[ROW_N2G : ROW_N2G + 1, :] + small[ROW_N2S : ROW_N2S + 1, :]
        s.out[...] = (result * used).astype(BF16)
        store(s.out.at[pl.ds(0, seg_rows)], o.content_out.at[0, slot])
        store(s.out.at[pl.ds(seg_rows, seg_rows)], o.query_out.at[0, slot])
        if section == 0:
            store(s.out, o.sent)
        for copy in stores:
            copy.wait()


def backward_body(section, slot, names_in, names_out, names_scratch, *refs):
    r, o, s = name_refs(names_in, names_out, names_scratch, refs)
    meta = r.meta
    rows, width = s.a.shape
    seg_rows = rows // 2
    ff = s.slope.shape[1]
    key_rows = s.k.shape[0]
    mem_rows = key_rows - seg_rows
    pairs_count = width // LANES
    score_scale = 0.125

    @pl.when(meta[META_SECTION] == section)
    def _run():
        first_loads = [
            (r.content_cot.at[0, slot], s.cot.at[pl.ds(0, seg_rows)]),
            (r.query_cot.at[0, slot], s.cot.at[pl.ds(seg_rows, seg_rows)]),
            (r.outer.at[slot], s.outer),
        ]
        if section == 0:
            first_loads.append((r.returned, s.returned))
        first = copy_in(first_loads, s.sem_first)
        loads = []
        for step in range(ff // width):
            part = pl.ds(step * width, width)
            loads.append((r.ffn_out.at[0, part], s.fo.at[part]))
            loads.append((r.slope.at[slot, :, part], s.slope.at[:, part]))
            loads.append((r.ffn_in.at[0, :, part], s.fi.at[:, part]))
        loads.append((r.mid_in.at[slot], s.mid_in))
        head_loads = [
            (r.w_out.at[0], s.wo),
            (r.v.at[slot], s.v),
            (r.p.at[slot], s.p),
            (r.k.at[slot], s.k),
            (r.qc.at[slot], s.qc),
            (r.qp.at[slot], s.qp),
            (r.qs.at[slot], s.qs),
            (r.rel, s.rel),
            (r.w_query.at[0], s.wq),
            (r.w_key.at[0], s.wk),
            (r.w_value.at[0], s.wv),
        ]
        stores = []

        def store(src, dst):
            copy = pltpu.make_async_copy(src, dst, s.sem_out.at[len(stores)])
            copy.start()
            stores.append(copy)

        small = r.small
        used = (r.slot_used[slot] > 0).astype(jnp.int32).astype(F32)
        for move in first:
            move.wait()
        moves = copy_in(loads, s.sem_tail)
        grad = s.cot[...].astype(F32) * used
        if section == 0:
            grad = grad + s.returned[...].astype(F32)
        unit, scale = norm_parts(s.outer[...])
        out = s.sums_t
        out[...] = jnp.zeros_like(out)
        out[4:5, :] = col_sum(grad * unit)
        out[5:6, :] = col_sum(grad)
        grad_outer = norm_back(grad, unit, scale, small[ROW_N2G : ROW_N2G + 1, :])
        s.e[...] = grad_outer.astype(BF16)
        store(s.e, o.me.at[1, slot])
        out[3:4, :] = col_sum(s.e[...].astype(F32))
        s.acc[...] = grad_outer
        for step in range(ff // width):
            for move in moves[3 * step : 3 * step + 3]:
                move.wait()
            cols = slice(step * width, (step + 1) * width)
            if step == 1:
                head_moves = copy_in(head_loads, s.sem_head)
            grad_active = dot_nt(s.e[...], s.fo[cols, :])
            inner_b = (s.slope[:, cols].astype(F32) * grad_active).astype(BF16)
            s.u[:, cols] = inner_b
            out[8 + step : 9 + step, :] = col_sum(inner_b.astype(F32))
            s.acc[...] += dot_nt(inner_b, s.fi[:, cols])
        store(s.u, o.ua.at[0, slot])
        moves[-1].wait()
        unit, scale = norm_parts(s.mid_in[...])
        grad = s.acc[...]
        out[1:2, :] = col_sum(grad * unit)
        out[2:3, :] = col_sum(grad)
        s.a[...] = norm_back(grad, unit, scale, small[ROW_N1G : ROW_N1G + 1, :])
        s.ab[...] = s.a[...].astype(BF16)
        store(s.ab, o.ab.at[slot])
        store(s.sums_t, o.sums.at[slot, pl.ds(8, 16)])

        square = (seg_rows, seg_rows)
        doc = jnp.broadcast_to(r.docs[slot : slot + 1, :].astype(F32), square)
        same_one = (doc == doc.T).astype(F32)
        same = jnp.concatenate([same_one, same_one], axis=0)
        flip_rows = lax.broadcasted_iota(jnp.int32, (rows, rows), 0)
        flip_cols = lax.broadcasted_iota(jnp.int32, (rows, rows), 1)
        flipped_to = jnp.where(flip_rows < seg_rows, seg_rows - 1, rows + seg_rows - 1) - flip_rows
        flip = (flip_cols == flipped_to).astype(F32).astype(BF16)
        out = s.sums
        out[...] = jnp.zeros_like(out)
        head_moves[0].wait()
        s.x[...] = dot_nt(s.ab[...], s.wo[...]).astype(BF16)
        for n in (1, 2, 3, 4, 5, 6, 7):
            head_moves[n].wait()
        s.qpf[...] = dot_nn(flip, s.qp[...]).astype(BF16)

        low, low_b, high_b = half_masks()
        past = lax.broadcasted_iota(jnp.int32, square, 1) >= lax.broadcasted_iota(jnp.int32, square, 0)
        for pair in range(pairs_count):
            sl = slice(pair * LANES, (pair + 1) * LANES)
            grads_mixed = stack_heads(s.x[:, sl], low_b, high_b)
            grad_probs = dot_nt(grads_mixed, s.v[:, sl])
            scores_b = []
            same_sums, other_sums = [], []
            for head in range(2):
                probs = s.p[2 * pair + head].astype(F32)
                product = probs * grad_probs[head * rows : (head + 1) * rows, :]
                delta = jnp.sum(product, axis=-1, keepdims=True)
                rounded = (product - probs * delta).astype(BF16)
                scores_b.append(rounded)
                wide = rounded.astype(F32)
                right = wide[:, mem_rows:] * same
                same_sum = jnp.sum(right, axis=-1, keepdims=True)
                same_sums.append(same_sum)
                other_sums.append(
                    jnp.sum(wide[:, :mem_rows] + (wide[:, mem_rows:] - right), axis=-1, keepdims=True)
                )
            stacked = jnp.concatenate(scores_b, axis=0)
            beside = jnp.concatenate(scores_b, axis=1)
            probs_stacked = jnp.concatenate([s.p[2 * pair], s.p[2 * pair + 1]], axis=0)
            s.dv[:, sl] = dot_tn(probs_stacked, grads_mixed).astype(BF16)
            s.dk[:, sl] = dot_tn(stacked, stack_heads(s.qc[:, sl], low_b, high_b)).astype(BF16)
            grad_content = dot_nn(beside, stack_heads(s.k[:, sl], low_b, high_b)) * score_scale
            same_sel = jnp.where(low, same_sums[0], same_sums[1])
            other_sel = jnp.where(low, other_sums[0], other_sums[1])
            seg0 = small[ROW_SEG0 : ROW_SEG0 + 1, sl]
            seg1 = small[ROW_SEG1 : ROW_SEG1 + 1, sl]
            grad_segment = (same_sel * seg0 + other_sel * seg1) * score_scale
            qs = s.qs[:, sl].astype(F32)
            out[0:1, sl] = col_sum(grad_content)
            out[2:3, sl] = col_sum(grad_segment)
            out[3:4, sl] = col_sum(same_sel * qs)
            out[4:5, sl] = col_sum(other_sel * qs)
            s.dq[:, sl] = grad_content + grad_segment
            turned = dot_nn(flip, beside)
            shifted_heads = []
            for head in range(2):
                parts = []
                for stream in range(2):
                    blocks = [
                        pltpu.roll(
                            turned[
                                stream * seg_rows : (stream + 1) * seg_rows,
                                head * key_rows + n * LANES : head * key_rows + (n + 1) * LANES,
                            ],
                            0, axis=1, stride=1, stride_axis=0,
                        )
                        for n in range(2)
                    ]
                    blocks = [
                        jnp.where(past, blocks[0], 0.0),
                        jnp.where(past, blocks[1], blocks[0]),
                        jnp.where(past, 0.0, blocks[1]),
                    ]
                    parts.append(jnp.concatenate(blocks, axis=1).astype(BF16))
                shifted_heads.append(jnp.concatenate(parts, axis=0))
            grad_position = (
                dot_nn(
                    jnp.concatenate(shifted_heads, axis=1),
                    stack_heads(s.rel[:, sl], low_b, high_b),
                )
                * score_scale
            )
            out[1:2, sl] = col_sum(grad_position)
            s.dqp[:, sl] = grad_position
            s.drel[:, sl] = dot_tn(
                jnp.concatenate(shifted_heads, axis=0),
                stack_heads(s.qpf[:, sl], low_b, high_b),
            )
        store(s.dk, o.dk.at[slot])
        store(s.dv, o.dv.at[slot])
        store(s.drel, o.drel.at[slot])
        grad_position = s.dqp[...]
        position_high = grad_position.astype(BF16)
        position_low = (grad_position - position_high.astype(F32)).astype(BF16)
        grad_queries = s.dq[...] + dot_nn(flip, position_high) + dot_nn(flip, position_low)
        s.dqb[...] = grad_queries.astype(BF16)
        store(s.dqb, o.dq.at[slot])
        for n in (8, 9, 10):
            head_moves[n].wait()
        grad_rows = s.a[...] + dot_nt(s.dqb[...], s.wq[...])
        grad_content = (
            grad_rows[:seg_rows, :]
            + dot_nt(s.dk[mem_rows:, :], s.wk[...])
            + dot_nt(s.dv[mem_rows:, :], s.wv[...])
        )
        grad_query = grad_rows[seg_rows:, :]
        s.out[:seg_rows, :] = grad_content.astype(BF16)
        s.out[seg_rows:, :] = grad_query.astype(BF16)
        store(s.out.at[pl.ds(0, seg_rows)], o.input_grad.at[0, slot])
        if section == 1:
            store(s.out, o.sent)
        if section == 0:
            out[5:6, :] = col_sum(grad_query)
        store(s.sums, o.sums.at[slot, pl.ds(0, 8)])
        for copy in stores:
            copy.wait()


ANY_SPEC = pl.BlockSpec(memory_space=pltpu.HBM)
SMEM_SPEC = pl.BlockSpec(memory_space=pltpu.SMEM)
VMEM_SPEC = pl.BlockSpec(memory_space=pltpu.VMEM)


def call_kernel(body, section, slot, inputs, carried, fresh, scratch):
    names_in = list(inputs)
    arrays = [inputs[n][1] for n in names_in]
    specs = [inputs[n][0] for n in names_in]
    aliases = {}
    names_out = list(carried) + list(fresh)
    out_shapes = []
    for position, key in enumerate(carried):
        value = carried[key]
        out_shapes.append(jax.ShapeDtypeStruct(value.shape, value.dtype))
        if not isinstance(value, jax.ShapeDtypeStruct):
            aliases[len(arrays)] = position
            arrays.append(value)
            specs.append(ANY_SPEC)
            names_in.append(key + "_")
    out_shapes += [fresh[key] for key in fresh]
    results = pl.pallas_call(
        functools.partial(body, section, slot, names_in, names_out, list(scratch)),
        out_shape=tuple(out_shapes),
        in_specs=specs,
        out_specs=tuple(ANY_SPEC for _ in out_shapes),
        scratch_shapes=list(scratch.values()),
        input_output_aliases=aliases,
        compiler_params=pltpu.CompilerParams(vmem_limit_bytes=VMEM_LIMIT),
        cost_estimate=pl.CostEstimate(flops=LAYER_FLOPS, bytes_accessed=20_000_000, transcendentals=0),
    )(*arrays)
    named = dict(zip(names_out, results))
    return {k: named[k] for k in carried}, {k: named[k] for k in fresh}


def in_hbm(**arrays):
    return {key: (ANY_SPEC, value) for key, value in arrays.items()}


def in_vmem(**arrays):
    return {key: (VMEM_SPEC, value) for key, value in arrays.items()}


def params():
    return pltpu.CompilerParams(vmem_limit_bytes=VMEM_LIMIT)


def cost(flops, moved):
    return pl.CostEstimate(flops=flops, bytes_accessed=moved, transcendentals=0)


def shape(*dims, dtype=BF16):
    return jax.ShapeDtypeStruct(dims, dtype)


def prepare_body(bc, bp, bs, seg, n1g, n1s, fob, n2g, n2s, mask, fib, pos, w_rel, small, rel):
    heads, dim = bc.shape[1:]
    width = heads * dim
    wide = [(row, value[0].astype(F32)) for row, value in ((ROW_BC, bc), (ROW_BP, bp), (ROW_BS, bs))]
    for head in range(heads):
        cols = slice(head * dim, (head + 1) * dim)
        for row, value in wide:
            small[row : row + 1, cols] = value[head : head + 1, :]
        small[ROW_SEG0 : ROW_SEG1 + 1, cols] = seg[head].astype(F32)
    for row, value in (
        (ROW_N1G, n1g), (ROW_N1S, n1s), (ROW_FOB, fob), (ROW_N2G, n2g), (ROW_N2S, n2s),
    ):
        small[row : row + 1, :] = value[...].astype(F32)
    small[ROW_MASK : ROW_MASK + 1, :] = mask[...].astype(F32).reshape(1, width)
    for step in range(4):
        small[ROW_FIB + step : ROW_FIB + step + 1, :] = fib[:, step * width : (step + 1) * width].astype(F32)
    small[SMALL_ROWS - 1 : SMALL_ROWS, :] = jnp.zeros((1, width), F32)
    rel[...] = dot_nn(pos[...], w_rel[0]).astype(BF16)


GROUP = 16
SUM_ROWS = 24
MASK_ROW = 5
HALF = 384
HEAD_ROWS = 320
REST_ROWS = HALF - HEAD_ROWS
REL_PIECE = 24
BLOCK = slice(REST_ROWS, REST_ROWS + HALF // 2)
REL = slice(BLOCK.stop, BLOCK.stop + REL_PIECE)
B_ROWS = BLOCK.stop + 32


def lane_slice(start, size):
    return pl.ds(pl.multiple_of(start, LANES), size)


def block_rows(index, size):
    return pl.ds(pl.multiple_of(index * size, size), size)


def pieces_body(meta, me, ua, stream, joined, mixed, dq, dk, dv, ab, drel, sums, *refs):
    own_a, own_b, first_a, first_b, other_a, other_b = refs[:6]
    vme, vua, vs, vj, vmix, vdq, vdk, vdv, vab, rel, small, stage_a, stage_b, sems, out_sems = refs[6:]
    core, count = meta[META_CORE], RING
    width = vs.shape[1]
    part = width

    loads = [(me.at[0], vme.at[0])]
    for half in range(2):
        for n in range(vua.shape[2] // part):
            cols = pl.ds(n * part, part)
            loads.append((ua.at[half, :, cols], vua.at[half, :, cols]))
        if half == 0:
            loads.append((me.at[1], vme.at[1]))
    blocks_from = len(loads)
    loads += [
        (stream, vs), (dq, vdq), (joined, vj), (dk, vdk), (dv, vdv), (mixed, vmix), (ab, vab), (drel, rel), (sums, small),
    ]
    moves = copy_in(loads, sems)
    moves[0].wait()
    writes = []

    def put(src, owner, step, own, first, other):
        sem = out_sems.at[len(writes)]
        mine = core == owner
        pl.when(mine)(lambda: pltpu.make_async_copy(src, own.at[step], sem).start())
        pl.when(~mine & (step == 0))(lambda: pltpu.make_async_copy(src, first.at[0], sem).start())
        pl.when(~mine & (step != 0))(
            lambda: pltpu.make_async_copy(src, other.at[jnp.maximum(step, 1) - 1], sem).start()
        )
        writes.append(pltpu.make_async_copy(src, own.at[step], sem))

    def step_of(owner, k):
        return (meta[owner * RING] - k) & (RING - 1)

    for owner in range(2):
        base = 1 + owner * (vua.shape[2] // part + 1)
        if owner == 1:
            moves[base - 1].wait()
        for k in range(count):
            if k % 2 == 0:
                moves[base + k // 2].wait()
            if owner == 0:
                lhs = vme[0, :, (k % 2) * HALF : (k % 2 + 1) * HALF]
                rhs = vua[0, :, (k // 2) * width : (k // 2 + 1) * width]
            else:
                lhs, rhs = vua[1, :, k * HALF : (k + 1) * HALF], vme[1]
            whole = dot_tn(lhs, rhs).astype(BF16)
            stage_a[owner, k] = whole[:HEAD_ROWS]
            stage_b[owner, k, :REST_ROWS] = whole[HEAD_ROWS:]
            put(stage_a.at[owner, k], owner, step_of(owner, k), own_a, first_a, other_a)
    for move in moves[blocks_from:]:
        move.wait()
    for owner in range(2):
        for k in range(count):
            left, right = (((vs, vdq), (vj, vdk)), ((vj, vdv), (vmix, vab)))[owner][k // 4]
            inside = k % 4
            value = dot_tn(
                left[:, (inside // 2) * HALF : (inside // 2 + 1) * HALF],
                right[:, (inside % 2) * HALF : (inside % 2 + 1) * HALF],
            ).astype(BF16)
            stage_b[owner, k, BLOCK.start : BLOCK.stop, :HALF] = value[: HALF // 2]
            stage_b[owner, k, BLOCK.start : BLOCK.stop, HALF:] = value[HALF // 2 :]
            at = (owner * RING + k) * REL_PIECE
            row = 2 * k + owner
            rows = [
                small[0, n : n + 1, :] + small[1, n : n + 1, :] for n in (row, min(row + 2 * RING, SUM_ROWS - 1))
            ]
            blank = jnp.zeros((B_ROWS - REL.stop - 2, width), F32)
            stage_b[owner, k, BLOCK.stop :] = jnp.concatenate(
                [rel[0, at : at + REL_PIECE, :] + rel[1, at : at + REL_PIECE, :], *rows, blank], axis=0
            ).astype(BF16)
            put(stage_b.at[owner, k], owner, step_of(owner, k), own_b, first_b, other_b)
    for copy in writes:
        copy.wait()


def pieces(meta, me, ua, operands):
    rows, width = operands[0].shape
    ff = ua.shape[2]

    def vm(*dims, dtype=BF16):
        return pltpu.VMEM(dims, dtype)

    return pl.pallas_call(
        pieces_body,
        out_shape=[
            shape(count, size, width) for count in (RING, 1, RING - 1) for size in (HEAD_ROWS, B_ROWS)
        ],
        in_specs=[SMEM_SPEC] + [ANY_SPEC] * (2 + len(operands)),
        out_specs=[ANY_SPEC] * 6,
        scratch_shapes=[
            vm(2, rows, width), vm(2, rows, ff), *[vm(rows, width)] * 7,
            vm(*operands[-2].shape, dtype=F32), vm(*operands[-1].shape, dtype=F32),
            vm(2, RING, HEAD_ROWS, width), vm(2, RING, B_ROWS, width),
            pltpu.SemaphoreType.DMA((11 + 2 * (ff // width),)), pltpu.SemaphoreType.DMA((4 * RING,)),
        ],
        compiler_params=params(),
        cost_estimate=cost(6 * rows * HALF * width * RING, 30_000_000),
    )(meta, me, ua, *operands)


def by_core(meta, own, other, low_f, high_f):
    low = meta[META_CORE] == 0

    @pl.when(low)
    def _low():
        low_f[...] = own[...].astype(F32)
        high_f[...] = other[...].astype(F32)

    @pl.when(~low)
    def _high():
        low_f[...] = other[...].astype(F32)
        high_f[...] = own[...].astype(F32)


def ffn_places(fi, fo, low_at, high_at, first, count):
    width = fo.shape[2]
    return (
        fi.at[0, pl.ds(pl.multiple_of((low_at % 2) * HALF + first, 8), count), lane_slice((low_at // 2) * width, width)],
        fo.at[0, pl.ds(pl.multiple_of(high_at * HALF + first, 8), count), :],
    )


def finish_small(gathered, bc, bp, bs, seg, n1g, n1s, fib, fob, n2g, n2s, mask_out):
    def row(at):
        place = 8 * (at % (2 * RING)) + at // (2 * RING)
        return gathered[place : place + 1, :]

    heads, dim = bc.shape[0], bc.shape[2]
    width = heads * dim
    rows = [row(at) for at in range(5)]
    for head in range(heads):
        cols = slice(head * dim, (head + 1) * dim)
        bc[head] = rows[0][:, cols]
        bp[head] = rows[1][:, cols]
        bs[head] = rows[2][:, cols]
        seg[head, 0:1, :] = rows[3][:, cols]
        seg[head, 1:2, :] = rows[4][:, cols]
    mask_out[...] = row(MASK_ROW).reshape(width)
    for out, at in ((n1g, 9), (n1s, 10), (fob, 11), (n2g, 12), (n2s, 13)):
        out[...] = row(at)
    for step in range(4):
        fib[:, step * width : (step + 1) * width] = row(16 + step)


def unpack_body(step, last, meta, own_a, other_a, own_b, other_b, *refs):
    if last:
        pos, rel_in, small_in = refs[0], refs[7], refs[8]
        *small_outs, low_a, high_a, low_f, high_f, sems, rel_all, small_all, rel_sem = refs[-19:]
        fi, fo, wq, wk, wv, wo, rel, small, w_rel = refs[-28:-19]
        rel_copies = [
            pltpu.make_async_copy(rel_in, rel_all, rel_sem.at[0]),
            pltpu.make_async_copy(small_in, small_all, rel_sem.at[1]),
        ]
        for copy in rel_copies:
            copy.start()
    else:
        fi, fo, wq, wk, wv, wo, rel, small, token, low_a, high_a, low_f, high_f, sems = refs[-14:]
        token[...] = jnp.zeros_like(token)
    low_at, high_at = meta[step], meta[RING + step]
    by_core(meta, own_a, other_a, low_a, high_a)
    low_to, high_to = ffn_places(fi, fo, low_at, high_at, 0, HEAD_ROWS)
    copies = [
        pltpu.make_async_copy(low_a, low_to, sems.at[8]),
        pltpu.make_async_copy(high_a, high_to, sems.at[9]),
    ]
    for copy in copies:
        copy.start()
    by_core(meta, own_b, other_b, low_f, high_f)
    low_to, high_to = ffn_places(fi, fo, low_at, high_at, HEAD_ROWS, REST_ROWS)
    rest = pl.ds(0, REST_ROWS)
    rel_part = pl.ds(REL.start, REL_PIECE)

    def rel_to(at):
        return rel.at[pl.ds(pl.multiple_of(at * REL_PIECE, 8), REL_PIECE), :]

    later = [
        pltpu.make_async_copy(low_f.at[rest], low_to, sems.at[0]),
        pltpu.make_async_copy(high_f.at[rest], high_to, sems.at[1]),
    ]
    blocks = ((low_f, low_at, 2 * low_at, 0), (high_f, RING + high_at, 2 * high_at + 1, 1))
    small_part = pl.ds(REL.stop, 8)
    if not last:
        for src, at, row, n in blocks:
            later.append(pltpu.make_async_copy(src.at[rel_part], rel_to(at), sems.at[2 + n]))
            later.append(
                pltpu.make_async_copy(src.at[small_part], small.at[pl.ds(pl.multiple_of(8 * row, 8), 8), :], sems.at[10 + n])
            )
    for copy in later:
        copy.start()

    def block_copies(src, at, dst, sem):
        inside = at % 4
        return [
            pltpu.make_async_copy(
                src.at[pl.ds(BLOCK.start, HALF // 2), pl.ds(part * HALF, HALF)],
                dst.at[
                    0,
                    pl.ds(pl.multiple_of((inside // 2) * HALF + part * (HALF // 2), 8), HALF // 2),
                    lane_slice((inside % 2) * HALF, HALF),
                ],
                sems.at[sem + part],
            )
            for part in range(2)
        ]

    for src, at, early, late, n in ((low_f, low_at, wq, wk, 4), (high_f, high_at, wv, wo, 6)):

        @pl.when(at < RING // 2)
        def _early(src=src, at=at, early=early, n=n):
            for copy in block_copies(src, at, early, n):
                copy.start()

        @pl.when(at >= RING // 2)
        def _late(src=src, at=at, late=late, n=n):
            for copy in block_copies(src, at, late, n):
                copy.start()

        later += block_copies(src, at, early, n)
    if last:
        for copy in rel_copies:
            copy.wait()
        for src, at, row, _ in blocks:
            rel_all[pl.ds(pl.multiple_of(at * REL_PIECE, 8), REL_PIECE), :] = src[REL, :]
            small_all[pl.ds(pl.multiple_of(8 * row, 8), 8), :] = src[REL.stop :, :]
        w_rel[0] = dot_tn(pos[...], rel_all[...].astype(BF16))
        finish_small(small_all, *small_outs)
    for copy in copies + later:
        copy.wait()


def unpack(step, meta, own_a, other_a, own_b, other_b, outs, earlier, pos, heads):
    given = [v for v in outs if not isinstance(v, jax.ShapeDtypeStruct)]
    width, ff = own_a.shape[1], outs[0].shape[2]
    last = pos is not None

    def f32(*dims):
        return shape(*dims, dtype=F32)

    extra = [f32(8, LANES)]
    scratch = [
        *[pltpu.VMEM((HEAD_ROWS, width), F32)] * 2,
        *[pltpu.VMEM((B_ROWS, width), F32)] * 2,
        pltpu.SemaphoreType.DMA((12,)),
    ]
    if last:
        by_head, line = f32(heads, 1, width // heads), f32(1, width)
        extra = [
            f32(1, width, width), by_head, by_head, by_head, f32(heads, 2, width // heads), line, line, f32(1, ff),
            line, line, line, f32(width),
        ]
        scratch += [
            pltpu.VMEM(pos.shape, F32), pltpu.VMEM((16 * RING, width), F32), pltpu.SemaphoreType.DMA((2,)),
        ]
    front = [meta, own_a, other_a, own_b, other_b] + ([pos] if last else [])
    results = pl.pallas_call(
        functools.partial(unpack_body, (step + RING - 1) % RING, last),
        out_shape=tuple(shape(*v.shape, dtype=v.dtype) for v in outs) + tuple(extra),
        in_specs=[SMEM_SPEC] + [VMEM_SPEC] * (len(front) - 1) + [ANY_SPEC] * (len(given) + len(earlier)),
        out_specs=tuple(ANY_SPEC for _ in outs) + (VMEM_SPEC,) * len(extra),
        input_output_aliases={len(front) + n: n for n in range(len(given))},
        scratch_shapes=scratch,
        compiler_params=params(),
        cost_estimate=cost(0, 8_000_000),
    )(*front, *given, *earlier)
    results, token = results[: len(outs)], results[len(outs) :]
    if not last:
        token = token[0]
    return results, token


def ring_steps(count):
    cycle = [(z, 0) for z in range(4)] + [(z, 1) for z in (3, 2, 1, 0)]
    steps = []
    for index in range(count):
        base, inside = index - index % GROUP, index % GROUP
        at = cycle.index((inside // 4, (inside // 2) % 2))
        z, y = cycle[(at + (1 if inside % 2 == 0 else -1)) % RING]
        steps.append((index, base + (z * 2 + y) * 2 + inside % 2))
    return steps


SECTION, DP = "section", "dp"


def swapped(value, axis, bit):
    count = lax.axis_size(axis)
    return lax.ppermute(value, axis, [(index, index ^ bit) for index in range(count)])


def position_table(total_rows, width_model, mem_rows, seg_rows):
    row_ids = np.arange(total_rows, dtype=np.float32)
    distance = np.float32(mem_rows + seg_rows - 1) - row_ids
    power = np.arange(0, width_model, 2, dtype=np.float32) / np.float32(width_model)
    freqs = np.float32(1.0) / np.power(np.float32(10000.0), power)
    angles = distance[:, None] * freqs[None, :]
    return np.concatenate([np.sin(angles), np.cos(angles)], axis=1).astype(np.float32)


def scratches(seg_rows, mem_rows, width, ff, heads):
    rows, key_rows, rel_rows = 2 * seg_rows, mem_rows + seg_rows, mem_rows + 2 * seg_rows
    vm, dma = pltpu.VMEM, pltpu.SemaphoreType.DMA
    vrow_b, vrow_f, square, wide = vm((rows, width), BF16), vm((rows, width), F32), vm((width, width), BF16), vm((rows, ff), BF16)
    weights_f = dict(fi=vm((width, ff), BF16), fo=vm((ff, width), BF16))
    weights_a = dict(wk=square, wq=square, wv=square, wo=square, rel=vm((rel_rows, width), BF16))
    probs_scratch = vm((heads, rows, key_rows), BF16)
    forward_scratch = dict(
        joined=vrow_b, stream=vrow_b, qc=vrow_b, qp=vrow_b, qs=vrow_b, k=vrow_b, v=vrow_b, mixed=vrow_b,
        midb=vrow_b, out=vrow_b, p=probs_scratch,
        pos=vm((heads // 2, 2 * rows, key_rows), F32),
        bias=vm((2, seg_rows, seg_rows), F32),
        mid_in=vrow_f, outer=vrow_f, act=wide, slope=wide,
        sem_in=dma((10,)),
        sem_first=dma((1,)),
        sem_out=dma((40,)),
        **weights_f, **weights_a,
    )
    backward_scratch = dict(
        outer=vrow_f, mid_in=vrow_f, cot=vrow_b, returned=vrow_b, e=vrow_b, ab=vrow_b, a=vrow_f, acc=vrow_f,
        u=wide, slope=wide, x=vrow_b, k=vrow_b, v=vrow_b, qc=vrow_b, qp=vrow_b, qs=vrow_b, qpf=vrow_b, dk=vrow_b,
        dv=vrow_b, dqb=vrow_b, out=vrow_b, p=probs_scratch, dq=vrow_f, dqp=vrow_f,
        drel=vm((rel_rows, width), F32),
        sums_t=vm((16, width), F32),
        sums=vm((8, width), F32),
        sem_tail=dma((1 + 3 * (ff // width),)),
        sem_first=dma((4,)),
        sem_head=dma((11,)),
        sem_out=dma((14,)),
        **weights_f, **weights_a,
    )
    return forward_scratch, backward_scratch


def shards(
    content_in, memory, mask_embed, doc_ids, orders, targets, slot_used,
    w_query, w_key, w_value, w_out, w_rel, bias_content, bias_position, bias_segment, seg_embed,
    norm1_gain, norm1_shift, ffn_in, ffn_in_bias, ffn_out, ffn_out_bias, norm2_gain, norm2_shift,
    content_cot, query_cot,
):
    slots, seg_rows, width = content_in.shape
    mem_rows = memory.shape[2]
    heads, dim = bias_content.shape[1:]
    ff = ffn_in.shape[2]
    key_rows, rows = mem_rows + seg_rows, 2 * seg_rows
    rel_rows = key_rows + seg_rows
    section = lax.axis_index(SECTION).astype(jnp.int32)
    dp = lax.axis_index(DP).astype(jnp.int32)
    dp_count = lax.axis_size(DP)
    inside = dp % GROUP
    at = jnp.where((inside // 2) % 2 == 0, inside // 4, RING - 1 - inside // 4)
    lane = jnp.arange(2 * RING + 2, dtype=jnp.int32)
    meta = jnp.where(
        lane < RING,
        (at - lane) & (RING - 1),
        jnp.where(
            lane < 2 * RING,
            (-at - lane) & (RING - 1),
            jnp.where(lane == META_CORE, dp % 2, section),
        ),
    )
    pos_b = jnp.asarray(position_table(rel_rows, width, mem_rows, seg_rows)).astype(BF16)
    small, rel = pl.pallas_call(
        prepare_body,
        out_shape=(shape(SMALL_ROWS, width, dtype=F32), shape(rel_rows, width)),
        compiler_params=params(),
    )(
        bias_content, bias_position, bias_segment,
        jnp.transpose(seg_embed[0], (1, 0, 2)), norm1_gain, norm1_shift, ffn_out_bias, norm2_gain,
        norm2_shift, mask_embed, ffn_in_bias, pos_b, w_rel,
    )

    row_b, row_f = shape(slots, rows, width), shape(slots, rows, width, dtype=F32)
    kept = dict(
        joined=row_b, stream=row_b, qc=row_b, qp=row_b, qs=row_b, k=row_b, v=row_b, mixed=row_b,
        p=shape(slots, heads, rows, key_rows),
        mid_in=row_f,
        outer=row_f,
        slope=shape(slots, rows, ff),
        me=shape(2, slots, rows, width),
        ua=shape(2, slots, rows, ff),
        content_out=shape(1, slots, seg_rows, width),
        query_out=shape(1, slots, seg_rows, width),
    )
    forward_scratch, backward_scratch = scratches(seg_rows, mem_rows, width, ff, heads)
    common = dict(meta=(SMEM_SPEC, meta), slot_used=(SMEM_SPEC, slot_used), **in_vmem(small=small))
    ids = in_vmem(docs=doc_ids, orders=orders, targets=targets)
    weights_attention = in_hbm(w_key=w_key, w_query=w_query, w_value=w_value, w_out=w_out, rel=rel)
    weights_ffn = in_hbm(ffn_in=ffn_in, ffn_out=ffn_out)
    sent = {}
    for call in range(4):
        layer, slot = call // 2, call % 2
        source = in_hbm(content_in=content_in) if layer == 0 else in_hbm(arrived=sent[slot])
        inputs = common | ids | in_hbm(memory=memory) | weights_attention | weights_ffn | source
        fresh = dict(sent=shape(rows, width)) if layer == 0 else {}
        kept, new = call_kernel(forward_body, layer, slot, inputs, kept, fresh, forward_scratch)
        if layer == 0:
            sent[slot] = lax.ppermute(new.popitem()[1], SECTION, [(0, 1)])
    kept = types.SimpleNamespace(**kept)

    grads = dict(
        me=kept.me, ua=kept.ua, ab=row_b, dk=row_b, dv=row_b, dq=row_b,
        drel=shape(slots, rel_rows, width, dtype=F32),
        input_grad=shape(1, slots, seg_rows, width),
        sums=shape(slots, SUM_ROWS, width, dtype=F32),
    )
    flat = lambda v: v.reshape(v.shape[:-3] + (slots * rows, v.shape[-1]))
    returned = {}
    for call in range(4):
        layer, slot = 1 - call // 2, 1 - call % 2
        inputs = common | in_vmem(docs=doc_ids) | weights_attention | weights_ffn | in_hbm(
            outer=kept.outer, slope=kept.slope, mid_in=kept.mid_in, content_cot=content_cot, query_cot=query_cot,
            p=kept.p, k=kept.k, v=kept.v, qc=kept.qc, qp=kept.qp, qs=kept.qs,
        )
        if layer == 0:
            inputs |= in_hbm(returned=returned[slot])
        fresh = dict(sent=shape(rows, width)) if layer == 1 else {}
        grads, new = call_kernel(backward_body, layer, slot, inputs, grads, fresh, backward_scratch)
        if layer == 1:
            returned[slot] = lax.ppermute(new.popitem()[1], SECTION, [(1, 0)])
    grads = types.SimpleNamespace(**grads)

    me, ua = flat(grads.me), flat(grads.ua)
    operands = [flat(v) for v in (kept.stream, kept.joined, kept.mixed, grads.dq, grads.dk, grads.dv, grads.ab)]
    operands += [grads.drel, grads.sums]
    own_a, own_b, *handed = pieces(meta, me, ua, operands)
    first_a, first_b = [swapped(value, DP, 1) for value in handed[:2]]
    first_a, first_b, *rest = lax.optimization_barrier((first_a, first_b, *handed[2:]))
    rest_a, rest_b = [swapped(value, DP, 1) for value in rest]
    own, others = (own_a, own_b), ((first_a, rest_a), (first_b, rest_b))

    def add(ring, step, came=None):
        other = others[ring][0][0] if step == 0 else others[ring][1][step - 1]
        total = own[ring][step].astype(F32) + other.astype(F32)
        return (total if came is None else total + came.astype(F32)).astype(BF16)

    acc = [add(0, 0), add(1, 0)]

    steps = ring_steps(dp_count)
    for step in range(1, RING):
        came = [lax.ppermute(acc[ring], DP, steps) for ring in range(2)]
        acc = [add(ring, step, came[ring]) for ring in range(2)]
    acc_a, acc_b = acc
    bit = GROUP
    while bit < dp_count:
        acc_a = (acc_a.astype(F32) + swapped(acc_a, DP, bit).astype(F32)).astype(BF16)
        acc_b = (acc_b.astype(F32) + swapped(acc_b, DP, bit).astype(F32)).astype(BF16)
        bit *= 2
    spare = lax.slice_in_dim(acc_b, REL.stop, B_ROWS, axis=0)
    came = swapped(spare, SECTION, 1)
    holds = (meta[META_CORE] == MASK_ROW % 2) & (meta[2 * RING - 1] == MASK_ROW // 2)
    row = lax.broadcasted_iota(jnp.int32, spare.shape, 0)
    spare = jnp.where(holds & (row == 0), (spare.astype(F32) + came.astype(F32)).astype(BF16), spare)
    acc_b = lax.dynamic_update_slice_in_dim(acc_b, spare, REL.stop, axis=0)
    ffn_outs = [shape(1, width, ff, dtype=F32), shape(1, ff, width, dtype=F32)]
    rest_outs = [shape(1, width, width, dtype=F32) for _ in range(4)] + [shape(rel_rows, width, dtype=F32)]
    rest_outs.append(shape(16 * RING, width, dtype=F32))
    tokens = []
    outs = ffn_outs + rest_outs
    for step in range(RING):
        if step:
            acc_a = lax.ppermute(acc_a, DP, steps)
            acc_b = lax.ppermute(acc_b, DP, steps)
        handed_a, handed_b, before = acc_a, acc_b, []
        if step > 1:
            handed_a, before_a = lax.optimization_barrier((acc_a, tokens[step - 2]))
            before.append(before_a)
        if step:
            handed_b, before_b = lax.optimization_barrier((acc_b, tokens[step - 1]))
            before.append(before_b)
        outs, token = unpack(
            step, meta, acc_a, swapped(handed_a, DP, 1), acc_b, swapped(handed_b, DP, 1), outs, before,
            pos_b if step == RING - 1 else None, heads,
        )
        tokens.append(token)
    ffn_outs, rest_outs = outs[:2], outs[2:]
    (
        grad_w_rel, grad_bc, grad_bp, grad_bs, grad_seg, grad_n1g, grad_n1s, grad_fib, grad_fob, grad_n2g, grad_n2s,
        mask_grad,
    ) = tokens[-1]
    grad_ffn_in, grad_ffn_out = ffn_outs
    grad_w_query, grad_w_key, grad_w_value, grad_w_out = rest_outs[:4]
    one_layer = lambda v: v.reshape(1, heads, dim)
    return (
        kept.content_out, kept.query_out, grads.input_grad, mask_grad,
        grad_w_query, grad_w_key, grad_w_value, grad_w_out, grad_w_rel,
        one_layer(grad_bc), one_layer(grad_bp), one_layer(grad_bs), jnp.transpose(grad_seg, (1, 0, 2))[None],
        grad_n1g, grad_n1s, grad_ffn_in, grad_fib, grad_ffn_out, grad_fob, grad_n2g, grad_n2s,
    )


def solution(mesh):
    two, three, four = P(SECTION, None), P(SECTION, None, None), P(SECTION, None, None, None)
    rows = P(SECTION, DP, None, None)
    return jax.shard_map(
        shards,
        mesh=mesh,
        in_specs=(
            P(DP, None, None), rows, P(), P(DP, None), P(DP, None), P(DP, None), P(DP), *[three] * 8, four,
            two, two, three, two, three, two, two, two, rows, rows,
        ),
        out_specs=(
            rows, rows, rows, P(), *[three] * 8, four, two, two, three, two, three, two, two, two,
        ),
        check_vma=False,
    )
```

```python
import functools
import types

import jax
import jax.numpy as jnp
import numpy as np
from jax import lax
from jax.experimental import pallas as pl
from jax.experimental.pallas import tpu as pltpu
from jax.sharding import PartitionSpec as P

BF16 = jnp.bfloat16
F32 = jnp.float32
NEG_FILL = -1e30
NORM_EPS = 1e-05
GELU_A = 0.7978845608028654
GELU_B = 0.044715
VMEM_LIMIT = 60 * 1024 * 1024
LANES = 128
LAYER_FLOPS = 9_000_000_000
RING = 8
META_CORE, META_SECTION = 2 * RING, 2 * RING + 1

ROW_BC, ROW_BP, ROW_BS, ROW_SEG0, ROW_SEG1 = 0, 1, 2, 3, 4
ROW_N1G, ROW_N1S, ROW_FOB, ROW_N2G, ROW_N2S, ROW_MASK, ROW_FIB = 5, 6, 7, 8, 9, 10, 11
SMALL_ROWS = 16


def dot_nn(left, right):
    return jnp.dot(left, right, preferred_element_type=F32)


def dot_nt(left, right):
    return lax.dot_general(left, right, (((1,), (1,)), ((), ())), preferred_element_type=F32)


def dot_tn(left, right):
    return lax.dot_general(left, right, (((0,), (0,)), ((), ())), preferred_element_type=F32)


def col_sum(block):
    return jnp.sum(block, axis=0, keepdims=True)


def norm_parts(rows):
    center = jnp.mean(rows, axis=-1, keepdims=True)
    offset = rows - center
    spread = jnp.mean(offset * offset, axis=-1, keepdims=True)
    scale = lax.rsqrt(spread + NORM_EPS)
    return offset * scale, scale


def norm_back(grad, unit, scale, gain):
    inner = grad * gain
    mean_inner = jnp.mean(inner, axis=-1, keepdims=True)
    mean_cross = jnp.mean(inner * unit, axis=-1, keepdims=True)
    return (inner - mean_inner - unit * mean_cross) * scale


def half_masks():
    lane = lax.broadcasted_iota(jnp.int32, (1, LANES), 1)
    low = lane < LANES // 2
    return low, low.astype(F32).astype(BF16), (~low).astype(F32).astype(BF16)


def stack_heads(block, low_b, high_b):
    return jnp.concatenate([block * low_b, block * high_b], axis=0)


def copy_in(pairs, sems):
    copies = [
        pltpu.make_async_copy(src, dst, sems.at[n]) for n, (src, dst) in enumerate(pairs)
    ]
    for copy in copies:
        copy.start()
    return copies


def name_refs(names_in, names_out, names_scratch, refs):
    groups, start = [], 0
    for names in (names_in, names_out, names_scratch):
        groups.append(types.SimpleNamespace(**dict(zip(names, refs[start : start + len(names)]))))
        start += len(names)
    return groups


def forward_body(section, slot, names_in, names_out, names_scratch, *refs):
    r, o, s = name_refs(names_in, names_out, names_scratch, refs)
    meta = r.meta
    seg_rows, width = s.stream.shape[0] // 2, s.stream.shape[1]
    key_rows = s.joined.shape[0]
    pairs_count = width // LANES
    ff = s.act.shape[1]
    score_scale = 0.125

    @pl.when(meta[META_SECTION] == section)
    def _run():
        sem_in, sem_out = s.sem_in, s.sem_out
        mem_rows = key_rows - seg_rows
        x_src = r.content_in.at[slot] if section == 0 else r.arrived.at[pl.ds(0, seg_rows)]
        loads = [
            (r.memory.at[0, slot], s.joined.at[pl.ds(0, mem_rows)]),
            (x_src, s.joined.at[pl.ds(mem_rows, seg_rows)]),
            (x_src, s.stream.at[pl.ds(0, seg_rows)]),
            (r.w_key.at[0], s.wk),
            (r.w_query.at[0], s.wq),
            (r.rel, s.rel),
            (r.w_value.at[0], s.wv),
            (r.w_out.at[0], s.wo),
            (r.ffn_in.at[0], s.fi),
            (r.ffn_out.at[0], s.fo),
        ]
        moves = []
        if section == 1:
            query_rows = pl.ds(seg_rows, seg_rows)
            moves = copy_in([(r.arrived.at[query_rows], s.stream.at[query_rows])], s.sem_first)
        moves = copy_in(loads, sem_in) + moves
        stores = []

        def store(src, dst):
            copy = pltpu.make_async_copy(src, dst, sem_out.at[len(stores)])
            copy.start()
            stores.append(copy)

        small = r.small
        used = (r.slot_used[slot] > 0).astype(jnp.int32).astype(F32)
        if section == 0:
            s.stream[seg_rows:, :] = jnp.broadcast_to(
                small[ROW_MASK : ROW_MASK + 1, :], (seg_rows, width)
            ).astype(BF16)
        square = (seg_rows, seg_rows)
        doc = jnp.broadcast_to(r.docs[slot : slot + 1, :].astype(F32), square)
        order = jnp.broadcast_to(r.orders[slot : slot + 1, :].astype(F32), square)
        target = jnp.broadcast_to(r.targets[slot : slot + 1, :].astype(F32), square)
        same = doc == doc.T
        visible = same & ((target == 0.0) | (order <= order.T))
        row_id = lax.broadcasted_iota(jnp.int32, square, 0)
        col_id = lax.broadcasted_iota(jnp.int32, square, 1)
        s.bias[0] = jnp.where(visible, 0.0, NEG_FILL)
        s.bias[1] = jnp.where(visible & (row_id != col_id), 0.0, NEG_FILL)

        for n in (0, 1, 3):
            moves[n].wait()
        s.k[...] = dot_nn(s.joined[...], s.wk[...]).astype(BF16)
        store(s.k, o.k.at[slot])
        store(s.joined, o.joined.at[slot])
        moves[2].wait()
        if section == 1:
            moves[10].wait()
        store(s.stream, o.stream.at[slot])
        moves[4].wait()
        queries = dot_nn(s.stream[...], s.wq[...])
        for block, kept, row in ((s.qc, o.qc, ROW_BC), (s.qp, o.qp, ROW_BP), (s.qs, o.qs, ROW_BS)):
            with_bias = (queries + small[row : row + 1, :]).astype(BF16)
            block[...] = (with_bias.astype(F32) * score_scale).astype(BF16)
            store(block, kept.at[slot])
        moves[6].wait()
        s.v[...] = dot_nn(s.joined[...], s.wv[...]).astype(BF16)
        store(s.v, o.v.at[slot])
        moves[5].wait()

        low, low_b, high_b = half_masks()
        bias_by_stream = [s.bias[0], s.bias[1]]
        inside = col_id <= row_id
        for pair in range(pairs_count):
            sl = slice(pair * LANES, (pair + 1) * LANES)
            position = dot_nt(stack_heads(s.qp[:, sl], low_b, high_b), s.rel[:, sl])
            for part in range(4):
                base = part * seg_rows
                turned = [
                    pltpu.roll(
                        position[base : base + seg_rows, n * LANES : (n + 1) * LANES],
                        1, axis=1, stride=1, stride_axis=0,
                    )
                    for n in range(3)
                ]
                rolled = jnp.concatenate(
                    [jnp.where(inside, turned[n], turned[n + 1]) for n in range(2)], axis=1
                )
                s.pos[pair, base : base + seg_rows, :] = rolled
        for pair in range(pairs_count):
            sl = slice(pair * LANES, (pair + 1) * LANES)
            content = dot_nt(stack_heads(s.qc[:, sl], low_b, high_b), s.k[:, sl])
            segments = jnp.concatenate(
                [
                    jnp.broadcast_to(small[row : row + 1, sl].astype(BF16) * mask, (LANES, LANES))
                    for mask in (low_b, high_b)
                    for row in (ROW_SEG0, ROW_SEG1)
                ],
                axis=0,
            )
            pieces_wide = dot_nt(s.qs[:, sl], segments)
            probs_pair = []
            for head in range(2):
                probs_streams = []
                for stream in range(2):
                    base = (2 * head + stream) * seg_rows
                    rows = slice(stream * seg_rows, (stream + 1) * seg_rows)
                    same_part = pieces_wide[rows, 2 * head * LANES : (2 * head + 1) * LANES]
                    other_part = pieces_wide[rows, (2 * head + 1) * LANES : (2 * head + 2) * LANES]
                    body = content[base : base + seg_rows, :] + s.pos[pair, base : base + seg_rows, :]
                    left = body[:, :mem_rows] + other_part
                    right = body[:, mem_rows:] + jnp.where(same, same_part, other_part) + bias_by_stream[stream]
                    peak = jnp.max(jnp.maximum(left, right), axis=-1, keepdims=True)
                    left = jnp.exp(left - peak)
                    right = jnp.exp(right - peak)
                    total = jnp.sum(left + right, axis=-1, keepdims=True)
                    inverse = 1.0 / total
                    probs_streams.append(
                        jnp.concatenate([left * inverse, right * inverse], axis=1).astype(BF16)
                    )
                probs = jnp.concatenate(probs_streams, axis=0)
                s.p[2 * pair + head] = probs
                store(s.p.at[2 * pair + head], o.p.at[slot, 2 * pair + head])
                probs_pair.append(probs)
            mixed = dot_nn(
                jnp.concatenate(probs_pair, axis=1), stack_heads(s.v[:, sl], low_b, high_b)
            )
            s.mixed[:, sl] = mixed.astype(BF16)
        store(s.mixed, o.mixed.at[slot])

        moves[7].wait()
        middle_in = dot_nn(s.mixed[...], s.wo[...]) + s.stream[...].astype(F32)
        s.mid_in[...] = middle_in
        store(s.mid_in, o.mid_in.at[slot])
        unit, _ = norm_parts(middle_in)
        middle = unit * small[ROW_N1G : ROW_N1G + 1, :] + small[ROW_N1S : ROW_N1S + 1, :]
        s.midb[...] = middle.astype(BF16)
        store(s.midb, o.me.at[0, slot])
        s.outer[...] = middle + small[ROW_FOB : ROW_FOB + 1, :]
        moves[8].wait()
        moves[9].wait()
        for step in range(ff // width):
            cols = slice(step * width, (step + 1) * width)
            inner = (
                dot_nn(s.midb[...], s.fi[:, cols])
                + small[ROW_FIB + step : ROW_FIB + step + 1, :]
            )
            square_in = inner * inner
            wave = jnp.tanh(GELU_A * inner * (1.0 + GELU_B * square_in))
            half = 0.5 * (1.0 + wave)
            active = (inner * half).astype(BF16)
            slope = half + (0.5 * GELU_A) * inner * (1.0 - wave * wave) * (1.0 + 3.0 * GELU_B * square_in)
            s.act[:, cols] = active
            s.slope[:, cols] = slope.astype(BF16)
            part = pl.ds(step * width, width)
            store(s.act.at[:, part], o.ua.at[1, slot, :, part])
            store(s.slope.at[:, part], o.slope.at[slot, :, part])
            s.outer[...] += dot_nn(active, s.fo[cols, :])
        store(s.outer, o.outer.at[slot])
        unit, _ = norm_parts(s.outer[...])
        result = unit * small[ROW_N2G : ROW_N2G + 1, :] + small[ROW_N2S : ROW_N2S + 1, :]
        s.out[...] = (result * used).astype(BF16)
        store(s.out.at[pl.ds(0, seg_rows)], o.content_out.at[0, slot])
        store(s.out.at[pl.ds(seg_rows, seg_rows)], o.query_out.at[0, slot])
        if section == 0:
            store(s.out, o.sent)
        for copy in stores:
            copy.wait()


def backward_body(section, slot, names_in, names_out, names_scratch, *refs):
    r, o, s = name_refs(names_in, names_out, names_scratch, refs)
    meta = r.meta
    rows, width = s.a.shape
    seg_rows = rows // 2
    ff = s.slope.shape[1]
    key_rows = s.k.shape[0]
    mem_rows = key_rows - seg_rows
    pairs_count = width // LANES
    score_scale = 0.125

    @pl.when(meta[META_SECTION] == section)
    def _run():
        first_loads = [
            (r.content_cot.at[0, slot], s.cot.at[pl.ds(0, seg_rows)]),
            (r.query_cot.at[0, slot], s.cot.at[pl.ds(seg_rows, seg_rows)]),
            (r.outer.at[slot], s.outer),
        ]
        if section == 0:
            first_loads.append((r.returned, s.returned))
        first = copy_in(first_loads, s.sem_first)
        loads = []
        for step in range(ff // width):
            part = pl.ds(step * width, width)
            loads.append((r.ffn_out.at[0, part], s.fo.at[part]))
            loads.append((r.slope.at[slot, :, part], s.slope.at[:, part]))
            loads.append((r.ffn_in.at[0, :, part], s.fi.at[:, part]))
        loads.append((r.mid_in.at[slot], s.mid_in))
        head_loads = [
            (r.w_out.at[0], s.wo),
            (r.v.at[slot], s.v),
            (r.p.at[slot], s.p),
            (r.k.at[slot], s.k),
            (r.qc.at[slot], s.qc),
            (r.qp.at[slot], s.qp),
            (r.qs.at[slot], s.qs),
            (r.rel, s.rel),
            (r.w_query.at[0], s.wq),
            (r.w_key.at[0], s.wk),
            (r.w_value.at[0], s.wv),
        ]
        stores = []

        def store(src, dst):
            copy = pltpu.make_async_copy(src, dst, s.sem_out.at[len(stores)])
            copy.start()
            stores.append(copy)

        small = r.small
        used = (r.slot_used[slot] > 0).astype(jnp.int32).astype(F32)
        for move in first:
            move.wait()
        moves = copy_in(loads, s.sem_tail)
        grad = s.cot[...].astype(F32) * used
        if section == 0:
            grad = grad + s.returned[...].astype(F32)
        unit, scale = norm_parts(s.outer[...])
        out = s.sums_t
        out[...] = jnp.zeros_like(out)
        out[4:5, :] = col_sum(grad * unit)
        out[5:6, :] = col_sum(grad)
        grad_outer = norm_back(grad, unit, scale, small[ROW_N2G : ROW_N2G + 1, :])
        s.e[...] = grad_outer.astype(BF16)
        store(s.e, o.me.at[1, slot])
        out[3:4, :] = col_sum(s.e[...].astype(F32))
        s.acc[...] = grad_outer
        for step in range(ff // width):
            for move in moves[3 * step : 3 * step + 3]:
                move.wait()
            cols = slice(step * width, (step + 1) * width)
            if step == 1:
                head_moves = copy_in(head_loads, s.sem_head)
            grad_active = dot_nt(s.e[...], s.fo[cols, :])
            inner_b = (s.slope[:, cols].astype(F32) * grad_active).astype(BF16)
            s.u[:, cols] = inner_b
            out[8 + step : 9 + step, :] = col_sum(inner_b.astype(F32))
            s.acc[...] += dot_nt(inner_b, s.fi[:, cols])
        store(s.u, o.ua.at[0, slot])
        moves[-1].wait()
        unit, scale = norm_parts(s.mid_in[...])
        grad = s.acc[...]
        out[1:2, :] = col_sum(grad * unit)
        out[2:3, :] = col_sum(grad)
        s.a[...] = norm_back(grad, unit, scale, small[ROW_N1G : ROW_N1G + 1, :])
        s.ab[...] = s.a[...].astype(BF16)
        store(s.ab, o.ab.at[slot])
        store(s.sums_t, o.sums.at[slot, pl.ds(8, 16)])

        square = (seg_rows, seg_rows)
        doc = jnp.broadcast_to(r.docs[slot : slot + 1, :].astype(F32), square)
        same_one = (doc == doc.T).astype(F32)
        same = jnp.concatenate([same_one, same_one], axis=0)
        flip_rows = lax.broadcasted_iota(jnp.int32, (rows, rows), 0)
        flip_cols = lax.broadcasted_iota(jnp.int32, (rows, rows), 1)
        flipped_to = jnp.where(flip_rows < seg_rows, seg_rows - 1, rows + seg_rows - 1) - flip_rows
        flip = (flip_cols == flipped_to).astype(F32).astype(BF16)
        out = s.sums
        out[...] = jnp.zeros_like(out)
        head_moves[0].wait()
        s.x[...] = dot_nt(s.ab[...], s.wo[...]).astype(BF16)
        for n in (1, 2, 3, 4, 5, 6, 7):
            head_moves[n].wait()
        s.qpf[...] = dot_nn(flip, s.qp[...]).astype(BF16)

        low, low_b, high_b = half_masks()
        past = lax.broadcasted_iota(jnp.int32, square, 1) >= lax.broadcasted_iota(jnp.int32, square, 0)
        for pair in range(pairs_count):
            sl = slice(pair * LANES, (pair + 1) * LANES)
            grads_mixed = stack_heads(s.x[:, sl], low_b, high_b)
            grad_probs = dot_nt(grads_mixed, s.v[:, sl])
            scores_b = []
            same_sums, other_sums = [], []
            for head in range(2):
                probs = s.p[2 * pair + head].astype(F32)
                product = probs * grad_probs[head * rows : (head + 1) * rows, :]
                delta = jnp.sum(product, axis=-1, keepdims=True)
                rounded = (product - probs * delta).astype(BF16)
                scores_b.append(rounded)
                wide = rounded.astype(F32)
                right = wide[:, mem_rows:] * same
                same_sum = jnp.sum(right, axis=-1, keepdims=True)
                same_sums.append(same_sum)
                other_sums.append(
                    jnp.sum(wide[:, :mem_rows] + (wide[:, mem_rows:] - right), axis=-1, keepdims=True)
                )
            stacked = jnp.concatenate(scores_b, axis=0)
            beside = jnp.concatenate(scores_b, axis=1)
            probs_stacked = jnp.concatenate([s.p[2 * pair], s.p[2 * pair + 1]], axis=0)
            s.dv[:, sl] = dot_tn(probs_stacked, grads_mixed).astype(BF16)
            s.dk[:, sl] = dot_tn(stack_heads(s.qc[:, sl], low_b, high_b), stacked).T.astype(BF16)
            grad_content = dot_nn(beside, stack_heads(s.k[:, sl], low_b, high_b)) * score_scale
            same_sel = jnp.where(low, same_sums[0], same_sums[1])
            other_sel = jnp.where(low, other_sums[0], other_sums[1])
            seg0 = small[ROW_SEG0 : ROW_SEG0 + 1, sl]
            seg1 = small[ROW_SEG1 : ROW_SEG1 + 1, sl]
            grad_segment = (same_sel * seg0 + other_sel * seg1) * score_scale
            qs = s.qs[:, sl].astype(F32)
            out[0:1, sl] = col_sum(grad_content)
            out[2:3, sl] = col_sum(grad_segment)
            out[3:4, sl] = col_sum(same_sel * qs)
            out[4:5, sl] = col_sum(other_sel * qs)
            s.dq[:, sl] = grad_content + grad_segment
            turned = dot_nn(flip, beside)
            shifted_heads = []
            for head in range(2):
                parts = []
                for stream in range(2):
                    blocks = [
                        pltpu.roll(
                            turned[
                                stream * seg_rows : (stream + 1) * seg_rows,
                                head * key_rows + n * LANES : head * key_rows + (n + 1) * LANES,
                            ],
                            0, axis=1, stride=1, stride_axis=0,
                        )
                        for n in range(2)
                    ]
                    blocks = [
                        jnp.where(past, blocks[0], 0.0),
                        jnp.where(past, blocks[1], blocks[0]),
                        jnp.where(past, 0.0, blocks[1]),
                    ]
                    parts.append(jnp.concatenate(blocks, axis=1).astype(BF16))
                shifted_heads.append(jnp.concatenate(parts, axis=0))
            grad_position = (
                dot_nn(
                    jnp.concatenate(shifted_heads, axis=1),
                    stack_heads(s.rel[:, sl], low_b, high_b),
                )
                * score_scale
            )
            out[1:2, sl] = col_sum(grad_position)
            s.dqp[:, sl] = grad_position
            s.drel[:, sl] = dot_tn(
                jnp.concatenate(shifted_heads, axis=0),
                stack_heads(s.qpf[:, sl], low_b, high_b),
            )
        store(s.dk, o.dk.at[slot])
        store(s.dv, o.dv.at[slot])
        store(s.drel, o.drel.at[slot])
        grad_position = s.dqp[...]
        position_high = grad_position.astype(BF16)
        position_low = (grad_position - position_high.astype(F32)).astype(BF16)
        grad_queries = s.dq[...] + dot_nn(flip, position_high) + dot_nn(flip, position_low)
        s.dqb[...] = grad_queries.astype(BF16)
        store(s.dqb, o.dq.at[slot])
        for n in (8, 9, 10):
            head_moves[n].wait()
        grad_rows = s.a[...] + dot_nt(s.dqb[...], s.wq[...])
        grad_content = (
            grad_rows[:seg_rows, :]
            + dot_nt(s.dk[mem_rows:, :], s.wk[...])
            + dot_nt(s.dv[mem_rows:, :], s.wv[...])
        )
        grad_query = grad_rows[seg_rows:, :]
        s.out[:seg_rows, :] = grad_content.astype(BF16)
        s.out[seg_rows:, :] = grad_query.astype(BF16)
        store(s.out.at[pl.ds(0, seg_rows)], o.input_grad.at[0, slot])
        if section == 1:
            store(s.out, o.sent)
        if section == 0:
            out[5:6, :] = col_sum(grad_query)
        store(s.sums, o.sums.at[slot, pl.ds(0, 8)])
        for copy in stores:
            copy.wait()


ANY_SPEC = pl.BlockSpec(memory_space=pltpu.HBM)
SMEM_SPEC = pl.BlockSpec(memory_space=pltpu.SMEM)
VMEM_SPEC = pl.BlockSpec(memory_space=pltpu.VMEM)


def call_kernel(body, section, slot, inputs, carried, fresh, scratch):
    names_in = list(inputs)
    arrays = [inputs[n][1] for n in names_in]
    specs = [inputs[n][0] for n in names_in]
    aliases = {}
    names_out = list(carried) + list(fresh)
    out_shapes = []
    for position, key in enumerate(carried):
        value = carried[key]
        out_shapes.append(jax.ShapeDtypeStruct(value.shape, value.dtype))
        if not isinstance(value, jax.ShapeDtypeStruct):
            aliases[len(arrays)] = position
            arrays.append(value)
            specs.append(ANY_SPEC)
            names_in.append(key + "_")
    out_shapes += [fresh[key] for key in fresh]
    results = pl.pallas_call(
        functools.partial(body, section, slot, names_in, names_out, list(scratch)),
        out_shape=tuple(out_shapes),
        in_specs=specs,
        out_specs=tuple(ANY_SPEC for _ in out_shapes),
        scratch_shapes=list(scratch.values()),
        input_output_aliases=aliases,
        compiler_params=pltpu.CompilerParams(vmem_limit_bytes=VMEM_LIMIT),
        cost_estimate=pl.CostEstimate(flops=LAYER_FLOPS, bytes_accessed=20_000_000, transcendentals=0),
    )(*arrays)
    named = dict(zip(names_out, results))
    return {k: named[k] for k in carried}, {k: named[k] for k in fresh}


def in_hbm(**arrays):
    return {key: (ANY_SPEC, value) for key, value in arrays.items()}


def in_vmem(**arrays):
    return {key: (VMEM_SPEC, value) for key, value in arrays.items()}


def params():
    return pltpu.CompilerParams(vmem_limit_bytes=VMEM_LIMIT)


def cost(flops, moved):
    return pl.CostEstimate(flops=flops, bytes_accessed=moved, transcendentals=0)


def shape(*dims, dtype=BF16):
    return jax.ShapeDtypeStruct(dims, dtype)


def prepare_body(bc, bp, bs, seg, n1g, n1s, fob, n2g, n2s, mask, fib, pos, w_rel, small, rel):
    heads, dim = bc.shape[1:]
    width = heads * dim
    wide = [(row, value[0].astype(F32)) for row, value in ((ROW_BC, bc), (ROW_BP, bp), (ROW_BS, bs))]
    for head in range(heads):
        cols = slice(head * dim, (head + 1) * dim)
        for row, value in wide:
            small[row : row + 1, cols] = value[head : head + 1, :]
        small[ROW_SEG0 : ROW_SEG1 + 1, cols] = seg[head].astype(F32)
    for row, value in (
        (ROW_N1G, n1g), (ROW_N1S, n1s), (ROW_FOB, fob), (ROW_N2G, n2g), (ROW_N2S, n2s),
    ):
        small[row : row + 1, :] = value[...].astype(F32)
    small[ROW_MASK : ROW_MASK + 1, :] = mask[...].astype(F32).reshape(1, width)
    for step in range(4):
        small[ROW_FIB + step : ROW_FIB + step + 1, :] = fib[:, step * width : (step + 1) * width].astype(F32)
    small[SMALL_ROWS - 1 : SMALL_ROWS, :] = jnp.zeros((1, width), F32)
    rel[...] = dot_nn(pos[...], w_rel[0]).astype(BF16)


GROUP = 16
SUM_ROWS = 24
MASK_ROW = 5
HALF = 384
HEAD_ROWS = 320
REST_ROWS = HALF - HEAD_ROWS
REL_PIECE = 24
BLOCK = slice(REST_ROWS, REST_ROWS + HALF // 2)
REL = slice(BLOCK.stop, BLOCK.stop + REL_PIECE)
B_ROWS = BLOCK.stop + 32


def lane_slice(start, size):
    return pl.ds(pl.multiple_of(start, LANES), size)


def block_rows(index, size):
    return pl.ds(pl.multiple_of(index * size, size), size)


def pieces_body(meta, me, ua, stream, joined, mixed, dq, dk, dv, ab, drel, sums, *refs):
    own_a, own_b, first_a, first_b, other_a, other_b = refs[:6]
    vme, vua, vs, vj, vmix, vdq, vdk, vdv, vab, rel, small, stage_a, stage_b, sems, out_sems = refs[6:]
    core, count = meta[META_CORE], RING
    width = vs.shape[1]
    part = width

    loads = [(me.at[0], vme.at[0])]
    for half in range(2):
        for n in range(vua.shape[2] // part):
            cols = pl.ds(n * part, part)
            loads.append((ua.at[half, :, cols], vua.at[half, :, cols]))
        if half == 0:
            loads.append((me.at[1], vme.at[1]))
    blocks_from = len(loads)
    loads += [
        (stream, vs), (dq, vdq), (joined, vj), (dk, vdk), (dv, vdv), (mixed, vmix), (ab, vab), (drel, rel), (sums, small),
    ]
    moves = copy_in(loads, sems)
    moves[0].wait()
    writes = []

    def put(src, owner, step, own, first, other):
        sem = out_sems.at[len(writes)]
        mine = core == owner
        pl.when(mine)(lambda: pltpu.make_async_copy(src, own.at[step], sem).start())
        pl.when(~mine & (step == 0))(lambda: pltpu.make_async_copy(src, first.at[0], sem).start())
        pl.when(~mine & (step != 0))(
            lambda: pltpu.make_async_copy(src, other.at[jnp.maximum(step, 1) - 1], sem).start()
        )
        writes.append(pltpu.make_async_copy(src, own.at[step], sem))

    def step_of(owner, k):
        return (meta[owner * RING] - k) & (RING - 1)

    for owner in range(2):
        base = 1 + owner * (vua.shape[2] // part + 1)
        if owner == 1:
            moves[base - 1].wait()
        for k in range(count):
            if k % 2 == 0:
                moves[base + k // 2].wait()
            if owner == 0:
                lhs = vme[0, :, (k % 2) * HALF : (k % 2 + 1) * HALF]
                rhs = vua[0, :, (k // 2) * width : (k // 2 + 1) * width]
            else:
                lhs, rhs = vua[1, :, k * HALF : (k + 1) * HALF], vme[1]
            whole = dot_tn(lhs, rhs).astype(BF16)
            stage_a[owner, k] = whole[:HEAD_ROWS]
            stage_b[owner, k, :REST_ROWS] = whole[HEAD_ROWS:]
            put(stage_a.at[owner, k], owner, step_of(owner, k), own_a, first_a, other_a)
    for move in moves[blocks_from:]:
        move.wait()
    for owner in range(2):
        for k in range(count):
            left, right = (((vs, vdq), (vj, vdk)), ((vj, vdv), (vmix, vab)))[owner][k // 4]
            inside = k % 4
            value = dot_tn(
                left[:, (inside // 2) * HALF : (inside // 2 + 1) * HALF],
                right[:, (inside % 2) * HALF : (inside % 2 + 1) * HALF],
            ).astype(BF16)
            stage_b[owner, k, BLOCK.start : BLOCK.stop, :HALF] = value[: HALF // 2]
            stage_b[owner, k, BLOCK.start : BLOCK.stop, HALF:] = value[HALF // 2 :]
            at = (owner * RING + k) * REL_PIECE
            row = 2 * k + owner
            rows = [
                small[0, n : n + 1, :] + small[1, n : n + 1, :] for n in (row, min(row + 2 * RING, SUM_ROWS - 1))
            ]
            blank = jnp.zeros((B_ROWS - REL.stop - 2, width), F32)
            stage_b[owner, k, BLOCK.stop :] = jnp.concatenate(
                [rel[0, at : at + REL_PIECE, :] + rel[1, at : at + REL_PIECE, :], *rows, blank], axis=0
            ).astype(BF16)
            put(stage_b.at[owner, k], owner, step_of(owner, k), own_b, first_b, other_b)
    for copy in writes:
        copy.wait()


def pieces(meta, me, ua, operands):
    rows, width = operands[0].shape
    ff = ua.shape[2]

    def vm(*dims, dtype=BF16):
        return pltpu.VMEM(dims, dtype)

    return pl.pallas_call(
        pieces_body,
        out_shape=[
            shape(count, size, width) for count in (RING, 1, RING - 1) for size in (HEAD_ROWS, B_ROWS)
        ],
        in_specs=[SMEM_SPEC] + [ANY_SPEC] * (2 + len(operands)),
        out_specs=[ANY_SPEC] * 6,
        scratch_shapes=[
            vm(2, rows, width), vm(2, rows, ff), *[vm(rows, width)] * 7,
            vm(*operands[-2].shape, dtype=F32), vm(*operands[-1].shape, dtype=F32),
            vm(2, RING, HEAD_ROWS, width), vm(2, RING, B_ROWS, width),
            pltpu.SemaphoreType.DMA((11 + 2 * (ff // width),)), pltpu.SemaphoreType.DMA((4 * RING,)),
        ],
        compiler_params=params(),
        cost_estimate=cost(6 * rows * HALF * width * RING, 30_000_000),
    )(meta, me, ua, *operands)


def by_core(meta, own, other, low_f, high_f):
    low = meta[META_CORE] == 0

    @pl.when(low)
    def _low():
        low_f[...] = own[...].astype(F32)
        high_f[...] = other[...].astype(F32)

    @pl.when(~low)
    def _high():
        low_f[...] = other[...].astype(F32)
        high_f[...] = own[...].astype(F32)


def ffn_places(fi, fo, low_at, high_at, first, count):
    width = fo.shape[2]
    return (
        fi.at[0, pl.ds(pl.multiple_of((low_at % 2) * HALF + first, 8), count), lane_slice((low_at // 2) * width, width)],
        fo.at[0, pl.ds(pl.multiple_of(high_at * HALF + first, 8), count), :],
    )


def finish_small(gathered, bc, bp, bs, seg, n1g, n1s, fib, fob, n2g, n2s, mask_out):
    def row(at):
        place = 8 * (at % (2 * RING)) + at // (2 * RING)
        return gathered[place : place + 1, :]

    heads, dim = bc.shape[0], bc.shape[2]
    width = heads * dim
    rows = [row(at) for at in range(5)]
    for head in range(heads):
        cols = slice(head * dim, (head + 1) * dim)
        bc[head] = rows[0][:, cols]
        bp[head] = rows[1][:, cols]
        bs[head] = rows[2][:, cols]
        seg[head, 0:1, :] = rows[3][:, cols]
        seg[head, 1:2, :] = rows[4][:, cols]
    mask_out[...] = row(MASK_ROW).reshape(width)
    for out, at in ((n1g, 9), (n1s, 10), (fob, 11), (n2g, 12), (n2s, 13)):
        out[...] = row(at)
    for step in range(4):
        fib[:, step * width : (step + 1) * width] = row(16 + step)


def unpack_body(step, last, meta, own_a, other_a, own_b, other_b, *refs):
    if last:
        pos, rel_in, small_in = refs[0], refs[7], refs[8]
        *small_outs, low_a, high_a, low_f, high_f, sems, rel_all, small_all, rel_sem = refs[-19:]
        fi, fo, wq, wk, wv, wo, rel, small, w_rel = refs[-28:-19]
        rel_copies = [
            pltpu.make_async_copy(rel_in, rel_all, rel_sem.at[0]),
            pltpu.make_async_copy(small_in, small_all, rel_sem.at[1]),
        ]
        for copy in rel_copies:
            copy.start()
    else:
        fi, fo, wq, wk, wv, wo, rel, small, token, low_a, high_a, low_f, high_f, sems = refs[-14:]
        token[...] = jnp.zeros_like(token)
    low_at, high_at = meta[step], meta[RING + step]
    by_core(meta, own_a, other_a, low_a, high_a)
    low_to, high_to = ffn_places(fi, fo, low_at, high_at, 0, HEAD_ROWS)
    copies = [
        pltpu.make_async_copy(low_a, low_to, sems.at[8]),
        pltpu.make_async_copy(high_a, high_to, sems.at[9]),
    ]
    for copy in copies:
        copy.start()
    by_core(meta, own_b, other_b, low_f, high_f)
    low_to, high_to = ffn_places(fi, fo, low_at, high_at, HEAD_ROWS, REST_ROWS)
    rest = pl.ds(0, REST_ROWS)
    rel_part = pl.ds(REL.start, REL_PIECE)

    def rel_to(at):
        return rel.at[pl.ds(pl.multiple_of(at * REL_PIECE, 8), REL_PIECE), :]

    later = [
        pltpu.make_async_copy(low_f.at[rest], low_to, sems.at[0]),
        pltpu.make_async_copy(high_f.at[rest], high_to, sems.at[1]),
    ]
    blocks = ((low_f, low_at, 2 * low_at, 0), (high_f, RING + high_at, 2 * high_at + 1, 1))
    small_part = pl.ds(REL.stop, 8)
    if not last:
        for src, at, row, n in blocks:
            later.append(pltpu.make_async_copy(src.at[rel_part], rel_to(at), sems.at[2 + n]))
            later.append(
                pltpu.make_async_copy(src.at[small_part], small.at[pl.ds(pl.multiple_of(8 * row, 8), 8), :], sems.at[10 + n])
            )
    for copy in later:
        copy.start()

    def block_copies(src, at, dst, sem):
        inside = at % 4
        return [
            pltpu.make_async_copy(
                src.at[pl.ds(BLOCK.start, HALF // 2), pl.ds(part * HALF, HALF)],
                dst.at[
                    0,
                    pl.ds(pl.multiple_of((inside // 2) * HALF + part * (HALF // 2), 8), HALF // 2),
                    lane_slice((inside % 2) * HALF, HALF),
                ],
                sems.at[sem + part],
            )
            for part in range(2)
        ]

    for src, at, early, late, n in ((low_f, low_at, wq, wk, 4), (high_f, high_at, wv, wo, 6)):

        @pl.when(at < RING // 2)
        def _early(src=src, at=at, early=early, n=n):
            for copy in block_copies(src, at, early, n):
                copy.start()

        @pl.when(at >= RING // 2)
        def _late(src=src, at=at, late=late, n=n):
            for copy in block_copies(src, at, late, n):
                copy.start()

        later += block_copies(src, at, early, n)
    if last:
        for copy in rel_copies:
            copy.wait()
        for src, at, row, _ in blocks:
            rel_all[pl.ds(pl.multiple_of(at * REL_PIECE, 8), REL_PIECE), :] = src[REL, :]
            small_all[pl.ds(pl.multiple_of(8 * row, 8), 8), :] = src[REL.stop :, :]
        w_rel[0] = dot_tn(pos[...], rel_all[...].astype(BF16))
        finish_small(small_all, *small_outs)
    for copy in copies + later:
        copy.wait()


def unpack(step, meta, own_a, other_a, own_b, other_b, outs, earlier, pos, heads):
    given = [v for v in outs if not isinstance(v, jax.ShapeDtypeStruct)]
    width, ff = own_a.shape[1], outs[0].shape[2]
    last = pos is not None

    def f32(*dims):
        return shape(*dims, dtype=F32)

    extra = [f32(8, LANES)]
    scratch = [
        *[pltpu.VMEM((HEAD_ROWS, width), F32)] * 2,
        *[pltpu.VMEM((B_ROWS, width), F32)] * 2,
        pltpu.SemaphoreType.DMA((12,)),
    ]
    if last:
        by_head, line = f32(heads, 1, width // heads), f32(1, width)
        extra = [
            f32(1, width, width), by_head, by_head, by_head, f32(heads, 2, width // heads), line, line, f32(1, ff),
            line, line, line, f32(width),
        ]
        scratch += [
            pltpu.VMEM(pos.shape, F32), pltpu.VMEM((16 * RING, width), F32), pltpu.SemaphoreType.DMA((2,)),
        ]
    front = [meta, own_a, other_a, own_b, other_b] + ([pos] if last else [])
    results = pl.pallas_call(
        functools.partial(unpack_body, (step + RING - 1) % RING, last),
        out_shape=tuple(shape(*v.shape, dtype=v.dtype) for v in outs) + tuple(extra),
        in_specs=[SMEM_SPEC] + [VMEM_SPEC] * (len(front) - 1) + [ANY_SPEC] * (len(given) + len(earlier)),
        out_specs=tuple(ANY_SPEC for _ in outs) + (VMEM_SPEC,) * len(extra),
        input_output_aliases={len(front) + n: n for n in range(len(given))},
        scratch_shapes=scratch,
        compiler_params=params(),
        cost_estimate=cost(0, 8_000_000),
    )(*front, *given, *earlier)
    results, token = results[: len(outs)], results[len(outs) :]
    if not last:
        token = token[0]
    return results, token


def ring_steps(count):
    cycle = [(z, 0) for z in range(4)] + [(z, 1) for z in (3, 2, 1, 0)]
    steps = []
    for index in range(count):
        base, inside = index - index % GROUP, index % GROUP
        at = cycle.index((inside // 4, (inside // 2) % 2))
        z, y = cycle[(at + (1 if inside % 2 == 0 else -1)) % RING]
        steps.append((index, base + (z * 2 + y) * 2 + inside % 2))
    return steps


SECTION, DP = "section", "dp"


def swapped(value, axis, bit):
    count = lax.axis_size(axis)
    return lax.ppermute(value, axis, [(index, index ^ bit) for index in range(count)])


def position_table(total_rows, width_model, mem_rows, seg_rows):
    row_ids = np.arange(total_rows, dtype=np.float32)
    distance = np.float32(mem_rows + seg_rows - 1) - row_ids
    power = np.arange(0, width_model, 2, dtype=np.float32) / np.float32(width_model)
    freqs = np.float32(1.0) / np.power(np.float32(10000.0), power)
    angles = distance[:, None] * freqs[None, :]
    return np.concatenate([np.sin(angles), np.cos(angles)], axis=1).astype(np.float32)


def scratches(seg_rows, mem_rows, width, ff, heads):
    rows, key_rows, rel_rows = 2 * seg_rows, mem_rows + seg_rows, mem_rows + 2 * seg_rows
    vm, dma = pltpu.VMEM, pltpu.SemaphoreType.DMA
    vrow_b, vrow_f, square, wide = vm((rows, width), BF16), vm((rows, width), F32), vm((width, width), BF16), vm((rows, ff), BF16)
    weights_f = dict(fi=vm((width, ff), BF16), fo=vm((ff, width), BF16))
    weights_a = dict(wk=square, wq=square, wv=square, wo=square, rel=vm((rel_rows, width), BF16))
    probs_scratch = vm((heads, rows, key_rows), BF16)
    forward_scratch = dict(
        joined=vrow_b, stream=vrow_b, qc=vrow_b, qp=vrow_b, qs=vrow_b, k=vrow_b, v=vrow_b, mixed=vrow_b,
        midb=vrow_b, out=vrow_b, p=probs_scratch,
        pos=vm((heads // 2, 2 * rows, key_rows), F32),
        bias=vm((2, seg_rows, seg_rows), F32),
        mid_in=vrow_f, outer=vrow_f, act=wide, slope=wide,
        sem_in=dma((10,)),
        sem_first=dma((1,)),
        sem_out=dma((40,)),
        **weights_f, **weights_a,
    )
    backward_scratch = dict(
        outer=vrow_f, mid_in=vrow_f, cot=vrow_b, returned=vrow_b, e=vrow_b, ab=vrow_b, a=vrow_f, acc=vrow_f,
        u=wide, slope=wide, x=vrow_b, k=vrow_b, v=vrow_b, qc=vrow_b, qp=vrow_b, qs=vrow_b, qpf=vrow_b, dk=vrow_b,
        dv=vrow_b, dqb=vrow_b, out=vrow_b, p=probs_scratch, dq=vrow_f, dqp=vrow_f,
        drel=vm((rel_rows, width), F32),
        sums_t=vm((16, width), F32),
        sums=vm((8, width), F32),
        sem_tail=dma((1 + 3 * (ff // width),)),
        sem_first=dma((4,)),
        sem_head=dma((11,)),
        sem_out=dma((14,)),
        **weights_f, **weights_a,
    )
    return forward_scratch, backward_scratch


def shards(
    content_in, memory, mask_embed, doc_ids, orders, targets, slot_used,
    w_query, w_key, w_value, w_out, w_rel, bias_content, bias_position, bias_segment, seg_embed,
    norm1_gain, norm1_shift, ffn_in, ffn_in_bias, ffn_out, ffn_out_bias, norm2_gain, norm2_shift,
    content_cot, query_cot,
):
    slots, seg_rows, width = content_in.shape
    mem_rows = memory.shape[2]
    heads, dim = bias_content.shape[1:]
    ff = ffn_in.shape[2]
    key_rows, rows = mem_rows + seg_rows, 2 * seg_rows
    rel_rows = key_rows + seg_rows
    section = lax.axis_index(SECTION).astype(jnp.int32)
    dp = lax.axis_index(DP).astype(jnp.int32)
    dp_count = lax.axis_size(DP)
    inside = dp % GROUP
    at = jnp.where((inside // 2) % 2 == 0, inside // 4, RING - 1 - inside // 4)
    lane = jnp.arange(2 * RING + 2, dtype=jnp.int32)
    meta = jnp.where(
        lane < RING,
        (at - lane) & (RING - 1),
        jnp.where(
            lane < 2 * RING,
            (-at - lane) & (RING - 1),
            jnp.where(lane == META_CORE, dp % 2, section),
        ),
    )
    pos_b = jnp.asarray(position_table(rel_rows, width, mem_rows, seg_rows)).astype(BF16)
    small, rel = pl.pallas_call(
        prepare_body,
        out_shape=(shape(SMALL_ROWS, width, dtype=F32), shape(rel_rows, width)),
        compiler_params=params(),
    )(
        bias_content, bias_position, bias_segment,
        jnp.transpose(seg_embed[0], (1, 0, 2)), norm1_gain, norm1_shift, ffn_out_bias, norm2_gain,
        norm2_shift, mask_embed, ffn_in_bias, pos_b, w_rel,
    )

    row_b, row_f = shape(slots, rows, width), shape(slots, rows, width, dtype=F32)
    kept = dict(
        joined=row_b, stream=row_b, qc=row_b, qp=row_b, qs=row_b, k=row_b, v=row_b, mixed=row_b,
        p=shape(slots, heads, rows, key_rows),
        mid_in=row_f,
        outer=row_f,
        slope=shape(slots, rows, ff),
        me=shape(2, slots, rows, width),
        ua=shape(2, slots, rows, ff),
        content_out=shape(1, slots, seg_rows, width),
        query_out=shape(1, slots, seg_rows, width),
    )
    forward_scratch, backward_scratch = scratches(seg_rows, mem_rows, width, ff, heads)
    common = dict(meta=(SMEM_SPEC, meta), slot_used=(SMEM_SPEC, slot_used), **in_vmem(small=small))
    ids = in_vmem(docs=doc_ids, orders=orders, targets=targets)
    weights_attention = in_hbm(w_key=w_key, w_query=w_query, w_value=w_value, w_out=w_out, rel=rel)
    weights_ffn = in_hbm(ffn_in=ffn_in, ffn_out=ffn_out)
    sent = {}
    for call in range(4):
        layer, slot = call // 2, call % 2
        source = in_hbm(content_in=content_in) if layer == 0 else in_hbm(arrived=sent[slot])
        inputs = common | ids | in_hbm(memory=memory) | weights_attention | weights_ffn | source
        fresh = dict(sent=shape(rows, width)) if layer == 0 else {}
        kept, new = call_kernel(forward_body, layer, slot, inputs, kept, fresh, forward_scratch)
        if layer == 0:
            sent[slot] = lax.ppermute(new.popitem()[1], SECTION, [(0, 1)])
    kept = types.SimpleNamespace(**kept)

    grads = dict(
        me=kept.me, ua=kept.ua, ab=row_b, dk=row_b, dv=row_b, dq=row_b,
        drel=shape(slots, rel_rows, width, dtype=F32),
        input_grad=shape(1, slots, seg_rows, width),
        sums=shape(slots, SUM_ROWS, width, dtype=F32),
    )
    flat = lambda v: v.reshape(v.shape[:-3] + (slots * rows, v.shape[-1]))
    returned = {}
    for call in range(4):
        layer, slot = 1 - call // 2, 1 - call % 2
        inputs = common | in_vmem(docs=doc_ids) | weights_attention | weights_ffn | in_hbm(
            outer=kept.outer, slope=kept.slope, mid_in=kept.mid_in, content_cot=content_cot, query_cot=query_cot,
            p=kept.p, k=kept.k, v=kept.v, qc=kept.qc, qp=kept.qp, qs=kept.qs,
        )
        if layer == 0:
            inputs |= in_hbm(returned=returned[slot])
        fresh = dict(sent=shape(rows, width)) if layer == 1 else {}
        grads, new = call_kernel(backward_body, layer, slot, inputs, grads, fresh, backward_scratch)
        if layer == 1:
            returned[slot] = lax.ppermute(new.popitem()[1], SECTION, [(1, 0)])
    grads = types.SimpleNamespace(**grads)

    me, ua = flat(grads.me), flat(grads.ua)
    operands = [flat(v) for v in (kept.stream, kept.joined, kept.mixed, grads.dq, grads.dk, grads.dv, grads.ab)]
    operands += [grads.drel, grads.sums]
    own_a, own_b, *handed = pieces(meta, me, ua, operands)
    first_a, first_b = [swapped(value, DP, 1) for value in handed[:2]]
    first_a, first_b, *rest = lax.optimization_barrier((first_a, first_b, *handed[2:]))
    rest_a, rest_b = [swapped(value, DP, 1) for value in rest]
    own, others = (own_a, own_b), ((first_a, rest_a), (first_b, rest_b))

    def add(ring, step, came=None):
        other = others[ring][0][0] if step == 0 else others[ring][1][step - 1]
        total = own[ring][step].astype(F32) + other.astype(F32)
        return (total if came is None else total + came.astype(F32)).astype(BF16)

    acc = [add(0, 0), add(1, 0)]

    steps = ring_steps(dp_count)
    for step in range(1, RING):
        came = [lax.ppermute(acc[ring], DP, steps) for ring in range(2)]
        acc = [add(ring, step, came[ring]) for ring in range(2)]
    acc_a, acc_b = acc
    bit = GROUP
    while bit < dp_count:
        acc_a = (acc_a.astype(F32) + swapped(acc_a, DP, bit).astype(F32)).astype(BF16)
        acc_b = (acc_b.astype(F32) + swapped(acc_b, DP, bit).astype(F32)).astype(BF16)
        bit *= 2
    spare = lax.slice_in_dim(acc_b, REL.stop, B_ROWS, axis=0)
    came = swapped(spare, SECTION, 1)
    holds = (meta[META_CORE] == MASK_ROW % 2) & (meta[2 * RING - 1] == MASK_ROW // 2)
    row = lax.broadcasted_iota(jnp.int32, spare.shape, 0)
    spare = jnp.where(holds & (row == 0), (spare.astype(F32) + came.astype(F32)).astype(BF16), spare)
    acc_b = lax.dynamic_update_slice_in_dim(acc_b, spare, REL.stop, axis=0)
    ffn_outs = [shape(1, width, ff, dtype=F32), shape(1, ff, width, dtype=F32)]
    rest_outs = [shape(1, width, width, dtype=F32) for _ in range(4)] + [shape(rel_rows, width, dtype=F32)]
    rest_outs.append(shape(16 * RING, width, dtype=F32))
    tokens = []
    outs = ffn_outs + rest_outs
    for step in range(RING):
        if step:
            acc_a = lax.ppermute(acc_a, DP, steps)
            acc_b = lax.ppermute(acc_b, DP, steps)
        handed_a, handed_b, before = acc_a, acc_b, []
        if step > 1:
            handed_a, before_a = lax.optimization_barrier((acc_a, tokens[step - 2]))
            before.append(before_a)
        if step:
            handed_b, before_b = lax.optimization_barrier((acc_b, tokens[step - 1]))
            before.append(before_b)
        outs, token = unpack(
            step, meta, acc_a, swapped(handed_a, DP, 1), acc_b, swapped(handed_b, DP, 1), outs, before,
            pos_b if step == RING - 1 else None, heads,
        )
        tokens.append(token)
    ffn_outs, rest_outs = outs[:2], outs[2:]
    (
        grad_w_rel, grad_bc, grad_bp, grad_bs, grad_seg, grad_n1g, grad_n1s, grad_fib, grad_fob, grad_n2g, grad_n2s,
        mask_grad,
    ) = tokens[-1]
    grad_ffn_in, grad_ffn_out = ffn_outs
    grad_w_query, grad_w_key, grad_w_value, grad_w_out = rest_outs[:4]
    one_layer = lambda v: v.reshape(1, heads, dim)
    return (
        kept.content_out, kept.query_out, grads.input_grad, mask_grad,
        grad_w_query, grad_w_key, grad_w_value, grad_w_out, grad_w_rel,
        one_layer(grad_bc), one_layer(grad_bp), one_layer(grad_bs), jnp.transpose(grad_seg, (1, 0, 2))[None],
        grad_n1g, grad_n1s, grad_ffn_in, grad_fib, grad_ffn_out, grad_fob, grad_n2g, grad_n2s,
    )


def solution(mesh):
    two, three, four = P(SECTION, None), P(SECTION, None, None), P(SECTION, None, None, None)
    rows = P(SECTION, DP, None, None)
    return jax.shard_map(
        shards,
        mesh=mesh,
        in_specs=(
            P(DP, None, None), rows, P(), P(DP, None), P(DP, None), P(DP, None), P(DP), *[three] * 8, four,
            two, two, three, two, three, two, two, two, rows, rows,
        ),
        out_specs=(
            rows, rows, rows, P(), *[three] * 8, four, two, two, three, two, three, two, two, two,
        ),
        check_vma=False,
    )
```

```python
import functools
import types

import jax
import jax.numpy as jnp
import numpy as np
from jax import lax
from jax.experimental import pallas as pl
from jax.experimental.pallas import tpu as pltpu
from jax.sharding import PartitionSpec as P

BF16 = jnp.bfloat16
F32 = jnp.float32
NEG_FILL = -1e30
NORM_EPS = 1e-05
GELU_A = 0.7978845608028654
GELU_B = 0.044715
VMEM_LIMIT = 60 * 1024 * 1024
LANES = 128
LAYER_FLOPS = 9_000_000_000
RING = 8
META_CORE, META_SECTION = 2 * RING, 2 * RING + 1

ROW_BC, ROW_BP, ROW_BS, ROW_SEG0, ROW_SEG1 = 0, 1, 2, 3, 4
ROW_N1G, ROW_N1S, ROW_FOB, ROW_N2G, ROW_N2S, ROW_MASK, ROW_FIB = 5, 6, 7, 8, 9, 10, 11
SMALL_ROWS = 16


def dot_nn(left, right):
    return jnp.dot(left, right, preferred_element_type=F32)


def dot_nt(left, right):
    return lax.dot_general(left, right, (((1,), (1,)), ((), ())), preferred_element_type=F32)


def dot_tn(left, right):
    return lax.dot_general(left, right, (((0,), (0,)), ((), ())), preferred_element_type=F32)


def col_sum(block):
    return jnp.sum(block, axis=0, keepdims=True)


def norm_parts(rows):
    center = jnp.mean(rows, axis=-1, keepdims=True)
    offset = rows - center
    spread = jnp.mean(offset * offset, axis=-1, keepdims=True)
    scale = lax.rsqrt(spread + NORM_EPS)
    return offset * scale, scale


def norm_back(grad, unit, scale, gain):
    inner = grad * gain
    mean_inner = jnp.mean(inner, axis=-1, keepdims=True)
    mean_cross = jnp.mean(inner * unit, axis=-1, keepdims=True)
    return (inner - mean_inner - unit * mean_cross) * scale


def half_masks():
    lane = lax.broadcasted_iota(jnp.int32, (1, LANES), 1)
    low = lane < LANES // 2
    return low, low.astype(F32).astype(BF16), (~low).astype(F32).astype(BF16)


def stack_heads(block, low_b, high_b):
    return jnp.concatenate([block * low_b, block * high_b], axis=0)


def copy_in(pairs, sems):
    copies = [
        pltpu.make_async_copy(src, dst, sems.at[n]) for n, (src, dst) in enumerate(pairs)
    ]
    for copy in copies:
        copy.start()
    return copies


def name_refs(names_in, names_out, names_scratch, refs):
    groups, start = [], 0
    for names in (names_in, names_out, names_scratch):
        groups.append(types.SimpleNamespace(**dict(zip(names, refs[start : start + len(names)]))))
        start += len(names)
    return groups


def forward_body(section, slot, names_in, names_out, names_scratch, *refs):
    r, o, s = name_refs(names_in, names_out, names_scratch, refs)
    meta = r.meta
    seg_rows, width = s.stream.shape[0] // 2, s.stream.shape[1]
    key_rows = s.joined.shape[0]
    pairs_count = width // LANES
    ff = s.act.shape[1]
    score_scale = 0.125

    @pl.when(meta[META_SECTION] == section)
    def _run():
        sem_in, sem_out = s.sem_in, s.sem_out
        mem_rows = key_rows - seg_rows
        x_src = r.content_in.at[slot] if section == 0 else r.arrived.at[pl.ds(0, seg_rows)]
        loads = [
            (r.memory.at[0, slot], s.joined.at[pl.ds(0, mem_rows)]),
            (x_src, s.joined.at[pl.ds(mem_rows, seg_rows)]),
            (x_src, s.stream.at[pl.ds(0, seg_rows)]),
            (r.w_key.at[0], s.wk),
            (r.w_query.at[0], s.wq),
            (r.rel, s.rel),
            (r.w_value.at[0], s.wv),
            (r.w_out.at[0], s.wo),
            (r.ffn_in.at[0], s.fi),
            (r.ffn_out.at[0], s.fo),
        ]
        moves = []
        if section == 1:
            query_rows = pl.ds(seg_rows, seg_rows)
            moves = copy_in([(r.arrived.at[query_rows], s.stream.at[query_rows])], s.sem_first)
        moves = copy_in(loads, sem_in) + moves
        stores = []

        def store(src, dst):
            copy = pltpu.make_async_copy(src, dst, sem_out.at[len(stores)])
            copy.start()
            stores.append(copy)

        small = r.small
        used = (r.slot_used[slot] > 0).astype(jnp.int32).astype(F32)
        if section == 0:
            s.stream[seg_rows:, :] = jnp.broadcast_to(
                small[ROW_MASK : ROW_MASK + 1, :], (seg_rows, width)
            ).astype(BF16)
        square = (seg_rows, seg_rows)
        doc = jnp.broadcast_to(r.docs[slot : slot + 1, :].astype(F32), square)
        order = jnp.broadcast_to(r.orders[slot : slot + 1, :].astype(F32), square)
        target = jnp.broadcast_to(r.targets[slot : slot + 1, :].astype(F32), square)
        same = doc == doc.T
        visible = same & ((target == 0.0) | (order <= order.T))
        row_id = lax.broadcasted_iota(jnp.int32, square, 0)
        col_id = lax.broadcasted_iota(jnp.int32, square, 1)
        s.bias[0] = jnp.where(visible, 0.0, NEG_FILL)
        s.bias[1] = jnp.where(visible & (row_id != col_id), 0.0, NEG_FILL)

        for n in (0, 1, 3):
            moves[n].wait()
        s.k[...] = dot_nn(s.joined[...], s.wk[...]).astype(BF16)
        store(s.k, o.k.at[slot])
        store(s.joined, o.joined.at[slot])
        moves[2].wait()
        if section == 1:
            moves[10].wait()
        store(s.stream, o.stream.at[slot])
        moves[4].wait()
        queries = dot_nn(s.stream[...], s.wq[...])
        for block, kept, row in ((s.qc, o.qc, ROW_BC), (s.qp, o.qp, ROW_BP), (s.qs, o.qs, ROW_BS)):
            with_bias = (queries + small[row : row + 1, :]).astype(BF16)
            block[...] = (with_bias.astype(F32) * score_scale).astype(BF16)
            store(block, kept.at[slot])
        moves[6].wait()
        s.v[...] = dot_nn(s.joined[...], s.wv[...]).astype(BF16)
        store(s.v, o.v.at[slot])
        moves[5].wait()

        low, low_b, high_b = half_masks()
        bias_by_stream = [s.bias[0], s.bias[1]]
        inside = col_id <= row_id
        for pair in range(pairs_count):
            sl = slice(pair * LANES, (pair + 1) * LANES)
            position = dot_nt(stack_heads(s.qp[:, sl], low_b, high_b), s.rel[:, sl])
            for part in range(4):
                base = part * seg_rows
                turned = [
                    pltpu.roll(
                        position[base : base + seg_rows, n * LANES : (n + 1) * LANES],
                        1, axis=1, stride=1, stride_axis=0,
                    )
                    for n in range(3)
                ]
                rolled = jnp.concatenate(
                    [jnp.where(inside, turned[n], turned[n + 1]) for n in range(2)], axis=1
                )
                s.pos[pair, base : base + seg_rows, :] = rolled
        for pair in range(pairs_count):
            sl = slice(pair * LANES, (pair + 1) * LANES)
            content = dot_nt(stack_heads(s.qc[:, sl], low_b, high_b), s.k[:, sl])
            segments = jnp.concatenate(
                [
                    jnp.broadcast_to(small[row : row + 1, sl].astype(BF16) * mask, (LANES, LANES))
                    for mask in (low_b, high_b)
                    for row in (ROW_SEG0, ROW_SEG1)
                ],
                axis=0,
            )
            pieces_wide = dot_nt(s.qs[:, sl], segments)
            probs_pair = []
            for head in range(2):
                probs_streams = []
                for stream in range(2):
                    base = (2 * head + stream) * seg_rows
                    rows = slice(stream * seg_rows, (stream + 1) * seg_rows)
                    same_part = pieces_wide[rows, 2 * head * LANES : (2 * head + 1) * LANES]
                    other_part = pieces_wide[rows, (2 * head + 1) * LANES : (2 * head + 2) * LANES]
                    body = content[base : base + seg_rows, :] + s.pos[pair, base : base + seg_rows, :]
                    left = body[:, :mem_rows] + other_part
                    right = body[:, mem_rows:] + jnp.where(same, same_part, other_part) + bias_by_stream[stream]
                    peak = jnp.max(jnp.maximum(left, right), axis=-1, keepdims=True)
                    left = jnp.exp(left - peak)
                    right = jnp.exp(right - peak)
                    total = jnp.sum(left + right, axis=-1, keepdims=True)
                    inverse = 1.0 / total
                    probs_streams.append(
                        jnp.concatenate([left * inverse, right * inverse], axis=1).astype(BF16)
                    )
                probs = jnp.concatenate(probs_streams, axis=0)
                s.p[2 * pair + head] = probs
                store(s.p.at[2 * pair + head], o.p.at[slot, 2 * pair + head])
                probs_pair.append(probs)
            mixed = dot_nn(
                jnp.concatenate(probs_pair, axis=1), stack_heads(s.v[:, sl], low_b, high_b)
            )
            s.mixed[:, sl] = mixed.astype(BF16)
        store(s.mixed, o.mixed.at[slot])

        moves[7].wait()
        middle_in = dot_nn(s.mixed[...], s.wo[...]) + s.stream[...].astype(F32)
        s.mid_in[...] = middle_in
        store(s.mid_in, o.mid_in.at[slot])
        unit, _ = norm_parts(middle_in)
        middle = unit * small[ROW_N1G : ROW_N1G + 1, :] + small[ROW_N1S : ROW_N1S + 1, :]
        s.midb[...] = middle.astype(BF16)
        store(s.midb, o.me.at[0, slot])
        s.outer[...] = middle + small[ROW_FOB : ROW_FOB + 1, :]
        moves[8].wait()
        moves[9].wait()
        for step in range(ff // width // 2):
            cols = slice(2 * step * width, 2 * (step + 1) * width)
            inner = (
                dot_nn(s.midb[...], s.fi[:, cols])
                + jnp.concatenate([small[ROW_FIB + 2 * step + n : ROW_FIB + 2 * step + n + 1, :] for n in range(2)], axis=1)
            )
            square_in = inner * inner
            wave = jnp.tanh(GELU_A * inner * (1.0 + GELU_B * square_in))
            half = 0.5 * (1.0 + wave)
            active = (inner * half).astype(BF16)
            slope = half + (0.5 * GELU_A) * inner * (1.0 - wave * wave) * (1.0 + 3.0 * GELU_B * square_in)
            s.act[:, cols] = active
            s.slope[:, cols] = slope.astype(BF16)
            part = pl.ds(2 * step * width, 2 * width)
            store(s.act.at[:, part], o.ua.at[1, slot, :, part])
            store(s.slope.at[:, part], o.slope.at[slot, :, part])
            s.outer[...] += dot_nn(active, s.fo[cols, :])
        store(s.outer, o.outer.at[slot])
        unit, _ = norm_parts(s.outer[...])
        result = unit * small[ROW_N2G : ROW_N2G + 1, :] + small[ROW_N2S : ROW_N2S + 1, :]
        s.out[...] = (result * used).astype(BF16)
        store(s.out.at[pl.ds(0, seg_rows)], o.content_out.at[0, slot])
        store(s.out.at[pl.ds(seg_rows, seg_rows)], o.query_out.at[0, slot])
        if section == 0:
            store(s.out, o.sent)
        for copy in stores:
            copy.wait()


def backward_body(section, slot, names_in, names_out, names_scratch, *refs):
    r, o, s = name_refs(names_in, names_out, names_scratch, refs)
    meta = r.meta
    rows, width = s.a.shape
    seg_rows = rows // 2
    ff = s.slope.shape[1]
    key_rows = s.k.shape[0]
    mem_rows = key_rows - seg_rows
    pairs_count = width // LANES
    score_scale = 0.125

    @pl.when(meta[META_SECTION] == section)
    def _run():
        first_loads = [
            (r.content_cot.at[0, slot], s.cot.at[pl.ds(0, seg_rows)]),
            (r.query_cot.at[0, slot], s.cot.at[pl.ds(seg_rows, seg_rows)]),
            (r.outer.at[slot], s.outer),
        ]
        if section == 0:
            first_loads.append((r.returned, s.returned))
        first = copy_in(first_loads, s.sem_first)
        loads = []
        for step in range(ff // width):
            part = pl.ds(step * width, width)
            loads.append((r.ffn_out.at[0, part], s.fo.at[part]))
            loads.append((r.slope.at[slot, :, part], s.slope.at[:, part]))
            loads.append((r.ffn_in.at[0, :, part], s.fi.at[:, part]))
        loads.append((r.mid_in.at[slot], s.mid_in))
        head_loads = [
            (r.w_out.at[0], s.wo),
            (r.v.at[slot], s.v),
            (r.p.at[slot], s.p),
            (r.k.at[slot], s.k),
            (r.qc.at[slot], s.qc),
            (r.qp.at[slot], s.qp),
            (r.qs.at[slot], s.qs),
            (r.rel, s.rel),
            (r.w_query.at[0], s.wq),
            (r.w_key.at[0], s.wk),
            (r.w_value.at[0], s.wv),
        ]
        stores = []

        def store(src, dst):
            copy = pltpu.make_async_copy(src, dst, s.sem_out.at[len(stores)])
            copy.start()
            stores.append(copy)

        small = r.small
        used = (r.slot_used[slot] > 0).astype(jnp.int32).astype(F32)
        for move in first:
            move.wait()
        moves = copy_in(loads, s.sem_tail)
        grad = s.cot[...].astype(F32) * used
        if section == 0:
            grad = grad + s.returned[...].astype(F32)
        unit, scale = norm_parts(s.outer[...])
        out = s.sums_t
        out[...] = jnp.zeros_like(out)
        out[4:5, :] = col_sum(grad * unit)
        out[5:6, :] = col_sum(grad)
        grad_outer = norm_back(grad, unit, scale, small[ROW_N2G : ROW_N2G + 1, :])
        s.e[...] = grad_outer.astype(BF16)
        store(s.e, o.me.at[1, slot])
        out[3:4, :] = col_sum(s.e[...].astype(F32))
        s.acc[...] = grad_outer
        for step in range(ff // width):
            for move in moves[3 * step : 3 * step + 3]:
                move.wait()
            cols = slice(step * width, (step + 1) * width)
            if step == 1:
                head_moves = copy_in(head_loads, s.sem_head)
            grad_active = dot_nt(s.e[...], s.fo[cols, :])
            inner_b = (s.slope[:, cols].astype(F32) * grad_active).astype(BF16)
            s.u[:, cols] = inner_b
            out[8 + step : 9 + step, :] = col_sum(inner_b.astype(F32))
            s.acc[...] += dot_nt(inner_b, s.fi[:, cols])
        store(s.u, o.ua.at[0, slot])
        moves[-1].wait()
        unit, scale = norm_parts(s.mid_in[...])
        grad = s.acc[...]
        out[1:2, :] = col_sum(grad * unit)
        out[2:3, :] = col_sum(grad)
        s.a[...] = norm_back(grad, unit, scale, small[ROW_N1G : ROW_N1G + 1, :])
        s.ab[...] = s.a[...].astype(BF16)
        store(s.ab, o.ab.at[slot])
        store(s.sums_t, o.sums.at[slot, pl.ds(8, 16)])

        square = (seg_rows, seg_rows)
        doc = jnp.broadcast_to(r.docs[slot : slot + 1, :].astype(F32), square)
        same_one = (doc == doc.T).astype(F32)
        same = jnp.concatenate([same_one, same_one], axis=0)
        flip_rows = lax.broadcasted_iota(jnp.int32, (rows, rows), 0)
        flip_cols = lax.broadcasted_iota(jnp.int32, (rows, rows), 1)
        flipped_to = jnp.where(flip_rows < seg_rows, seg_rows - 1, rows + seg_rows - 1) - flip_rows
        flip = (flip_cols == flipped_to).astype(F32).astype(BF16)
        out = s.sums
        out[...] = jnp.zeros_like(out)
        head_moves[0].wait()
        s.x[...] = dot_nt(s.ab[...], s.wo[...]).astype(BF16)
        for n in (1, 2, 3, 4, 5, 6, 7):
            head_moves[n].wait()
        s.qpf[...] = dot_nn(flip, s.qp[...]).astype(BF16)

        low, low_b, high_b = half_masks()
        past = lax.broadcasted_iota(jnp.int32, square, 1) >= lax.broadcasted_iota(jnp.int32, square, 0)
        for pair in range(pairs_count):
            sl = slice(pair * LANES, (pair + 1) * LANES)
            grads_mixed = stack_heads(s.x[:, sl], low_b, high_b)
            grad_probs = dot_nt(grads_mixed, s.v[:, sl])
            scores_b = []
            same_sums, other_sums = [], []
            for head in range(2):
                probs = s.p[2 * pair + head].astype(F32)
                product = probs * grad_probs[head * rows : (head + 1) * rows, :]
                delta = jnp.sum(product, axis=-1, keepdims=True)
                rounded = (product - probs * delta).astype(BF16)
                scores_b.append(rounded)
                wide = rounded.astype(F32)
                right = wide[:, mem_rows:] * same
                same_sum = jnp.sum(right, axis=-1, keepdims=True)
                same_sums.append(same_sum)
                other_sums.append(
                    jnp.sum(wide[:, :mem_rows] + (wide[:, mem_rows:] - right), axis=-1, keepdims=True)
                )
            stacked = jnp.concatenate(scores_b, axis=0)
            beside = jnp.concatenate(scores_b, axis=1)
            probs_stacked = jnp.concatenate([s.p[2 * pair], s.p[2 * pair + 1]], axis=0)
            s.dv[:, sl] = dot_tn(probs_stacked, grads_mixed).astype(BF16)
            s.dk[:, sl] = dot_tn(stack_heads(s.qc[:, sl], low_b, high_b), stacked).T.astype(BF16)
            grad_content = dot_nn(beside, stack_heads(s.k[:, sl], low_b, high_b)) * score_scale
            same_sel = jnp.where(low, same_sums[0], same_sums[1])
            other_sel = jnp.where(low, other_sums[0], other_sums[1])
            seg0 = small[ROW_SEG0 : ROW_SEG0 + 1, sl]
            seg1 = small[ROW_SEG1 : ROW_SEG1 + 1, sl]
            grad_segment = (same_sel * seg0 + other_sel * seg1) * score_scale
            qs = s.qs[:, sl].astype(F32)
            out[0:1, sl] = col_sum(grad_content)
            out[2:3, sl] = col_sum(grad_segment)
            out[3:4, sl] = col_sum(same_sel * qs)
            out[4:5, sl] = col_sum(other_sel * qs)
            s.dq[:, sl] = grad_content + grad_segment
            turned = dot_nn(flip, beside)
            shifted_heads = []
            for head in range(2):
                parts = []
                for stream in range(2):
                    blocks = [
                        pltpu.roll(
                            turned[
                                stream * seg_rows : (stream + 1) * seg_rows,
                                head * key_rows + n * LANES : head * key_rows + (n + 1) * LANES,
                            ],
                            0, axis=1, stride=1, stride_axis=0,
                        )
                        for n in range(2)
                    ]
                    blocks = [
                        jnp.where(past, blocks[0], 0.0),
                        jnp.where(past, blocks[1], blocks[0]),
                        jnp.where(past, 0.0, blocks[1]),
                    ]
                    parts.append(jnp.concatenate(blocks, axis=1).astype(BF16))
                shifted_heads.append(jnp.concatenate(parts, axis=0))
            grad_position = (
                dot_nn(
                    jnp.concatenate(shifted_heads, axis=1),
                    stack_heads(s.rel[:, sl], low_b, high_b),
                )
                * score_scale
            )
            out[1:2, sl] = col_sum(grad_position)
            s.dqp[:, sl] = grad_position
            s.drel[:, sl] = dot_tn(
                jnp.concatenate(shifted_heads, axis=0),
                stack_heads(s.qpf[:, sl], low_b, high_b),
            )
        store(s.dk, o.dk.at[slot])
        store(s.dv, o.dv.at[slot])
        store(s.drel, o.drel.at[slot])
        grad_position = s.dqp[...]
        position_high = grad_position.astype(BF16)
        position_low = (grad_position - position_high.astype(F32)).astype(BF16)
        grad_queries = s.dq[...] + dot_nn(flip, position_high) + dot_nn(flip, position_low)
        s.dqb[...] = grad_queries.astype(BF16)
        store(s.dqb, o.dq.at[slot])
        for n in (8, 9, 10):
            head_moves[n].wait()
        grad_rows = s.a[...] + dot_nt(s.dqb[...], s.wq[...])
        grad_content = (
            grad_rows[:seg_rows, :]
            + dot_nt(s.dk[mem_rows:, :], s.wk[...])
            + dot_nt(s.dv[mem_rows:, :], s.wv[...])
        )
        grad_query = grad_rows[seg_rows:, :]
        s.out[:seg_rows, :] = grad_content.astype(BF16)
        s.out[seg_rows:, :] = grad_query.astype(BF16)
        store(s.out.at[pl.ds(0, seg_rows)], o.input_grad.at[0, slot])
        if section == 1:
            store(s.out, o.sent)
        if section == 0:
            out[5:6, :] = col_sum(grad_query)
        store(s.sums, o.sums.at[slot, pl.ds(0, 8)])
        for copy in stores:
            copy.wait()


ANY_SPEC = pl.BlockSpec(memory_space=pltpu.HBM)
SMEM_SPEC = pl.BlockSpec(memory_space=pltpu.SMEM)
VMEM_SPEC = pl.BlockSpec(memory_space=pltpu.VMEM)


def call_kernel(body, section, slot, inputs, carried, fresh, scratch):
    names_in = list(inputs)
    arrays = [inputs[n][1] for n in names_in]
    specs = [inputs[n][0] for n in names_in]
    aliases = {}
    names_out = list(carried) + list(fresh)
    out_shapes = []
    for position, key in enumerate(carried):
        value = carried[key]
        out_shapes.append(jax.ShapeDtypeStruct(value.shape, value.dtype))
        if not isinstance(value, jax.ShapeDtypeStruct):
            aliases[len(arrays)] = position
            arrays.append(value)
            specs.append(ANY_SPEC)
            names_in.append(key + "_")
    out_shapes += [fresh[key] for key in fresh]
    results = pl.pallas_call(
        functools.partial(body, section, slot, names_in, names_out, list(scratch)),
        out_shape=tuple(out_shapes),
        in_specs=specs,
        out_specs=tuple(ANY_SPEC for _ in out_shapes),
        scratch_shapes=list(scratch.values()),
        input_output_aliases=aliases,
        compiler_params=pltpu.CompilerParams(vmem_limit_bytes=VMEM_LIMIT),
        cost_estimate=pl.CostEstimate(flops=LAYER_FLOPS, bytes_accessed=20_000_000, transcendentals=0),
    )(*arrays)
    named = dict(zip(names_out, results))
    return {k: named[k] for k in carried}, {k: named[k] for k in fresh}


def in_hbm(**arrays):
    return {key: (ANY_SPEC, value) for key, value in arrays.items()}


def in_vmem(**arrays):
    return {key: (VMEM_SPEC, value) for key, value in arrays.items()}


def params():
    return pltpu.CompilerParams(vmem_limit_bytes=VMEM_LIMIT)


def cost(flops, moved):
    return pl.CostEstimate(flops=flops, bytes_accessed=moved, transcendentals=0)


def shape(*dims, dtype=BF16):
    return jax.ShapeDtypeStruct(dims, dtype)


def prepare_body(bc, bp, bs, seg, n1g, n1s, fob, n2g, n2s, mask, fib, pos, w_rel, small, rel):
    heads, dim = bc.shape[1:]
    width = heads * dim
    wide = [(row, value[0].astype(F32)) for row, value in ((ROW_BC, bc), (ROW_BP, bp), (ROW_BS, bs))]
    for head in range(heads):
        cols = slice(head * dim, (head + 1) * dim)
        for row, value in wide:
            small[row : row + 1, cols] = value[head : head + 1, :]
        small[ROW_SEG0 : ROW_SEG1 + 1, cols] = seg[head].astype(F32)
    for row, value in (
        (ROW_N1G, n1g), (ROW_N1S, n1s), (ROW_FOB, fob), (ROW_N2G, n2g), (ROW_N2S, n2s),
    ):
        small[row : row + 1, :] = value[...].astype(F32)
    small[ROW_MASK : ROW_MASK + 1, :] = mask[...].astype(F32).reshape(1, width)
    for step in range(4):
        small[ROW_FIB + step : ROW_FIB + step + 1, :] = fib[:, step * width : (step + 1) * width].astype(F32)
    small[SMALL_ROWS - 1 : SMALL_ROWS, :] = jnp.zeros((1, width), F32)
    rel[...] = dot_nn(pos[...], w_rel[0]).astype(BF16)


GROUP = 16
SUM_ROWS = 24
MASK_ROW = 5
HALF = 384
HEAD_ROWS = 320
REST_ROWS = HALF - HEAD_ROWS
REL_PIECE = 24
BLOCK = slice(REST_ROWS, REST_ROWS + HALF // 2)
REL = slice(BLOCK.stop, BLOCK.stop + REL_PIECE)
B_ROWS = BLOCK.stop + 32


def lane_slice(start, size):
    return pl.ds(pl.multiple_of(start, LANES), size)


def block_rows(index, size):
    return pl.ds(pl.multiple_of(index * size, size), size)


def pieces_body(meta, me, ua, stream, joined, mixed, dq, dk, dv, ab, drel, sums, *refs):
    own_a, own_b, first_a, first_b, other_a, other_b = refs[:6]
    vme, vua, vs, vj, vmix, vdq, vdk, vdv, vab, rel, small, stage_a, stage_b, sems, out_sems = refs[6:]
    core, count = meta[META_CORE], RING
    width = vs.shape[1]
    part = width

    loads = [(me.at[0], vme.at[0])]
    for half in range(2):
        for n in range(vua.shape[2] // part):
            cols = pl.ds(n * part, part)
            loads.append((ua.at[half, :, cols], vua.at[half, :, cols]))
        if half == 0:
            loads.append((me.at[1], vme.at[1]))
    blocks_from = len(loads)
    loads += [
        (stream, vs), (dq, vdq), (joined, vj), (dk, vdk), (dv, vdv), (mixed, vmix), (ab, vab), (drel, rel), (sums, small),
    ]
    moves = copy_in(loads, sems)
    moves[0].wait()
    writes = []

    def put(src, owner, step, own, first, other):
        sem = out_sems.at[len(writes)]
        mine = core == owner
        pl.when(mine)(lambda: pltpu.make_async_copy(src, own.at[step], sem).start())
        pl.when(~mine & (step == 0))(lambda: pltpu.make_async_copy(src, first.at[0], sem).start())
        pl.when(~mine & (step != 0))(
            lambda: pltpu.make_async_copy(src, other.at[jnp.maximum(step, 1) - 1], sem).start()
        )
        writes.append(pltpu.make_async_copy(src, own.at[step], sem))

    def step_of(owner, k):
        return (meta[owner * RING] - k) & (RING - 1)

    for owner in range(2):
        base = 1 + owner * (vua.shape[2] // part + 1)
        if owner == 1:
            moves[base - 1].wait()
        for k in range(count):
            if k % 2 == 0:
                moves[base + k // 2].wait()
            if owner == 0:
                lhs = vme[0, :, (k % 2) * HALF : (k % 2 + 1) * HALF]
                rhs = vua[0, :, (k // 2) * width : (k // 2 + 1) * width]
            else:
                lhs, rhs = vua[1, :, k * HALF : (k + 1) * HALF], vme[1]
            whole = dot_tn(lhs, rhs).astype(BF16)
            stage_a[owner, k] = whole[:HEAD_ROWS]
            stage_b[owner, k, :REST_ROWS] = whole[HEAD_ROWS:]
            put(stage_a.at[owner, k], owner, step_of(owner, k), own_a, first_a, other_a)
    for move in moves[blocks_from:]:
        move.wait()
    for owner in range(2):
        for k in range(count):
            left, right = (((vs, vdq), (vj, vdk)), ((vj, vdv), (vmix, vab)))[owner][k // 4]
            inside = k % 4
            value = dot_tn(
                left[:, (inside // 2) * HALF : (inside // 2 + 1) * HALF],
                right[:, (inside % 2) * HALF : (inside % 2 + 1) * HALF],
            ).astype(BF16)
            stage_b[owner, k, BLOCK.start : BLOCK.stop, :HALF] = value[: HALF // 2]
            stage_b[owner, k, BLOCK.start : BLOCK.stop, HALF:] = value[HALF // 2 :]
            at = (owner * RING + k) * REL_PIECE
            row = 2 * k + owner
            rows = [
                small[0, n : n + 1, :] + small[1, n : n + 1, :] for n in (row, min(row + 2 * RING, SUM_ROWS - 1))
            ]
            blank = jnp.zeros((B_ROWS - REL.stop - 2, width), F32)
            stage_b[owner, k, BLOCK.stop :] = jnp.concatenate(
                [rel[0, at : at + REL_PIECE, :] + rel[1, at : at + REL_PIECE, :], *rows, blank], axis=0
            ).astype(BF16)
            put(stage_b.at[owner, k], owner, step_of(owner, k), own_b, first_b, other_b)
    for copy in writes:
        copy.wait()


def pieces(meta, me, ua, operands):
    rows, width = operands[0].shape
    ff = ua.shape[2]

    def vm(*dims, dtype=BF16):
        return pltpu.VMEM(dims, dtype)

    return pl.pallas_call(
        pieces_body,
        out_shape=[
            shape(count, size, width) for count in (RING, 1, RING - 1) for size in (HEAD_ROWS, B_ROWS)
        ],
        in_specs=[SMEM_SPEC] + [ANY_SPEC] * (2 + len(operands)),
        out_specs=[ANY_SPEC] * 6,
        scratch_shapes=[
            vm(2, rows, width), vm(2, rows, ff), *[vm(rows, width)] * 7,
            vm(*operands[-2].shape, dtype=F32), vm(*operands[-1].shape, dtype=F32),
            vm(2, RING, HEAD_ROWS, width), vm(2, RING, B_ROWS, width),
            pltpu.SemaphoreType.DMA((11 + 2 * (ff // width),)), pltpu.SemaphoreType.DMA((4 * RING,)),
        ],
        compiler_params=params(),
        cost_estimate=cost(6 * rows * HALF * width * RING, 30_000_000),
    )(meta, me, ua, *operands)


def by_core(meta, own, other, low_f, high_f):
    low = meta[META_CORE] == 0

    @pl.when(low)
    def _low():
        low_f[...] = own[...].astype(F32)
        high_f[...] = other[...].astype(F32)

    @pl.when(~low)
    def _high():
        low_f[...] = other[...].astype(F32)
        high_f[...] = own[...].astype(F32)


def ffn_places(fi, fo, low_at, high_at, first, count):
    width = fo.shape[2]
    return (
        fi.at[0, pl.ds(pl.multiple_of((low_at % 2) * HALF + first, 8), count), lane_slice((low_at // 2) * width, width)],
        fo.at[0, pl.ds(pl.multiple_of(high_at * HALF + first, 8), count), :],
    )


def finish_small(gathered, bc, bp, bs, seg, n1g, n1s, fib, fob, n2g, n2s, mask_out):
    def row(at):
        place = 8 * (at % (2 * RING)) + at // (2 * RING)
        return gathered[place : place + 1, :]

    heads, dim = bc.shape[0], bc.shape[2]
    width = heads * dim
    rows = [row(at) for at in range(5)]
    for head in range(heads):
        cols = slice(head * dim, (head + 1) * dim)
        bc[head] = rows[0][:, cols]
        bp[head] = rows[1][:, cols]
        bs[head] = rows[2][:, cols]
        seg[head, 0:1, :] = rows[3][:, cols]
        seg[head, 1:2, :] = rows[4][:, cols]
    mask_out[...] = row(MASK_ROW).reshape(width)
    for out, at in ((n1g, 9), (n1s, 10), (fob, 11), (n2g, 12), (n2s, 13)):
        out[...] = row(at)
    for step in range(4):
        fib[:, step * width : (step + 1) * width] = row(16 + step)


def unpack_body(step, last, meta, own_a, other_a, own_b, other_b, *refs):
    if last:
        pos, rel_in, small_in = refs[0], refs[7], refs[8]
        *small_outs, low_a, high_a, low_f, high_f, sems, rel_all, small_all, rel_sem = refs[-19:]
        fi, fo, wq, wk, wv, wo, rel, small, w_rel = refs[-28:-19]
        rel_copies = [
            pltpu.make_async_copy(rel_in, rel_all, rel_sem.at[0]),
            pltpu.make_async_copy(small_in, small_all, rel_sem.at[1]),
        ]
        for copy in rel_copies:
            copy.start()
    else:
        fi, fo, wq, wk, wv, wo, rel, small, token, low_a, high_a, low_f, high_f, sems = refs[-14:]
        token[...] = jnp.zeros_like(token)
    low_at, high_at = meta[step], meta[RING + step]
    by_core(meta, own_a, other_a, low_a, high_a)
    low_to, high_to = ffn_places(fi, fo, low_at, high_at, 0, HEAD_ROWS)
    copies = [
        pltpu.make_async_copy(low_a, low_to, sems.at[8]),
        pltpu.make_async_copy(high_a, high_to, sems.at[9]),
    ]
    for copy in copies:
        copy.start()
    by_core(meta, own_b, other_b, low_f, high_f)
    low_to, high_to = ffn_places(fi, fo, low_at, high_at, HEAD_ROWS, REST_ROWS)
    rest = pl.ds(0, REST_ROWS)
    rel_part = pl.ds(REL.start, REL_PIECE)

    def rel_to(at):
        return rel.at[pl.ds(pl.multiple_of(at * REL_PIECE, 8), REL_PIECE), :]

    later = [
        pltpu.make_async_copy(low_f.at[rest], low_to, sems.at[0]),
        pltpu.make_async_copy(high_f.at[rest], high_to, sems.at[1]),
    ]
    blocks = ((low_f, low_at, 2 * low_at, 0), (high_f, RING + high_at, 2 * high_at + 1, 1))
    small_part = pl.ds(REL.stop, 8)
    if not last:
        for src, at, row, n in blocks:
            later.append(pltpu.make_async_copy(src.at[rel_part], rel_to(at), sems.at[2 + n]))
            later.append(
                pltpu.make_async_copy(src.at[small_part], small.at[pl.ds(pl.multiple_of(8 * row, 8), 8), :], sems.at[10 + n])
            )
    for copy in later:
        copy.start()

    def block_copies(src, at, dst, sem):
        inside = at % 4
        return [
            pltpu.make_async_copy(
                src.at[pl.ds(BLOCK.start, HALF // 2), pl.ds(part * HALF, HALF)],
                dst.at[
                    0,
                    pl.ds(pl.multiple_of((inside // 2) * HALF + part * (HALF // 2), 8), HALF // 2),
                    lane_slice((inside % 2) * HALF, HALF),
                ],
                sems.at[sem + part],
            )
            for part in range(2)
        ]

    for src, at, early, late, n in ((low_f, low_at, wq, wk, 4), (high_f, high_at, wv, wo, 6)):

        @pl.when(at < RING // 2)
        def _early(src=src, at=at, early=early, n=n):
            for copy in block_copies(src, at, early, n):
                copy.start()

        @pl.when(at >= RING // 2)
        def _late(src=src, at=at, late=late, n=n):
            for copy in block_copies(src, at, late, n):
                copy.start()

        later += block_copies(src, at, early, n)
    if last:
        for copy in rel_copies:
            copy.wait()
        for src, at, row, _ in blocks:
            rel_all[pl.ds(pl.multiple_of(at * REL_PIECE, 8), REL_PIECE), :] = src[REL, :]
            small_all[pl.ds(pl.multiple_of(8 * row, 8), 8), :] = src[REL.stop :, :]
        w_rel[0] = dot_tn(pos[...], rel_all[...].astype(BF16))
        finish_small(small_all, *small_outs)
    for copy in copies + later:
        copy.wait()


def unpack(step, meta, own_a, other_a, own_b, other_b, outs, earlier, pos, heads):
    given = [v for v in outs if not isinstance(v, jax.ShapeDtypeStruct)]
    width, ff = own_a.shape[1], outs[0].shape[2]
    last = pos is not None

    def f32(*dims):
        return shape(*dims, dtype=F32)

    extra = [f32(8, LANES)]
    scratch = [
        *[pltpu.VMEM((HEAD_ROWS, width), F32)] * 2,
        *[pltpu.VMEM((B_ROWS, width), F32)] * 2,
        pltpu.SemaphoreType.DMA((12,)),
    ]
    if last:
        by_head, line = f32(heads, 1, width // heads), f32(1, width)
        extra = [
            f32(1, width, width), by_head, by_head, by_head, f32(heads, 2, width // heads), line, line, f32(1, ff),
            line, line, line, f32(width),
        ]
        scratch += [
            pltpu.VMEM(pos.shape, F32), pltpu.VMEM((16 * RING, width), F32), pltpu.SemaphoreType.DMA((2,)),
        ]
    front = [meta, own_a, other_a, own_b, other_b] + ([pos] if last else [])
    results = pl.pallas_call(
        functools.partial(unpack_body, (step + RING - 1) % RING, last),
        out_shape=tuple(shape(*v.shape, dtype=v.dtype) for v in outs) + tuple(extra),
        in_specs=[SMEM_SPEC] + [VMEM_SPEC] * (len(front) - 1) + [ANY_SPEC] * (len(given) + len(earlier)),
        out_specs=tuple(ANY_SPEC for _ in outs) + (VMEM_SPEC,) * len(extra),
        input_output_aliases={len(front) + n: n for n in range(len(given))},
        scratch_shapes=scratch,
        compiler_params=params(),
        cost_estimate=cost(0, 8_000_000),
    )(*front, *given, *earlier)
    results, token = results[: len(outs)], results[len(outs) :]
    if not last:
        token = token[0]
    return results, token


def ring_steps(count):
    cycle = [(z, 0) for z in range(4)] + [(z, 1) for z in (3, 2, 1, 0)]
    steps = []
    for index in range(count):
        base, inside = index - index % GROUP, index % GROUP
        at = cycle.index((inside // 4, (inside // 2) % 2))
        z, y = cycle[(at + (1 if inside % 2 == 0 else -1)) % RING]
        steps.append((index, base + (z * 2 + y) * 2 + inside % 2))
    return steps


SECTION, DP = "section", "dp"


def swapped(value, axis, bit):
    count = lax.axis_size(axis)
    return lax.ppermute(value, axis, [(index, index ^ bit) for index in range(count)])


def position_table(total_rows, width_model, mem_rows, seg_rows):
    row_ids = np.arange(total_rows, dtype=np.float32)
    distance = np.float32(mem_rows + seg_rows - 1) - row_ids
    power = np.arange(0, width_model, 2, dtype=np.float32) / np.float32(width_model)
    freqs = np.float32(1.0) / np.power(np.float32(10000.0), power)
    angles = distance[:, None] * freqs[None, :]
    return np.concatenate([np.sin(angles), np.cos(angles)], axis=1).astype(np.float32)


def scratches(seg_rows, mem_rows, width, ff, heads):
    rows, key_rows, rel_rows = 2 * seg_rows, mem_rows + seg_rows, mem_rows + 2 * seg_rows
    vm, dma = pltpu.VMEM, pltpu.SemaphoreType.DMA
    vrow_b, vrow_f, square, wide = vm((rows, width), BF16), vm((rows, width), F32), vm((width, width), BF16), vm((rows, ff), BF16)
    weights_f = dict(fi=vm((width, ff), BF16), fo=vm((ff, width), BF16))
    weights_a = dict(wk=square, wq=square, wv=square, wo=square, rel=vm((rel_rows, width), BF16))
    probs_scratch = vm((heads, rows, key_rows), BF16)
    forward_scratch = dict(
        joined=vrow_b, stream=vrow_b, qc=vrow_b, qp=vrow_b, qs=vrow_b, k=vrow_b, v=vrow_b, mixed=vrow_b,
        midb=vrow_b, out=vrow_b, p=probs_scratch,
        pos=vm((heads // 2, 2 * rows, key_rows), F32),
        bias=vm((2, seg_rows, seg_rows), F32),
        mid_in=vrow_f, outer=vrow_f, act=wide, slope=wide,
        sem_in=dma((10,)),
        sem_first=dma((1,)),
        sem_out=dma((40,)),
        **weights_f, **weights_a,
    )
    backward_scratch = dict(
        outer=vrow_f, mid_in=vrow_f, cot=vrow_b, returned=vrow_b, e=vrow_b, ab=vrow_b, a=vrow_f, acc=vrow_f,
        u=wide, slope=wide, x=vrow_b, k=vrow_b, v=vrow_b, qc=vrow_b, qp=vrow_b, qs=vrow_b, qpf=vrow_b, dk=vrow_b,
        dv=vrow_b, dqb=vrow_b, out=vrow_b, p=probs_scratch, dq=vrow_f, dqp=vrow_f,
        drel=vm((rel_rows, width), F32),
        sums_t=vm((16, width), F32),
        sums=vm((8, width), F32),
        sem_tail=dma((1 + 3 * (ff // width),)),
        sem_first=dma((4,)),
        sem_head=dma((11,)),
        sem_out=dma((14,)),
        **weights_f, **weights_a,
    )
    return forward_scratch, backward_scratch


def shards(
    content_in, memory, mask_embed, doc_ids, orders, targets, slot_used,
    w_query, w_key, w_value, w_out, w_rel, bias_content, bias_position, bias_segment, seg_embed,
    norm1_gain, norm1_shift, ffn_in, ffn_in_bias, ffn_out, ffn_out_bias, norm2_gain, norm2_shift,
    content_cot, query_cot,
):
    slots, seg_rows, width = content_in.shape
    mem_rows = memory.shape[2]
    heads, dim = bias_content.shape[1:]
    ff = ffn_in.shape[2]
    key_rows, rows = mem_rows + seg_rows, 2 * seg_rows
    rel_rows = key_rows + seg_rows
    section = lax.axis_index(SECTION).astype(jnp.int32)
    dp = lax.axis_index(DP).astype(jnp.int32)
    dp_count = lax.axis_size(DP)
    inside = dp % GROUP
    at = jnp.where((inside // 2) % 2 == 0, inside // 4, RING - 1 - inside // 4)
    lane = jnp.arange(2 * RING + 2, dtype=jnp.int32)
    meta = jnp.where(
        lane < RING,
        (at - lane) & (RING - 1),
        jnp.where(
            lane < 2 * RING,
            (-at - lane) & (RING - 1),
            jnp.where(lane == META_CORE, dp % 2, section),
        ),
    )
    pos_b = jnp.asarray(position_table(rel_rows, width, mem_rows, seg_rows)).astype(BF16)
    small, rel = pl.pallas_call(
        prepare_body,
        out_shape=(shape(SMALL_ROWS, width, dtype=F32), shape(rel_rows, width)),
        compiler_params=params(),
    )(
        bias_content, bias_position, bias_segment,
        jnp.transpose(seg_embed[0], (1, 0, 2)), norm1_gain, norm1_shift, ffn_out_bias, norm2_gain,
        norm2_shift, mask_embed, ffn_in_bias, pos_b, w_rel,
    )

    row_b, row_f = shape(slots, rows, width), shape(slots, rows, width, dtype=F32)
    kept = dict(
        joined=row_b, stream=row_b, qc=row_b, qp=row_b, qs=row_b, k=row_b, v=row_b, mixed=row_b,
        p=shape(slots, heads, rows, key_rows),
        mid_in=row_f,
        outer=row_f,
        slope=shape(slots, rows, ff),
        me=shape(2, slots, rows, width),
        ua=shape(2, slots, rows, ff),
        content_out=shape(1, slots, seg_rows, width),
        query_out=shape(1, slots, seg_rows, width),
    )
    forward_scratch, backward_scratch = scratches(seg_rows, mem_rows, width, ff, heads)
    common = dict(meta=(SMEM_SPEC, meta), slot_used=(SMEM_SPEC, slot_used), **in_vmem(small=small))
    ids = in_vmem(docs=doc_ids, orders=orders, targets=targets)
    weights_attention = in_hbm(w_key=w_key, w_query=w_query, w_value=w_value, w_out=w_out, rel=rel)
    weights_ffn = in_hbm(ffn_in=ffn_in, ffn_out=ffn_out)
    sent = {}
    for call in range(4):
        layer, slot = call // 2, call % 2
        source = in_hbm(content_in=content_in) if layer == 0 else in_hbm(arrived=sent[slot])
        inputs = common | ids | in_hbm(memory=memory) | weights_attention | weights_ffn | source
        fresh = dict(sent=shape(rows, width)) if layer == 0 else {}
        kept, new = call_kernel(forward_body, layer, slot, inputs, kept, fresh, forward_scratch)
        if layer == 0:
            sent[slot] = lax.ppermute(new.popitem()[1], SECTION, [(0, 1)])
    kept = types.SimpleNamespace(**kept)

    grads = dict(
        me=kept.me, ua=kept.ua, ab=row_b, dk=row_b, dv=row_b, dq=row_b,
        drel=shape(slots, rel_rows, width, dtype=F32),
        input_grad=shape(1, slots, seg_rows, width),
        sums=shape(slots, SUM_ROWS, width, dtype=F32),
    )
    flat = lambda v: v.reshape(v.shape[:-3] + (slots * rows, v.shape[-1]))
    returned = {}
    for call in range(4):
        layer, slot = 1 - call // 2, 1 - call % 2
        inputs = common | in_vmem(docs=doc_ids) | weights_attention | weights_ffn | in_hbm(
            outer=kept.outer, slope=kept.slope, mid_in=kept.mid_in, content_cot=content_cot, query_cot=query_cot,
            p=kept.p, k=kept.k, v=kept.v, qc=kept.qc, qp=kept.qp, qs=kept.qs,
        )
        if layer == 0:
            inputs |= in_hbm(returned=returned[slot])
        fresh = dict(sent=shape(rows, width)) if layer == 1 else {}
        grads, new = call_kernel(backward_body, layer, slot, inputs, grads, fresh, backward_scratch)
        if layer == 1:
            returned[slot] = lax.ppermute(new.popitem()[1], SECTION, [(1, 0)])
    grads = types.SimpleNamespace(**grads)

    me, ua = flat(grads.me), flat(grads.ua)
    operands = [flat(v) for v in (kept.stream, kept.joined, kept.mixed, grads.dq, grads.dk, grads.dv, grads.ab)]
    operands += [grads.drel, grads.sums]
    own_a, own_b, *handed = pieces(meta, me, ua, operands)
    first_a, first_b = [swapped(value, DP, 1) for value in handed[:2]]
    first_a, first_b, *rest = lax.optimization_barrier((first_a, first_b, *handed[2:]))
    rest_a, rest_b = [swapped(value, DP, 1) for value in rest]
    own, others = (own_a, own_b), ((first_a, rest_a), (first_b, rest_b))

    def add(ring, step, came=None):
        other = others[ring][0][0] if step == 0 else others[ring][1][step - 1]
        total = own[ring][step].astype(F32) + other.astype(F32)
        return (total if came is None else total + came.astype(F32)).astype(BF16)

    acc = [add(0, 0), add(1, 0)]

    steps = ring_steps(dp_count)
    for step in range(1, RING):
        came = [lax.ppermute(acc[ring], DP, steps) for ring in range(2)]
        acc = [add(ring, step, came[ring]) for ring in range(2)]
    acc_a, acc_b = acc
    bit = GROUP
    while bit < dp_count:
        acc_a = (acc_a.astype(F32) + swapped(acc_a, DP, bit).astype(F32)).astype(BF16)
        acc_b = (acc_b.astype(F32) + swapped(acc_b, DP, bit).astype(F32)).astype(BF16)
        bit *= 2
    spare = lax.slice_in_dim(acc_b, REL.stop, B_ROWS, axis=0)
    came = swapped(spare, SECTION, 1)
    holds = (meta[META_CORE] == MASK_ROW % 2) & (meta[2 * RING - 1] == MASK_ROW // 2)
    row = lax.broadcasted_iota(jnp.int32, spare.shape, 0)
    spare = jnp.where(holds & (row == 0), (spare.astype(F32) + came.astype(F32)).astype(BF16), spare)
    acc_b = lax.dynamic_update_slice_in_dim(acc_b, spare, REL.stop, axis=0)
    ffn_outs = [shape(1, width, ff, dtype=F32), shape(1, ff, width, dtype=F32)]
    rest_outs = [shape(1, width, width, dtype=F32) for _ in range(4)] + [shape(rel_rows, width, dtype=F32)]
    rest_outs.append(shape(16 * RING, width, dtype=F32))
    tokens = []
    outs = ffn_outs + rest_outs
    for step in range(RING):
        if step:
            acc_a = lax.ppermute(acc_a, DP, steps)
            acc_b = lax.ppermute(acc_b, DP, steps)
        handed_a, handed_b, before = acc_a, acc_b, []
        if step > 1:
            handed_a, before_a = lax.optimization_barrier((acc_a, tokens[step - 2]))
            before.append(before_a)
        if step:
            handed_b, before_b = lax.optimization_barrier((acc_b, tokens[step - 1]))
            before.append(before_b)
        outs, token = unpack(
            step, meta, acc_a, swapped(handed_a, DP, 1), acc_b, swapped(handed_b, DP, 1), outs, before,
            pos_b if step == RING - 1 else None, heads,
        )
        tokens.append(token)
    ffn_outs, rest_outs = outs[:2], outs[2:]
    (
        grad_w_rel, grad_bc, grad_bp, grad_bs, grad_seg, grad_n1g, grad_n1s, grad_fib, grad_fob, grad_n2g, grad_n2s,
        mask_grad,
    ) = tokens[-1]
    grad_ffn_in, grad_ffn_out = ffn_outs
    grad_w_query, grad_w_key, grad_w_value, grad_w_out = rest_outs[:4]
    one_layer = lambda v: v.reshape(1, heads, dim)
    return (
        kept.content_out, kept.query_out, grads.input_grad, mask_grad,
        grad_w_query, grad_w_key, grad_w_value, grad_w_out, grad_w_rel,
        one_layer(grad_bc), one_layer(grad_bp), one_layer(grad_bs), jnp.transpose(grad_seg, (1, 0, 2))[None],
        grad_n1g, grad_n1s, grad_ffn_in, grad_fib, grad_ffn_out, grad_fob, grad_n2g, grad_n2s,
    )


def solution(mesh):
    two, three, four = P(SECTION, None), P(SECTION, None, None), P(SECTION, None, None, None)
    rows = P(SECTION, DP, None, None)
    return jax.shard_map(
        shards,
        mesh=mesh,
        in_specs=(
            P(DP, None, None), rows, P(), P(DP, None), P(DP, None), P(DP, None), P(DP), *[three] * 8, four,
            two, two, three, two, three, two, two, two, rows, rows,
        ),
        out_specs=(
            rows, rows, rows, P(), *[three] * 8, four, two, two, three, two, three, two, two, two,
        ),
        check_vma=False,
    )
```
